256 devices in a mesh: dp: 16 (over y, z_hi, core), owner: 16 (over z_lo, x).
Axes of the slice: x: 4, y: 4, z: 8 (z_hi: 2, z_lo: 4; z = z_hi * 4 + z_lo), core: 2. Of those that a mesh axis runs over, the one named last changes fastest.
Arguments:
- acts: bfloat16 [57344, 4096], P(('dp', 'owner')), may hold values from -64 to 64
- grads_out: bfloat16 [57344, 11008], P(('dp', 'owner')), may hold values from -64 to 64
- weight_grad: bfloat16 [4096, 11008], P('owner', 'dp'), may hold values from -6 to 6
Outputs:
- preconditioned: bfloat16 [4096, 11008], P('owner')
The draws below stay inside these ranges and needn't reach their ends.
All inputs are finite; a program needn't handle non-finite values.
Results may differ from the reference program's by a relative error of at most 0.0011.
Values may be sent and summed in bfloat16 or wider, within the bound.
A program may use at most 320 MiB of HBM per device.

```python
import math
import jax
import jax.numpy as jnp
from jax import lax

D = 4096
FF = 11008
AB = 256
GB = 344
TOK_DEV = 224
TOKENS = 57344
NAB = 16
NGB = 32


def shape_rows(noise, key, rows, width, rise, size):
    column_key, row_key, block_key = jax.random.split(key, 3)
    mixed = noise[:, 2:] + 0.8 * noise[:, 1:-1] + 0.5 * noise[:, :-2]
    slope = jnp.sqrt(1.0 + rise * jnp.arange(width, dtype=jnp.float32) / width)
    column = jnp.exp(jax.random.uniform(column_key, (width,), jnp.float32, math.log(0.4), math.log(2.5))) * slope
    scales = jnp.exp(jax.random.uniform(row_key, (rows,), jnp.float32, math.log(0.3), math.log(2.5)))
    table = jnp.exp(jax.random.uniform(block_key, (rows // TOK_DEV, width // size), jnp.float32, math.log(0.3), math.log(3.0)))
    table = jnp.repeat(jnp.repeat(table, TOK_DEV, axis=0), size, axis=1)
    values = 0.25 * mixed * column[None, :] * scales[:, None] * table
    return jnp.clip(values, -60.0, 60.0).astype(jnp.bfloat16)


def draw_acts(key, part):
    key = jax.random.fold_in(key, 11)
    noise_key, shape_key = jax.random.split(key)
    noise = jax.random.truncated_normal(noise_key, -4.0, 4.0, (TOKENS, D + 2), jnp.float32)
    return shape_rows(noise, shape_key, TOKENS, D, 2.0, AB)


def draw_grads_out(key, part):
    key = jax.random.fold_in(key, 23)
    noise_key, shape_key = jax.random.split(key)
    noise = jax.random.truncated_normal(noise_key, -4.0, 4.0, (TOKENS, FF + 2), jnp.float32)
    return shape_rows(noise, shape_key, TOKENS, FF, 2.0, GB)


def steps_of(rng, dims, shards, least, high):
    def one(position, parts):
        steps = jax.random.uniform(jax.random.fold_in(jax.random.fold_in(rng, 6), position), (parts,), jnp.float32, least / len(shards), high / len(shards))
        return jnp.repeat(jnp.exp(steps), dims[position] // parts).reshape((-1,) + (1,) * (len(dims) - position - 1))

    factor_of = one(*shards[0])
    for cut in shards[1:]:
        factor_of = factor_of * one(*cut)
    return factor_of


def normal_values(own_key, extent, deviation, limit, cuts=(), held_as=jnp.bfloat16):
    values = jax.random.normal(own_key, extent, jnp.float32) * deviation
    if len(cuts) > 0:
        values = steps_of(own_key, extent, cuts, -0.22, 0.18) * values
    return jnp.clip(values, min=-limit, max=limit).astype(held_as)


def setup_inputs(seed: int = 0) -> dict:
    key_list = jax.random.split(jax.random.key(seed), 4)
    return {
        "acts": draw_acts(jax.random.fold_in(key_list[3], 71), 0),
        "grads_out": draw_grads_out(jax.random.fold_in(key_list[3], 71), 0),
        "weight_grad": normal_values(key_list[2], (D, FF), 1.0, 6.0, ((0, 16), (1, 16))),
    }


damping_level = 0.03

def block_grams(data, size, count):

    def one_block(index):
        columns = lax.dynamic_slice_in_dim(data, index * size, size, 1)
        return jnp.dot(columns.T.astype(jnp.float32), columns.astype(jnp.float32), preferred_element_type=jnp.float32)
    return lax.map(one_block, jnp.arange(count, dtype=jnp.int32))

def damped_inverse(blocks, damping):
    identity = jnp.eye(blocks.shape[-1], dtype=blocks.dtype)
    lower = jnp.linalg.cholesky(blocks + damping * identity)

    def solve_one(factor):
        return jax.scipy.linalg.cho_solve((factor, True), identity)
    return jax.vmap(solve_one)(lower)

def reference(acts, grads_out, weight_grad):
    act_factor = block_grams(acts, AB, NAB) / TOKENS
    grad_factor = block_grams(grads_out, GB, NGB) / TOKENS
    act_trace = jnp.sum(jnp.diagonal(act_factor, axis1=1, axis2=2))
    grad_trace = jnp.sum(jnp.diagonal(grad_factor, axis1=1, axis2=2))
    ratio = jnp.sqrt(act_trace / D / (grad_trace / FF))
    act_inverse = damped_inverse(act_factor, ratio * math.sqrt(damping_level))
    grad_inverse = damped_inverse(grad_factor, math.sqrt(damping_level) / ratio)
    gradient = weight_grad.astype(jnp.float32).reshape(NAB, AB, FF)
    left = jnp.einsum('kab,kbf->kaf', act_inverse, gradient, precision=lax.Precision.HIGHEST)
    left = left.reshape(D, NGB, GB)
    result = jnp.einsum('rkb,kbc->rkc', left, grad_inverse, precision=lax.Precision.HIGHEST)
    return result.reshape(D, FF).astype(jnp.bfloat16)
```

```python
import functools
import math

import jax
import jax.numpy as jnp
from jax import lax
from jax.experimental import pallas as pl
from jax.experimental.pallas import tpu as pltpu
from jax.sharding import PartitionSpec as P

D = 4096
FF = 11008
AB = 256
GB = 344
TOKENS = 57344
DAMP = math.sqrt(0.03)
MESH = pl.DeviceIdType.MESH
HIGH = lax.Precision.HIGHEST
F32 = jnp.float32
GROWS = 96
AROWS = 24
CH = GROWS + AROWS
HALF = 4 * CH
VLIM = 56 * 1024 * 1024


def place():
    dp = lax.axis_index("dp")
    own = lax.axis_index("owner")
    return dp, own


def swap_kernel(a_ref, g_ref, ao_ref, go_ref, local, send, recv):
    dp, own = place()
    core = lax.rem(dp, 2)
    sib = dp + 1 - 2 * core
    barrier = pltpu.get_barrier_semaphore()
    pl.semaphore_signal(barrier, inc=1, device_id=(sib, own), device_id_type=MESH)
    pl.semaphore_wait(barrier, 1)
    remote = []
    locals_ = []
    for i, (src, dst) in enumerate(((a_ref, ao_ref), (g_ref, go_ref))):
        width = dst.shape[2]
        theirs = pl.ds(pl.multiple_of((1 - core) * width, 128), width)
        mine = pl.ds(pl.multiple_of(core * width, 128), width)
        copy = pltpu.make_async_remote_copy(
            src_ref=src.at[:, theirs], dst_ref=dst.at[1], send_sem=send.at[i], recv_sem=recv.at[i],
            device_id=(sib, own), device_id_type=MESH)
        copy.start()
        remote.append(copy)
        keep = pltpu.make_async_copy(src.at[:, mine], dst.at[0], local.at[i])
        keep.start()
        locals_.append(keep)
    for copy in remote + locals_:
        copy.wait()


def swap(acts, grads):
    rows = acts.shape[0]
    return pl.pallas_call(
        swap_kernel,
        out_shape=(jax.ShapeDtypeStruct((2, rows, D // 2), acts.dtype),
                   jax.ShapeDtypeStruct((2, rows, FF // 2), acts.dtype)),
        in_specs=[pl.BlockSpec(memory_space=pl.ANY)] * 2,
        out_specs=(pl.BlockSpec(memory_space=pl.ANY),) * 2,
        scratch_shapes=[pltpu.SemaphoreType.DMA((2,))] * 3,
        compiler_params=pltpu.CompilerParams(collective_id=0, has_side_effects=True),
        name="swap",
    )(acts, grads)


def gram(block):
    return lax.dot_general(block, block, (((0,), (0,)), ((), ())), preferred_element_type=F32)


def gram_kernel(a_ref, g_ref, x_ref, y_ref, t_ref):
    def store(j, rows, start, value):
        chunk = start // CH
        px, py = j // 4, j % 4
        if chunk < 4:
            x_ref[px * 4 + py, pl.ds(start, rows), :] = value
        else:
            y_ref[py * 4 + px, pl.ds(start - HALF, rows), :] = value

    zero = jnp.zeros((128, 128), F32)
    grad_sum = jnp.zeros((8, 128), F32)
    act_sum = jnp.zeros((8, 128), F32)
    eye = (lax.broadcasted_iota(jnp.int32, (128, 128), 0)
           == lax.broadcasted_iota(jnp.int32, (128, 128), 1))

    def diag(tile):
        return jnp.sum(jnp.where(eye, tile, 0.0).reshape(16, 8, 128), axis=0)

    for j in range(16):
        g = gram(g_ref[:, j * GB:(j + 1) * GB])
        low = jnp.concatenate([g[256:344, :], jnp.zeros((40, GB), F32)], axis=0)
        low2 = jnp.concatenate([low[:, 256:344], jnp.zeros((128, 40), F32)], axis=1)
        tiles = [g[0:128, 0:128], g[128:256, 0:128], g[128:256, 128:256], low[:, 0:128], low[:, 128:256], low2]
        grad_sum += diag(tiles[0]) + diag(tiles[2]) + diag(tiles[5])
        for u in range(24):
            start = (u // 3) * CH + (u % 3) * 32
            r = (u % 4) * 32
            store(j, 32, start, tiles[u // 4][r:r + 32])
    for k in range(8):
        g = gram(a_ref[:, k * AB:(k + 1) * AB])
        tiles = [g[0:128, 0:128], g[128:256, 0:128], g[128:256, 128:256]]
        act_sum += diag(tiles[0]) + diag(tiles[2])
        for u in range(48):
            j = 2 * k + u // 24
            v = u % 24
            start = (v // 3) * CH + GROWS + (v % 3) * 8
            r = (u % 16) * 8
            store(j, 8, start, tiles[u // 16][r:r + 8])
    t_ref[0:8, :] = act_sum
    t_ref[8:16, :] = grad_sum


def grams(acts, grads):
    shape = jax.ShapeDtypeStruct((16, HALF, 128), F32)
    vmem = pl.BlockSpec(memory_space=pltpu.VMEM)
    return pl.pallas_call(
        gram_kernel,
        out_shape=(shape, shape, jax.ShapeDtypeStruct((16, 128), F32)),
        in_specs=[vmem] * 2,
        out_specs=(vmem,) * 3,
        compiler_params=pltpu.CompilerParams(vmem_limit_bytes=VLIM),
        name="grams",
    )(acts, grads)


def reduce_kernel(gx, gy, tr, fg_out, fa_out, t_out,
                  sx, sy, rx, ry, rx2, ry2, st, rz, fin, fg, fa, t1, t2, t3, q1, q2, q3, q4,
                  local, s1, r1, s2, r2, s3, r3, sg, rg, sa, ra, s4, r4):
    dp, own = place()
    core = lax.rem(dp, 2)
    zh = lax.rem(dp // 2, 2)
    y = dp // 4
    x = lax.rem(own, 4)
    zl = own // 4
    z = zh * 4 + zl
    sib = dp + 1 - 2 * core

    def at(ax, ay, az, ac):
        return ((ay * 2 + az // 4) * 2 + ac, lax.rem(az, 4) * 4 + ax)

    xs = [at(lax.rem(x + k, 4), y, z, core) for k in (1, 2, 3)]
    ys = [at(x, lax.rem(y + k, 4), z, core) for k in (1, 2, 3)]
    zs = [at(x, y, lax.rem(z + k, 8), core) for k in range(1, 8)]
    j = x * 4 + y
    unit = core * 8 + j // 2
    part = lax.rem(j, 2)

    barrier = pltpu.get_barrier_semaphore()

    def greet(device):
        pl.semaphore_signal(barrier, inc=1, device_id=device, device_id_type=MESH)

    for device in xs + ys + zs + [(sib, own)]:
        greet(device)

    def greet_sources(base):
        def body(i, _):
            js = lax.rem(base, 8) * 2 + i // 8
            device = at(js // 4, lax.rem(js, 4), lax.rem(i, 8), base // 8)

            @pl.when(jnp.logical_or(device[0] != dp, device[1] != own))
            def _():
                greet(device)
            return 0
        lax.fori_loop(0, 16, body, 0)

    greet_sources(dp)
    greet_sources(own)
    self_g = jnp.where(unit == dp, 1, 0)
    self_a = jnp.where(unit == own, 1, 0)
    pl.semaphore_wait(barrier, 14 + 32 - self_g - self_a)

    def send(src, dst, ssem, rsem, device):
        copy = pltpu.make_async_remote_copy(src_ref=src, dst_ref=dst, send_sem=ssem, recv_sem=rsem,
                                            device_id=device, device_id_type=MESH)
        copy.start()
        return copy

    copies = []
    for k in range(3):
        copies.append(send(gx.at[pl.ds(lax.rem(x + k + 1, 4) * 4, 4)], rx.at[k], s1.at[k], r1.at[k], xs[k]))
        copies.append(send(gy.at[pl.ds(lax.rem(y + k + 1, 4) * 4, 4)], ry.at[k], s1.at[3 + k], r1.at[3 + k], ys[k]))
        copies.append(send(tr, q1.at[k], s1.at[6 + k], r1.at[6 + k], xs[k]))
    copies.append(pltpu.make_async_copy(gx.at[pl.ds(x * 4, 4)], sx, local.at[0]))
    copies[-1].start()
    copies.append(pltpu.make_async_copy(gy.at[pl.ds(y * 4, 4)], sy, local.at[1]))
    copies[-1].start()
    for copy in copies:
        copy.wait()

    @pl.loop(0, 16)
    def _(i):
        a = i // 4
        rows = pl.ds(pl.multiple_of(lax.rem(i, 4) * CH, 8), CH)
        sx[a, rows, :] = (sx[a, rows, :] + rx[0, a, rows, :]) + (rx[1, a, rows, :] + rx[2, a, rows, :])
        sy[a, rows, :] = (sy[a, rows, :] + ry[0, a, rows, :]) + (ry[1, a, rows, :] + ry[2, a, rows, :])
    t1[...] = (tr[...] + q1[0]) + (q1[1] + q1[2])

    copies = []
    for k in range(3):
        copies.append(send(sx.at[lax.rem(y + k + 1, 4)], rx2.at[k], s2.at[k], r2.at[k], ys[k]))
        copies.append(send(sy.at[lax.rem(x + k + 1, 4)], ry2.at[k], s2.at[3 + k], r2.at[3 + k], xs[k]))
        copies.append(send(t1, q2.at[k], s2.at[6 + k], r2.at[6 + k], ys[k]))
    for copy in copies:
        copy.wait()

    @pl.loop(0, 4)
    def _(i):
        rows = pl.ds(pl.multiple_of(i * CH, 8), CH)
        st[i] = (sx[y, rows, :] + rx2[0, rows, :]) + (rx2[1, rows, :] + rx2[2, rows, :])
        st[4 + i] = (sy[x, rows, :] + ry2[0, rows, :]) + (ry2[1, rows, :] + ry2[2, rows, :])
    t2[...] = (t1[...] + q2[0]) + (q2[1] + q2[2])

    copies = []
    for k in range(7):
        copies.append(send(st.at[lax.rem(z + k + 1, 8)], rz.at[k], s3.at[k], r3.at[k], zs[k]))
        copies.append(send(t2, q3.at[k], s3.at[7 + k], r3.at[7 + k], zs[k]))
    for copy in copies:
        copy.wait()
    total = st[z]
    trace = t2[...]
    for k in range(7):
        total += rz[k]
        trace += q3[k]
    fin[...] = total
    t3[...] = trace

    side = send(t3, q4, s4, r4, (sib, own))
    gsrc = fin.at[pl.ds(0, GROWS)]
    asrc = fin.at[pl.ds(GROWS, AROWS)]
    gdst = fg.at[part, z]
    adst = fa.at[part, z]
    slot = part * 8 + z

    def put(src, dst, ssem, rsem, device, mine):
        @pl.when(mine)
        def _():
            pltpu.make_async_copy(src, dst, rsem).start()

        @pl.when(jnp.logical_not(mine))
        def _():
            send(src, dst, ssem, rsem, device)

    put(gsrc, gdst, sg.at[0], rg.at[slot], (unit, own), unit == dp)
    put(asrc, adst, sa.at[0], ra.at[slot], (dp, unit), unit == own)

    def out(k, _):
        send(gsrc, gdst, sg.at[k], rg.at[slot], (unit, lax.rem(own + k, 16)))
        send(asrc, adst, sa.at[k], ra.at[slot], (lax.rem(dp + k, 16), unit))
        return 0
    lax.fori_loop(1, 16, out, 0)

    def sent(src, dst, ssem):
        pltpu.make_async_remote_copy(src_ref=src, dst_ref=dst, send_sem=ssem, recv_sem=r4,
                                     device_id=(sib, own), device_id_type=MESH).wait_send()

    def got(dst, src, rsem):
        pltpu.make_async_copy(src, dst, rsem).wait()

    def arrive(k, _):
        got(fg.at[k // 8, lax.rem(k, 8)], gsrc, rg.at[k])
        got(fa.at[k // 8, lax.rem(k, 8)], asrc, ra.at[k])
        return 0
    lax.fori_loop(0, 16, arrive, 0)

    def left(k, _):
        sent(gsrc, gdst, sg.at[k])
        sent(asrc, adst, sa.at[k])
        return 0
    lax.fori_loop(1, 16, left, 0)

    @pl.when(unit != dp)
    def _():
        sent(gsrc, gdst, sg.at[0])

    @pl.when(unit != own)
    def _():
        sent(asrc, adst, sa.at[0])
    side.wait()
    fg_out[...] = fg[...]
    fa_out[...] = fa[...]
    t_out[...] = t3[...] + q4[...]


def reduce_all(gx, gy, tr):
    vmem = pl.BlockSpec(memory_space=pltpu.VMEM)
    dma = pltpu.SemaphoreType.DMA
    tile = pltpu.VMEM((16, 128), F32)
    return pl.pallas_call(
        reduce_kernel,
        out_shape=(jax.ShapeDtypeStruct((2, 8, GROWS, 128), F32),
                   jax.ShapeDtypeStruct((2, 8, AROWS, 128), F32),
                   jax.ShapeDtypeStruct((16, 128), F32)),
        in_specs=[pl.BlockSpec(memory_space=pl.ANY)] * 2 + [vmem],
        out_specs=(vmem,) * 3,
        scratch_shapes=[
            pltpu.VMEM((4, HALF, 128), F32), pltpu.VMEM((4, HALF, 128), F32),
            pltpu.VMEM((3, 4, HALF, 128), F32), pltpu.VMEM((3, 4, HALF, 128), F32),
            pltpu.VMEM((3, HALF, 128), F32), pltpu.VMEM((3, HALF, 128), F32),
            pltpu.VMEM((8, CH, 128), F32), pltpu.VMEM((7, CH, 128), F32), pltpu.VMEM((CH, 128), F32),
            pltpu.VMEM((2, 8, GROWS, 128), F32), pltpu.VMEM((2, 8, AROWS, 128), F32),
            tile, tile, tile,
            pltpu.VMEM((3, 16, 128), F32), pltpu.VMEM((3, 16, 128), F32), pltpu.VMEM((7, 16, 128), F32), tile,
            dma((2,)), dma((9,)), dma((9,)), dma((9,)), dma((9,)), dma((14,)), dma((14,)),
            dma((16,)), dma((16,)), dma((16,)), dma((16,)), dma, dma,
        ],
        compiler_params=pltpu.CompilerParams(collective_id=1, has_side_effects=True, vmem_limit_bytes=VLIM),
        name="reduce_all",
    )(gx, gy, tr)


def dot(a, b, ca=1, cb=0):
    return lax.dot_general(a, b, (((ca,), (cb,)), ((), ())), precision=HIGH, preferred_element_type=F32)


def sweep_tiles(refs, panels):
    sub = lax.broadcasted_iota(jnp.int32, (8, 128), 0)
    lane = lax.broadcasted_iota(jnp.int32, (8, 128), 1)
    lane_all = lax.broadcasted_iota(jnp.int32, (128, 128), 1)

    def panel(p, _):
        base = pl.multiple_of(p * 8, 8)
        rows = pl.ds(base, 8)
        back = lax.rem(128 - base, 128)
        olds = [ref[rows, :] for ref in refs]
        news = [pltpu.roll(old, back, 1) for old in olds]
        for s in range(8):
            for i, now in enumerate(news):
                col = jnp.broadcast_to(now[:, s:s + 1], (8, 128))
                row = jnp.broadcast_to(now[s:s + 1, :], (8, 128))
                inv = 1.0 / jnp.broadcast_to(col[s:s + 1, :], (8, 128))
                col = jnp.where(sub == s, -1.0, col)
                row = jnp.where(lane == s, -1.0, row)
                keep = jnp.where(jnp.logical_or(sub == s, lane == s), 0.0, now)
                news[i] = keep - col * (row * inv)
        inside = jnp.logical_and(lane_all >= base, lane_all < base + 8)
        for ref, old, new in zip(refs, olds, news):
            new = pltpu.roll(new, base, 1)
            ref[...] = jnp.where(inside, 0.0, ref[...]) - dot(old, new, 0, 0)
            ref[rows, :] = new
        return 0

    lax.fori_loop(0, panels, panel, 0)


def solve_kernel(fg_ref, fa_ref, t_ref, w_ref, p_ref, g_ref, a_ref, gi_ref, ai_ref):
    act_trace = jnp.sum(t_ref[0:8, :], keepdims=True) / TOKENS
    grad_trace = jnp.sum(t_ref[8:16, :], keepdims=True) / TOKENS
    ratio = jnp.sqrt(act_trace / D / (grad_trace / FF))
    act_damp = ratio * DAMP
    grad_damp = DAMP / ratio
    r = lax.broadcasted_iota(jnp.int32, (128, 128), 0)
    c = lax.broadcasted_iota(jnp.int32, (128, 128), 1)
    eye = jnp.where(r == c, 1.0, 0.0)
    last = GB - 256
    for b in range(2):
        for t in range(6):
            tile = fg_ref[b, t * 128:(t + 1) * 128, :] / TOKENS
            if t in (0, 2):
                tile = tile + grad_damp * eye
            if t in (3, 4):
                tile = jnp.where(r < last, tile, 0.0)
            if t == 5:
                tile = jnp.where(jnp.logical_and(r < last, c < last), tile + grad_damp * eye, eye)
            g_ref[b * 6 + t] = tile
    for t in range(3):
        tile = fa_ref[t * 128:(t + 1) * 128, :] / TOKENS
        if t != 1:
            tile = tile + act_damp * eye
        a_ref[t] = tile
    gs = [[g_ref.at[b * 6 + t] for t in range(6)] for b in range(2)]
    am = [a_ref.at[t] for t in range(3)]
    sweep_tiles([gs[0][0], gs[1][0], am[0]], 16)
    for m in gs:
        neg = m[0][...]
        a10, a20 = m[1][...], m[3][...]
        v10, v20 = -dot(a10, neg), -dot(a20, neg)
        m[2][...] -= dot(v10, a10, 1, 1)
        m[4][...] -= dot(v20, a10, 1, 1)
        m[5][...] -= dot(v20, a20, 1, 1)
        m[1][...] = v10
        m[3][...] = v20
    a10 = am[1][...]
    v10 = -dot(a10, am[0][...])
    am[2][...] -= dot(v10, a10, 1, 1)
    am[1][...] = v10
    sweep_tiles([gs[0][2], gs[1][2], am[2]], 16)
    for m in gs:
        neg = m[2][...]
        a10, a21 = m[1][...], m[4][...]
        v10, v21 = -dot(neg, a10), -dot(a21, neg)
        m[0][...] -= dot(a10, v10, 0, 0)
        m[3][...] -= dot(a21, v10)
        m[5][...] -= dot(v21, a21, 1, 1)
        m[1][...] = v10
        m[4][...] = v21
    a10 = am[1][...]
    v10 = -dot(am[2][...], a10)
    am[0][...] -= dot(a10, v10, 0, 0)
    am[1][...] = v10
    sweep_tiles([gs[0][5], gs[1][5]], last // 8)
    for m in gs:
        neg = m[5][...]
        a20, a21 = m[3][...], m[4][...]
        v20, v21 = -dot(neg, a20), -dot(neg, a21)
        m[0][...] -= dot(a20, v20, 0, 0)
        m[1][...] -= dot(a21, v20, 0, 0)
        m[2][...] -= dot(a21, v21, 0, 0)
        m[3][...] = v20
        m[4][...] = v21
    ai_ref[0:128, 0:128] = -am[0][...]
    ai_ref[128:256, 0:128] = -am[1][...]
    ai_ref[0:128, 128:256] = -am[1][...].T
    ai_ref[128:256, 128:256] = -am[2][...]
    for b, m in enumerate(gs):
        for t, (i, j) in enumerate(((0, 0), (1, 0), (1, 1), (2, 0), (2, 1), (2, 2))):
            tile = -m[t][...]
            gi_ref[b, i * 128:(i + 1) * 128, j * 128:(j + 1) * 128] = tile
            if i != j:
                gi_ref[b, j * 128:(j + 1) * 128, i * 128:(i + 1) * 128] = tile.T
    for b in range(2):
        left = dot(ai_ref[...], w_ref[b].astype(F32))
        p_ref[:, b * 384:(b + 1) * 384] = dot(left, gi_ref[b]).astype(jnp.bfloat16)


def solve(fg, fa, tr, w):
    vmem = pl.BlockSpec(memory_space=pltpu.VMEM)
    return pl.pallas_call(
        solve_kernel,
        out_shape=jax.ShapeDtypeStruct((256, 768), jnp.bfloat16),
        in_specs=[vmem] * 4,
        out_specs=vmem,
        scratch_shapes=[pltpu.VMEM((12, 128, 128), F32), pltpu.VMEM((3, 128, 128), F32),
                        pltpu.VMEM((2, 384, 384), F32), pltpu.VMEM((256, 256), F32)],
        compiler_params=pltpu.CompilerParams(vmem_limit_bytes=VLIM),
        name="solve",
    )(fg, fa, tr, w)


def gather_kernel(p_ref, o_ref, local, sz, rz, sy, ry, sh, rh, sc, rc):
    dp, own = place()
    core = lax.rem(dp, 2)
    y = dp // 4
    sib = dp + 1 - 2 * core
    zh = lax.rem(dp // 2, 2)
    anti = dp + 2 - 4 * zh
    up = lax.rem(y + 1, 4) * 4 + lax.rem(dp, 4)
    down = lax.rem(y + 3, 4) * 4 + lax.rem(dp, 4)
    barrier = pltpu.get_barrier_semaphore()
    for device in (sib, anti, up, down):
        pl.semaphore_signal(barrier, inc=1, device_id=(device, own), device_id_type=MESH)
    pl.semaphore_wait(barrier, 4)

    def other(d):
        return d + 2 - 4 * lax.rem(d // 2, 2)

    waits = []

    def send(d, ssem, rsem, device, src=None, half=None):
        src = o_ref.at[d] if src is None else src
        dst = o_ref.at[d]
        if half is not None:
            src = src.at[pl.ds(half * 128, 128)]
            dst = dst.at[pl.ds(half * 128, 128)]
        copy = pltpu.make_async_remote_copy(src_ref=src, dst_ref=dst, send_sem=ssem, recv_sem=rsem,
                                            device_id=(device, own), device_id_type=MESH)
        copy.start()
        waits.append(copy)

    def arrived(d, sem, half=None):
        dst = o_ref.at[d]
        if half is not None:
            dst = dst.at[pl.ds(half * 128, 128)]
        pltpu.make_async_remote_copy(src_ref=dst, dst_ref=dst, send_sem=sz, recv_sem=sem,
                                     device_id=(sib, own), device_id_type=MESH).wait_recv()

    send(dp, sz, rz, anti, p_ref)
    send(dp, sy.at[0], ry.at[0], up, p_ref)
    send(dp, sy.at[1], ry.at[1], down, p_ref)
    send(dp, sc.at[0], rc.at[0], sib, p_ref)
    keep = pltpu.make_async_copy(p_ref, o_ref.at[dp], local)
    keep.start()
    arrived(down, ry.at[0])
    send(down, sh.at[0], rh.at[0], up, half=0)
    send(down, sc.at[1], rc.at[1], sib)
    arrived(up, ry.at[1])
    send(up, sh.at[1], rh.at[1], down, half=1)
    send(up, sc.at[2], rc.at[2], sib)
    arrived(anti, rz)
    send(anti, sy.at[2], ry.at[2], up)
    send(anti, sy.at[3], ry.at[3], down)
    send(anti, sc.at[3], rc.at[3], sib)
    far = other(down) * 0 + lax.rem(y + 2, 4) * 4 + lax.rem(dp, 4)
    arrived(other(down), ry.at[2])
    send(other(down), sh.at[2], rh.at[2], up, half=0)
    send(other(down), sc.at[4], rc.at[4], sib)
    arrived(other(up), ry.at[3])
    send(other(up), sh.at[3], rh.at[3], down, half=1)
    send(other(up), sc.at[5], rc.at[5], sib)
    arrived(far, rh.at[0], half=0)
    arrived(far, rh.at[1], half=1)
    send(far, sc.at[6], rc.at[6], sib)
    arrived(other(far), rh.at[2], half=0)
    arrived(other(far), rh.at[3], half=1)
    send(other(far), sc.at[7], rc.at[7], sib)

    def twin(d):
        return d + 1 - 2 * lax.rem(d, 2)

    for i, d in enumerate((dp, down, up, anti, other(down), other(up), far, other(far))):
        arrived(twin(d), rc.at[i])
    keep.wait()
    for copy in waits:
        copy.wait_send()


def gather(p):
    dma = pltpu.SemaphoreType.DMA
    return pl.pallas_call(
        gather_kernel,
        out_shape=jax.ShapeDtypeStruct((16, 256, 768), jnp.bfloat16),
        in_specs=[pl.BlockSpec(memory_space=pl.ANY)],
        out_specs=pl.BlockSpec(memory_space=pl.ANY),
        scratch_shapes=[dma, dma, dma, dma((4,)), dma((4,)), dma((4,)), dma((4,)), dma((8,)), dma((8,))],
        compiler_params=pltpu.CompilerParams(collective_id=2, has_side_effects=True),
        name="gather",
    )(p)


def flat_kernel(i_ref, o_ref):
    for d in range(16):
        for b in range(2):
            start = (2 * d + b) * GB
            o_ref[:, start:start + GB] = i_ref[d, :, b * 384:b * 384 + GB]


def flatten(slices):
    rows = 64
    return pl.pallas_call(
        flat_kernel,
        out_shape=jax.ShapeDtypeStruct((256, FF), jnp.bfloat16),
        grid=(256 // rows,),
        in_specs=[pl.BlockSpec((16, rows, 768), lambda i: (0, i, 0))],
        out_specs=pl.BlockSpec((rows, FF), lambda i: (i, 0)),
        compiler_params=pltpu.CompilerParams(vmem_limit_bytes=VLIM),
        name="flatten",
    )(slices)


def shards(acts, grads_out, weight_grad):
    a2, g2 = swap(acts, grads_out)
    rows = 2 * acts.shape[0]
    gx, gy, tr = grams(a2.reshape(rows, D // 2), g2.reshape(rows, FF // 2))
    fg, fa, tr = reduce_all(gx, gy, tr)
    w = jnp.pad(weight_grad.reshape(256, 2, GB).transpose(1, 0, 2), ((0, 0), (0, 0), (0, 384 - GB)))
    p = solve(fg.reshape(2, 8 * GROWS, 128), fa.reshape(16 * AROWS, 128), tr, w)
    return flatten(gather(p))


def solution(mesh):
    in_specs = (P(("dp", "owner"), None), P(("dp", "owner"), None), P("owner", "dp"))
    out_specs = P("owner", None)
    return jax.shard_map(shards, mesh=mesh, in_specs=in_specs, out_specs=out_specs, check_vma=False)
```

```python
import functools
import math

import jax
import jax.numpy as jnp
from jax import lax
from jax.experimental import pallas as pl
from jax.experimental.pallas import tpu as pltpu
from jax.sharding import PartitionSpec as P

D = 4096
FF = 11008
AB = 256
GB = 344
TOKENS = 57344
DAMP = math.sqrt(0.03)
MESH = pl.DeviceIdType.MESH
HIGH = lax.Precision.HIGHEST
F32 = jnp.float32
GROWS = 64
AROWS = 16
CH = GROWS + AROWS
HALF = 4 * CH
VLIM = 56 * 1024 * 1024


def place():
    dp = lax.axis_index("dp")
    own = lax.axis_index("owner")
    return dp, own


def swap_kernel(a_ref, g_ref, ao_ref, go_ref, send, recv):
    dp, own = place()
    core = lax.rem(dp, 2)
    sib = dp + 1 - 2 * core
    barrier = pltpu.get_barrier_semaphore()
    pl.semaphore_signal(barrier, inc=1, device_id=(sib, own), device_id_type=MESH)
    pl.semaphore_wait(barrier, 1)
    copies = []
    for i, (src, dst) in enumerate(((a_ref, ao_ref), (g_ref, go_ref))):
        width = dst.shape[1]
        theirs = pl.ds(pl.multiple_of((1 - core) * width, 128), width)
        copy = pltpu.make_async_remote_copy(
            src_ref=src.at[:, theirs], dst_ref=dst, send_sem=send.at[i], recv_sem=recv.at[i],
            device_id=(sib, own), device_id_type=MESH)
        copy.start()
        copies.append(copy)
    for copy in copies:
        copy.wait()


def swap(acts, grads):
    rows = acts.shape[0]
    return pl.pallas_call(
        swap_kernel,
        out_shape=(jax.ShapeDtypeStruct((rows, D // 2), acts.dtype),
                   jax.ShapeDtypeStruct((rows, FF // 2), acts.dtype)),
        in_specs=[pl.BlockSpec(memory_space=pl.ANY)] * 2,
        out_specs=(pl.BlockSpec(memory_space=pl.ANY),) * 2,
        scratch_shapes=[pltpu.SemaphoreType.DMA((2,))] * 2,
        compiler_params=pltpu.CompilerParams(collective_id=0, has_side_effects=True),
        name="swap",
    )(acts, grads)


def gram(block):
    return lax.dot_general(block, block, (((0,), (0,)), ((), ())), preferred_element_type=F32)


def gram_kernel(a_ref, g_ref, as_ref, gs_ref, x_ref, y_ref, t_ref, abuf, gbuf, sems):
    core = lax.rem(lax.axis_index("dp"), 2)
    rows = a_ref.shape[0]
    cut = 22 * 128
    copies = []
    for i, (whole, other, buf, lo, hi) in enumerate((
            (a_ref, as_ref, abuf, 0, D // 2), (g_ref, gs_ref, gbuf, 0, cut), (g_ref, gs_ref, gbuf, cut, FF // 2))):
        mine = whole.at[:, pl.ds(pl.multiple_of(core * buf.shape[1] + lo, 128), hi - lo)]
        here = pltpu.make_async_copy(mine, buf.at[pl.ds(0, rows), pl.ds(lo, hi - lo)], sems.at[2 * i])
        there = pltpu.make_async_copy(other.at[:, pl.ds(lo, hi - lo)],
                                      buf.at[pl.ds(rows, rows), pl.ds(lo, hi - lo)], sems.at[2 * i + 1])
        here.start()
        there.start()
        copies.append((here, there))

    def store(j, start, value):
        px, py = j // 4, j % 4
        at = pl.ds(start % HALF, value.shape[0])
        if start < HALF:
            x_ref[px * 4 + py, at, :] = value
        else:
            y_ref[py * 4 + px, at, :] = value

    def store_all(j, size, lead, row, value):
        done = 0
        while done < value.shape[0]:
            at = row + done
            n = min(size - at % size, value.shape[0] - done)
            store(j, (at // size) * CH + lead + at % size, value[done:done + n])
            done += n

    r = lax.broadcasted_iota(jnp.int32, (128, 128), 0)
    c = lax.broadcasted_iota(jnp.int32, (128, 128), 1)

    def diag(tile):
        return jnp.sum(jnp.where(r == c, tile, 0.0), axis=0, keepdims=True)

    act_sum = jnp.zeros((1, 128), F32)
    grad_sum = jnp.zeros((1, 128), F32)
    for copy in copies[0]:
        copy.wait()
    for k in range(8):
        g = gram(abuf[:, k * AB:(k + 1) * AB])
        t0, t2 = g[0:128, 0:128], g[128:256, 128:256]
        second = diag(t2)
        act_sum += diag(t0) + second
        t_ref[8 + k:9 + k, :] = second
        store_all(2 * k, AROWS, GROWS, 0, g[128:256, 0:128])
        store_all(2 * k + 1, AROWS, GROWS, 0, jnp.where(r >= c, t0, t2))
    for j in range(16):
        if j in (0, 8):
            for copy in copies[1 + j // 8]:
                copy.wait()
        g = gram(gbuf[:, j * GB:(j + 1) * GB])
        t0, t2 = g[0:128, 0:128], g[128:256, 128:256]
        t5 = jnp.concatenate([g[256:344, 256:344], jnp.zeros((88, 40), F32)], axis=1)
        second = diag(t2)
        grad_sum += diag(t0) + second + jnp.sum(jnp.where(r[:88] == c[:88], t5, 0.0), axis=0, keepdims=True)
        tail = jnp.concatenate([pltpu.roll(t5[48:88], 40, 1), jnp.zeros((8, 128), F32)], axis=0)
        store_all(j, GROWS, 0, 0, g[128:256, 0:128])
        store_all(j, GROWS, 0, 128, jnp.where(r >= c, t0, t2))
        store_all(j, GROWS, 0, 256, g[256:344, 0:128])
        store_all(j, GROWS, 0, 344, g[256:344, 128:256])
        store_all(j, GROWS, 0, 432, jnp.where(c[:48] < 88, t5[0:48], tail))
        store_all(j, GROWS, 0, 480, jnp.concatenate([second, jnp.zeros((31, 128), F32)], axis=0))
    t_ref[0:8, :] = jnp.concatenate([act_sum, grad_sum, jnp.zeros((6, 128), F32)], axis=0)


def grams(acts, grads, sib_acts, sib_grads):
    shape = jax.ShapeDtypeStruct((16, HALF, 128), F32)
    vmem = pl.BlockSpec(memory_space=pltpu.VMEM)
    rows = acts.shape[0]
    return pl.pallas_call(
        gram_kernel,
        out_shape=(shape, shape, jax.ShapeDtypeStruct((16, 128), F32)),
        in_specs=[pl.BlockSpec(memory_space=pl.ANY)] * 4,
        out_specs=(vmem,) * 3,
        scratch_shapes=[pltpu.VMEM((2 * rows, D // 2), acts.dtype), pltpu.VMEM((2 * rows, FF // 2), acts.dtype),
                        pltpu.SemaphoreType.DMA((6,))],
        compiler_params=pltpu.CompilerParams(vmem_limit_bytes=VLIM),
        name="grams",
    )(acts, grads, sib_acts, sib_grads)


def reduce_kernel(gx, gy, tr, fg_out, fa_out, t_out,
                  sx, sy, rx, ry, rx2, ry2, st, rz, fin, fg, fa, t1, t2, t3, q1, q2, q3, q4, tt,
                  local, s1, r1, s2, r2, s3, r3, sg, rg, sa, ra, s4, r4):
    dp, own = place()
    core = lax.rem(dp, 2)
    zh = lax.rem(dp // 2, 2)
    y = dp // 4
    x = lax.rem(own, 4)
    zl = own // 4
    z = zh * 4 + zl
    sib = dp + 1 - 2 * core

    def at(ax, ay, az, ac):
        return ((ay * 2 + az // 4) * 2 + ac, lax.rem(az, 4) * 4 + ax)

    xs = [at(lax.rem(x + k, 4), y, z, core) for k in (1, 2, 3)]
    ys = [at(x, lax.rem(y + k, 4), z, core) for k in (1, 2, 3)]
    zs = [at(x, y, lax.rem(z + k, 8), core) for k in range(1, 8)]
    j = x * 4 + y
    unit = core * 8 + j // 2
    part = lax.rem(j, 2)

    barrier = pltpu.get_barrier_semaphore()

    def greet(device):
        pl.semaphore_signal(barrier, inc=1, device_id=device, device_id_type=MESH)

    for device in xs + ys + zs + [(sib, own)]:
        greet(device)

    def greet_sources(base):
        def body(i, _):
            js = lax.rem(base, 8) * 2 + i // 8
            device = at(js // 4, lax.rem(js, 4), lax.rem(i, 8), base // 8)

            @pl.when(jnp.logical_or(device[0] != dp, device[1] != own))
            def _():
                greet(device)
            return 0
        lax.fori_loop(0, 16, body, 0)

    greet_sources(dp)
    greet_sources(own)
    self_g = jnp.where(unit == dp, 1, 0)
    self_a = jnp.where(unit == own, 1, 0)
    pl.semaphore_wait(barrier, 14 + 32 - self_g - self_a)

    def send(src, dst, ssem, rsem, device):
        copy = pltpu.make_async_remote_copy(src_ref=src, dst_ref=dst, send_sem=ssem, recv_sem=rsem,
                                            device_id=device, device_id_type=MESH)
        copy.start()
        return copy

    copies = []
    for k in range(3):
        copies.append(send(gx.at[pl.ds(lax.rem(x + k + 1, 4) * 4, 4)], rx.at[k], s1.at[k], r1.at[k], xs[k]))
        copies.append(send(gy.at[pl.ds(lax.rem(y + k + 1, 4) * 4, 4)], ry.at[k], s1.at[3 + k], r1.at[3 + k], ys[k]))
        copies.append(send(tr, q1.at[k], s1.at[6 + k], r1.at[6 + k], xs[k]))
    copies.append(pltpu.make_async_copy(gx.at[pl.ds(x * 4, 4)], sx, local.at[0]))
    copies[-1].start()
    copies.append(pltpu.make_async_copy(gy.at[pl.ds(y * 4, 4)], sy, local.at[1]))
    copies[-1].start()
    for copy in copies:
        copy.wait()

    @pl.loop(0, 16)
    def _(i):
        a = i // 4
        rows = pl.ds(pl.multiple_of(lax.rem(i, 4) * CH, 8), CH)
        sx[a, rows, :] = (sx[a, rows, :] + rx[0, a, rows, :]) + (rx[1, a, rows, :] + rx[2, a, rows, :])
        sy[a, rows, :] = (sy[a, rows, :] + ry[0, a, rows, :]) + (ry[1, a, rows, :] + ry[2, a, rows, :])
    t1[...] = (tr[...] + q1[0]) + (q1[1] + q1[2])

    copies = []
    for k in range(3):
        copies.append(send(sx.at[lax.rem(y + k + 1, 4)], rx2.at[k], s2.at[k], r2.at[k], ys[k]))
        copies.append(send(sy.at[lax.rem(x + k + 1, 4)], ry2.at[k], s2.at[3 + k], r2.at[3 + k], xs[k]))
        copies.append(send(t1, q2.at[k], s2.at[6 + k], r2.at[6 + k], ys[k]))
    for copy in copies:
        copy.wait()

    @pl.loop(0, 4)
    def _(i):
        rows = pl.ds(pl.multiple_of(i * CH, 8), CH)
        st[i] = (sx[y, rows, :] + rx2[0, rows, :]) + (rx2[1, rows, :] + rx2[2, rows, :])
        st[4 + i] = (sy[x, rows, :] + ry2[0, rows, :]) + (ry2[1, rows, :] + ry2[2, rows, :])
    t2[...] = (t1[...] + q2[0]) + (q2[1] + q2[2])

    copies = []
    for k in range(7):
        copies.append(send(st.at[lax.rem(z + k + 1, 8)], rz.at[k], s3.at[k], r3.at[k], zs[k]))
        copies.append(send(t2, q3.at[k], s3.at[7 + k], r3.at[7 + k], zs[k]))
    for copy in copies:
        copy.wait()
    total = st[z]
    trace = t2[...]
    for k in range(7):
        total += rz[k]
        trace += q3[k]
    fin[...] = total
    t3[...] = trace

    side = send(t3, q4, s4, r4, (sib, own))
    gsrc = fin.at[pl.ds(0, GROWS)]
    asrc = fin.at[pl.ds(GROWS, AROWS)]
    gdst = fg.at[part, z]
    adst = fa.at[part, z]
    slot = part * 8 + z

    def put(src, dst, ssem, rsem, device, mine):
        @pl.when(mine)
        def _():
            pltpu.make_async_copy(src, dst, rsem).start()

        @pl.when(jnp.logical_not(mine))
        def _():
            send(src, dst, ssem, rsem, device)

    put(gsrc, gdst, sg.at[0], rg.at[slot], (unit, own), unit == dp)
    put(asrc, adst, sa.at[0], ra.at[slot], (dp, unit), unit == own)

    def out(k, _):
        send(gsrc, gdst, sg.at[k], rg.at[slot], (unit, lax.rem(own + k, 16)))
        send(asrc, adst, sa.at[k], ra.at[slot], (lax.rem(dp + k, 16), unit))
        return 0
    lax.fori_loop(1, 16, out, 0)

    def sent(src, dst, ssem):
        pltpu.make_async_remote_copy(src_ref=src, dst_ref=dst, send_sem=ssem, recv_sem=r4,
                                     device_id=(sib, own), device_id_type=MESH).wait_send()

    def got(dst, src, rsem):
        pltpu.make_async_copy(src, dst, rsem).wait()

    def arrive(k, _):
        got(fg.at[k // 8, lax.rem(k, 8)], gsrc, rg.at[k])
        got(fa.at[k // 8, lax.rem(k, 8)], asrc, ra.at[k])
        return 0
    lax.fori_loop(0, 16, arrive, 0)

    def left(k, _):
        sent(gsrc, gdst, sg.at[k])
        sent(asrc, adst, sa.at[k])
        return 0
    lax.fori_loop(1, 16, left, 0)

    @pl.when(unit != dp)
    def _():
        sent(gsrc, gdst, sg.at[0])

    @pl.when(unit != own)
    def _():
        sent(asrc, adst, sa.at[0])
    side.wait()
    fg_out[...] = fg[...]
    fa_out[...] = fa[...]
    tt[core] = t3[...]
    tt[1 - core] = q4[...]
    t_out[0:8, :] = tt[0, 0:8, :] + tt[1, 0:8, :]
    t_out[8:16, :] = jnp.broadcast_to(tt[own // 8, pl.ds(8 + lax.rem(own, 8), 1), :], (8, 128))


def reduce_all(gx, gy, tr):
    vmem = pl.BlockSpec(memory_space=pltpu.VMEM)
    dma = pltpu.SemaphoreType.DMA
    tile = pltpu.VMEM((16, 128), F32)
    return pl.pallas_call(
        reduce_kernel,
        out_shape=(jax.ShapeDtypeStruct((2, 8, GROWS, 128), F32),
                   jax.ShapeDtypeStruct((2, 8, AROWS, 128), F32),
                   jax.ShapeDtypeStruct((16, 128), F32)),
        in_specs=[pl.BlockSpec(memory_space=pl.ANY)] * 2 + [vmem],
        out_specs=(vmem,) * 3,
        scratch_shapes=[
            pltpu.VMEM((4, HALF, 128), F32), pltpu.VMEM((4, HALF, 128), F32),
            pltpu.VMEM((3, 4, HALF, 128), F32), pltpu.VMEM((3, 4, HALF, 128), F32),
            pltpu.VMEM((3, HALF, 128), F32), pltpu.VMEM((3, HALF, 128), F32),
            pltpu.VMEM((8, CH, 128), F32), pltpu.VMEM((7, CH, 128), F32), pltpu.VMEM((CH, 128), F32),
            pltpu.VMEM((2, 8, GROWS, 128), F32), pltpu.VMEM((2, 8, AROWS, 128), F32),
            tile, tile, tile,
            pltpu.VMEM((3, 16, 128), F32), pltpu.VMEM((3, 16, 128), F32), pltpu.VMEM((7, 16, 128), F32), tile, pltpu.VMEM((2, 16, 128), F32),
            dma((2,)), dma((9,)), dma((9,)), dma((9,)), dma((9,)), dma((14,)), dma((14,)),
            dma((16,)), dma((16,)), dma((16,)), dma((16,)), dma, dma,
        ],
        compiler_params=pltpu.CompilerParams(collective_id=1, has_side_effects=True, vmem_limit_bytes=VLIM),
        name="reduce_all",
    )(gx, gy, tr)


def dot(a, b, ca=1, cb=0):
    return lax.dot_general(a, b, (((ca,), (cb,)), ((), ())), precision=HIGH, preferred_element_type=F32)


def split(v):
    high = v.astype(jnp.bfloat16).astype(F32)
    rest = v - high
    mid = rest.astype(jnp.bfloat16).astype(F32)
    return high, mid, rest - mid


def outer(a, b):
    ah, am, al = split(a)
    bh, bm, bl = split(b)
    left = jnp.concatenate([ah, ah, am, ah, am, al], axis=0).astype(jnp.bfloat16)
    right = jnp.concatenate([bh, bm, bh, bl, bm, bh], axis=0).astype(jnp.bfloat16)
    return lax.dot_general(left, right, (((0,), (0,)), ((), ())), preferred_element_type=F32)


def sweep_four(now, at, row, sub, lane):
    def full(v):
        return jnp.broadcast_to(v, (8, 128))

    four = range(4)
    cols = [full(now[:, at + i:at + i + 1]) for i in four]
    rows = [full(now[row + i:row + i + 1, :]) for i in four]
    m = {(i, j): full(cols[j][row + i:row + i + 1, :]) for i in four for j in range(i + 1)}
    for p in four:
        inv = 1.0 / m[(p, p)]
        line = {i: m[(max(i, p), min(i, p))] * inv for i in four if i != p}
        new = {}
        for i in four:
            for j in range(i + 1):
                if i == p and j == p:
                    new[(i, j)] = -inv
                elif i == p:
                    new[(i, j)] = line[j]
                elif j == p:
                    new[(i, j)] = line[i]
                else:
                    new[(i, j)] = m[(i, j)] - m[(max(i, p), min(i, p))] * line[j]
        m = new
    in_rows = jnp.logical_and(sub >= row, sub < row + 4)
    in_cols = jnp.logical_and(lane >= at, lane < at + 4)
    out = jnp.where(jnp.logical_or(in_rows, in_cols), 0.0, now)
    rows = [jnp.where(in_cols, jnp.where(lane == at + i, -1.0, 0.0), rows[i]) for i in four]
    for i in four:
        col = jnp.where(in_rows, jnp.where(sub == row + i, -1.0, 0.0), cols[i])
        term = m[(i, 0)] * rows[0]
        for j in range(1, 4):
            term = term + m[(max(i, j), min(i, j))] * rows[j]
        out = out + col * term
    return out


def sweep_tiles(refs, panels):
    sub = lax.broadcasted_iota(jnp.int32, (8, 128), 0)
    lane = lax.broadcasted_iota(jnp.int32, (8, 128), 1)
    lane_all = lax.broadcasted_iota(jnp.int32, (128, 128), 1)
    for p in range(panels):
        base = 8 * p
        inside = jnp.logical_and(lane_all >= base, lane_all < base + 8)
        olds = [ref[base:base + 8, :] for ref in refs]
        news = [sweep_four(old, base, 0, sub, lane) for old in olds]
        news = [sweep_four(new, base + 4, 4, sub, lane) for new in news]
        for ref, old, new in zip(refs, olds, news):
            ref[...] = jnp.where(inside, 0.0, ref[...]) - outer(old, new)
            ref[base:base + 8, :] = new


def solve_kernel(fg_ref, fa_ref, t_ref, w_ref, p_ref, g_ref, a_ref, gi_ref, ai_ref):
    act_trace = jnp.sum(t_ref[0:1, :], keepdims=True) / TOKENS
    grad_trace = jnp.sum(t_ref[1:2, :], keepdims=True) / TOKENS
    ratio = jnp.sqrt(act_trace / D / (grad_trace / FF))
    act_damp = ratio * DAMP
    grad_damp = DAMP / ratio
    r = lax.broadcasted_iota(jnp.int32, (128, 128), 0)
    c = lax.broadcasted_iota(jnp.int32, (128, 128), 1)
    last = GB - 256

    def pair(both, second):
        turned = both.T
        first = jnp.where(r >= c, both, turned)
        other = jnp.where(r < c, both, jnp.where(r == c, jnp.broadcast_to(second, (128, 128)), turned))
        return first, other

    def damped(tile, damp):
        return tile / TOKENS + jnp.where(r == c, damp, 0.0)

    zeros = jnp.zeros((128 - last, 128), F32)
    for b in range(2):
        first, second = pair(fg_ref[b, 128:256, :], fg_ref[b, 480:481, :])
        g_ref[b * 6] = damped(first, grad_damp)
        g_ref[b * 6 + 1] = fg_ref[b, 0:128, :] / TOKENS
        g_ref[b * 6 + 2] = damped(second, grad_damp)
        g_ref[b * 6 + 3] = jnp.concatenate([fg_ref[b, 256:344, :] / TOKENS, zeros], axis=0)
        g_ref[b * 6 + 4] = jnp.concatenate([fg_ref[b, 344:432, :] / TOKENS, zeros], axis=0)
        packed = fg_ref[b, 432:480, :]
        low = pltpu.roll(packed[0:40], 88, 1)
        upper = jnp.concatenate([packed, low, jnp.zeros((40, 128), F32)], axis=0)
        corner = jnp.where(jnp.logical_and(r >= 48, c < 48), upper.T, upper)
        inside = jnp.logical_and(r < last, c < last)
        g_ref[b * 6 + 5] = jnp.where(inside, damped(corner, grad_damp), jnp.where(r == c, 1.0, 0.0))
    first, second = pair(fa_ref[128:256, :], t_ref[8:9, :])
    a_ref[0] = damped(first, act_damp)
    a_ref[1] = fa_ref[0:128, :] / TOKENS
    a_ref[2] = damped(second, act_damp)
    gs = [[g_ref.at[b * 6 + t] for t in range(6)] for b in range(2)]
    am = [a_ref.at[t] for t in range(3)]
    sweep_tiles([gs[0][0], gs[1][0], am[0]], 16)
    for m in gs:
        neg = m[0][...]
        a10, a20 = m[1][...], m[3][...]
        v10, v20 = -dot(a10, neg), -dot(a20, neg)
        m[2][...] -= dot(v10, a10, 1, 1)
        m[4][...] -= dot(v20, a10, 1, 1)
        m[5][...] -= dot(v20, a20, 1, 1)
        m[1][...] = v10
        m[3][...] = v20
    a10 = am[1][...]
    v10 = -dot(a10, am[0][...])
    am[2][...] -= dot(v10, a10, 1, 1)
    am[1][...] = v10
    sweep_tiles([gs[0][2], gs[1][2], am[2]], 16)
    for m in gs:
        neg = m[2][...]
        a10, a21 = m[1][...], m[4][...]
        v10, v21 = -dot(neg, a10), -dot(a21, neg)
        m[0][...] -= dot(a10, v10, 0, 0)
        m[3][...] -= dot(a21, v10)
        m[5][...] -= dot(v21, a21, 1, 1)
        m[1][...] = v10
        m[4][...] = v21
    a10 = am[1][...]
    v10 = -dot(am[2][...], a10)
    am[0][...] -= dot(a10, v10, 0, 0)
    am[1][...] = v10
    sweep_tiles([gs[0][5], gs[1][5]], last // 8)
    for m in gs:
        neg = m[5][...]
        a20, a21 = m[3][...], m[4][...]
        v20, v21 = -dot(neg, a20), -dot(neg, a21)
        m[0][...] -= dot(a20, v20, 0, 0)
        m[1][...] -= dot(a21, v20, 0, 0)
        m[2][...] -= dot(a21, v21, 0, 0)
        m[3][...] = v20
        m[4][...] = v21
    ai_ref[0:128, 0:128] = -am[0][...]
    ai_ref[128:256, 0:128] = -am[1][...]
    ai_ref[0:128, 128:256] = -am[1][...].T
    ai_ref[128:256, 128:256] = -am[2][...]
    for b, m in enumerate(gs):
        for t, (i, j) in enumerate(((0, 0), (1, 0), (1, 1), (2, 0), (2, 1), (2, 2))):
            tile = -m[t][...]
            gi_ref[b, i * 128:(i + 1) * 128, j * 128:(j + 1) * 128] = tile
            if i != j:
                gi_ref[b, j * 128:(j + 1) * 128, i * 128:(i + 1) * 128] = tile.T
    for b in range(2):
        left = dot(ai_ref[...], w_ref[b].astype(F32))
        p_ref[:, b * 384:(b + 1) * 384] = dot(left, gi_ref[b]).astype(jnp.bfloat16)


def solve(fg, fa, tr, w):
    vmem = pl.BlockSpec(memory_space=pltpu.VMEM)
    return pl.pallas_call(
        solve_kernel,
        out_shape=jax.ShapeDtypeStruct((256, 768), jnp.bfloat16),
        in_specs=[vmem] * 4,
        out_specs=vmem,
        scratch_shapes=[pltpu.VMEM((12, 128, 128), F32), pltpu.VMEM((3, 128, 128), F32),
                        pltpu.VMEM((2, 384, 384), F32), pltpu.VMEM((256, 256), F32)],
        compiler_params=pltpu.CompilerParams(vmem_limit_bytes=VLIM),
        name="solve",
    )(fg, fa, tr, w)


def gather_kernel(p_ref, o_ref, local, sz, rz, sy, ry, sh, rh, sc, rc):
    dp, own = place()
    core = lax.rem(dp, 2)
    y = dp // 4
    sib = dp + 1 - 2 * core
    zh = lax.rem(dp // 2, 2)
    anti = dp + 2 - 4 * zh
    up = lax.rem(y + 1, 4) * 4 + lax.rem(dp, 4)
    down = lax.rem(y + 3, 4) * 4 + lax.rem(dp, 4)
    barrier = pltpu.get_barrier_semaphore()
    for device in (sib, anti, up, down):
        pl.semaphore_signal(barrier, inc=1, device_id=(device, own), device_id_type=MESH)
    pl.semaphore_wait(barrier, 4)

    def other(d):
        return d + 2 - 4 * lax.rem(d // 2, 2)

    waits = []

    def send(d, ssem, rsem, device, src=None, half=None):
        src = o_ref.at[d] if src is None else src
        dst = o_ref.at[d]
        if half is not None:
            src = src.at[pl.ds(half * 128, 128)]
            dst = dst.at[pl.ds(half * 128, 128)]
        copy = pltpu.make_async_remote_copy(src_ref=src, dst_ref=dst, send_sem=ssem, recv_sem=rsem,
                                            device_id=(device, own), device_id_type=MESH)
        copy.start()
        waits.append(copy)

    def arrived(d, sem, half=None):
        dst = o_ref.at[d]
        if half is not None:
            dst = dst.at[pl.ds(half * 128, 128)]
        pltpu.make_async_remote_copy(src_ref=dst, dst_ref=dst, send_sem=sz, recv_sem=sem,
                                     device_id=(sib, own), device_id_type=MESH).wait_recv()

    send(dp, sz, rz, anti, p_ref)
    send(dp, sy.at[0], ry.at[0], up, p_ref)
    send(dp, sy.at[1], ry.at[1], down, p_ref)
    send(dp, sc.at[0], rc.at[0], sib, p_ref)
    keep = pltpu.make_async_copy(p_ref, o_ref.at[dp], local)
    keep.start()
    arrived(down, ry.at[0])
    send(down, sh.at[0], rh.at[0], up, half=0)
    send(down, sc.at[1], rc.at[1], sib)
    arrived(up, ry.at[1])
    send(up, sh.at[1], rh.at[1], down, half=1)
    send(up, sc.at[2], rc.at[2], sib)
    arrived(anti, rz)
    send(anti, sy.at[2], ry.at[2], up)
    send(anti, sy.at[3], ry.at[3], down)
    send(anti, sc.at[3], rc.at[3], sib)
    far = other(down) * 0 + lax.rem(y + 2, 4) * 4 + lax.rem(dp, 4)
    arrived(other(down), ry.at[2])
    send(other(down), sh.at[2], rh.at[2], up, half=0)
    send(other(down), sc.at[4], rc.at[4], sib)
    arrived(other(up), ry.at[3])
    send(other(up), sh.at[3], rh.at[3], down, half=1)
    send(other(up), sc.at[5], rc.at[5], sib)
    arrived(far, rh.at[0], half=0)
    arrived(far, rh.at[1], half=1)
    send(far, sc.at[6], rc.at[6], sib)
    arrived(other(far), rh.at[2], half=0)
    arrived(other(far), rh.at[3], half=1)
    send(other(far), sc.at[7], rc.at[7], sib)

    def twin(d):
        return d + 1 - 2 * lax.rem(d, 2)

    for i, d in enumerate((dp, down, up, anti, other(down), other(up), far, other(far))):
        arrived(twin(d), rc.at[i])
    keep.wait()
    for copy in waits:
        copy.wait_send()


def gather(p):
    dma = pltpu.SemaphoreType.DMA
    return pl.pallas_call(
        gather_kernel,
        out_shape=jax.ShapeDtypeStruct((16, 256, 768), jnp.bfloat16),
        in_specs=[pl.BlockSpec(memory_space=pl.ANY)],
        out_specs=pl.BlockSpec(memory_space=pl.ANY),
        scratch_shapes=[dma, dma, dma, dma((4,)), dma((4,)), dma((4,)), dma((4,)), dma((8,)), dma((8,))],
        compiler_params=pltpu.CompilerParams(collective_id=2, has_side_effects=True),
        name="gather",
    )(p)


def flat_kernel(i_ref, o_ref):
    for d in range(16):
        for b in range(2):
            start = (2 * d + b) * GB
            o_ref[:, start:start + GB] = i_ref[d, :, b * 384:b * 384 + GB]


def flatten(slices):
    rows = 64
    return pl.pallas_call(
        flat_kernel,
        out_shape=jax.ShapeDtypeStruct((256, FF), jnp.bfloat16),
        grid=(256 // rows,),
        in_specs=[pl.BlockSpec((16, rows, 768), lambda i: (0, i, 0))],
        out_specs=pl.BlockSpec((rows, FF), lambda i: (i, 0)),
        compiler_params=pltpu.CompilerParams(vmem_limit_bytes=VLIM),
        name="flatten",
    )(slices)


def shards(acts, grads_out, weight_grad):
    sib_acts, sib_grads = swap(acts, grads_out)
    gx, gy, tr = grams(acts, grads_out, sib_acts, sib_grads)
    fg, fa, tr = reduce_all(gx, gy, tr)
    w = jnp.pad(weight_grad.reshape(256, 2, GB).transpose(1, 0, 2), ((0, 0), (0, 0), (0, 384 - GB)))
    p = solve(fg.reshape(2, 8 * GROWS, 128), fa.reshape(16 * AROWS, 128), tr, w)
    return flatten(gather(p))


def solution(mesh):
    in_specs = (P(("dp", "owner"), None), P(("dp", "owner"), None), P("owner", "dp"))
    out_specs = P("owner", None)
    return jax.shard_map(shards, mesh=mesh, in_specs=in_specs, out_specs=out_specs, check_vma=False)
```

```python
import functools
import math

import jax
import jax.numpy as jnp
from jax import lax
from jax.experimental import pallas as pl
from jax.experimental.pallas import tpu as pltpu
from jax.sharding import PartitionSpec as P

D = 4096
FF = 11008
AB = 256
GB = 344
TOKENS = 57344
DAMP = math.sqrt(0.03)
MESH = pl.DeviceIdType.MESH
HIGH = lax.Precision.HIGHEST
F32 = jnp.float32
NB = 2
GROWS = 64 // NB
AROWS = 16 // NB
CH = GROWS + AROWS
HALF = 4 * CH
VLIM = 56 * 1024 * 1024


def position(j):
    x = 2 * (j // 2 % 2) + (j // 4 + j // 8) % 2
    y = 2 * (j % 2) + j // 8
    return x, y


def place():
    dp = lax.axis_index("dp")
    own = lax.axis_index("owner")
    return dp, own


def swap_kernel(a_ref, g_ref, ao_ref, go_ref, send, recv):
    dp, own = place()
    core = lax.rem(dp, 2)
    sib = dp + 1 - 2 * core
    barrier = pltpu.get_barrier_semaphore()
    pl.semaphore_signal(barrier, inc=1, device_id=(sib, own), device_id_type=MESH)
    pl.semaphore_wait(barrier, 1)
    copies = []
    for i, (src, dst) in enumerate(((a_ref, ao_ref), (g_ref, go_ref))):
        width = dst.shape[1]
        theirs = pl.ds(pl.multiple_of((1 - core) * width, 128), width)
        copy = pltpu.make_async_remote_copy(
            src_ref=src.at[:, theirs], dst_ref=dst, send_sem=send.at[i], recv_sem=recv.at[i],
            device_id=(sib, own), device_id_type=MESH)
        copy.start()
        copies.append(copy)
    for copy in copies:
        copy.wait()


def swap(acts, grads):
    rows = acts.shape[0]
    return pl.pallas_call(
        swap_kernel,
        out_shape=(jax.ShapeDtypeStruct((rows, D // 2), acts.dtype),
                   jax.ShapeDtypeStruct((rows, FF // 2), acts.dtype)),
        in_specs=[pl.BlockSpec(memory_space=pl.ANY)] * 2,
        out_specs=(pl.BlockSpec(memory_space=pl.ANY),) * 2,
        scratch_shapes=[pltpu.SemaphoreType.DMA((2,))] * 2,
        compiler_params=pltpu.CompilerParams(collective_id=0, has_side_effects=True),
        name="swap",
    )(acts, grads)


def gram(block):
    return lax.dot_general(block, block, (((0,), (0,)), ((), ())), preferred_element_type=F32)


def gram_kernel(a_ref, g_ref, as_ref, gs_ref, x_out, y_out, t_ref, abuf, gbuf, x_ref, y_ref, sems, out_sems):
    core = lax.rem(lax.axis_index("dp"), 2)
    rows = a_ref.shape[0]
    cut = 22 * 128
    copies = []
    for i, (whole, other, buf, lo, hi) in enumerate((
            (a_ref, as_ref, abuf, 0, D // 2), (g_ref, gs_ref, gbuf, 0, cut), (g_ref, gs_ref, gbuf, cut, FF // 2))):
        mine = whole.at[:, pl.ds(pl.multiple_of(core * buf.shape[1] + lo, 128), hi - lo)]
        here = pltpu.make_async_copy(mine, buf.at[pl.ds(0, rows), pl.ds(lo, hi - lo)], sems.at[2 * i])
        there = pltpu.make_async_copy(other.at[:, pl.ds(lo, hi - lo)],
                                      buf.at[pl.ds(rows, rows), pl.ds(lo, hi - lo)], sems.at[2 * i + 1])
        here.start()
        there.start()
        copies.append((here, there))

    def store_all(j, size, lead, row, value):
        px, py = position(j)
        done = 0
        while done < value.shape[0]:
            at = row + done
            n = min(size - at % size, value.shape[0] - done)
            chunk, batch = at // size // NB, at // size % NB
            rows_at = pl.ds(chunk % 4 * CH + lead + at % size, n)
            if chunk < 4:
                x_ref[batch, px * 4 + py, rows_at, :] = value[done:done + n]
            else:
                y_ref[batch, py * 4 + px, rows_at, :] = value[done:done + n]
            done += n

    outs = []

    def finish(j):
        px, py = position(j)
        for i, (src, dst, at) in enumerate(((x_ref, x_out, px * 4 + py), (y_ref, y_out, py * 4 + px))):
            copy = pltpu.make_async_copy(src.at[:, at], dst.at[:, at], out_sems.at[i, j])
            copy.start()
            outs.append(copy)

    r = lax.broadcasted_iota(jnp.int32, (128, 128), 0)
    c = lax.broadcasted_iota(jnp.int32, (128, 128), 1)

    def diag(tile):
        return jnp.sum(jnp.where(r == c, tile, 0.0), axis=0, keepdims=True)

    act_sum = jnp.zeros((1, 128), F32)
    grad_sum = jnp.zeros((1, 128), F32)
    for copy in copies[0]:
        copy.wait()
    for k in range(8):
        g = gram(abuf[:, k * AB:(k + 1) * AB])
        t0, t2 = g[0:128, 0:128], g[128:256, 128:256]
        second = diag(t2)
        act_sum += diag(t0) + second
        t_ref[8 + k:9 + k, :] = second
        store_all(2 * k, AROWS, GROWS, 0, g[128:256, 0:128])
        store_all(2 * k + 1, AROWS, GROWS, 0, jnp.where(r >= c, t0, t2))
    for j in range(16):
        if j in (0, 8):
            for copy in copies[1 + j // 8]:
                copy.wait()
        g = gram(gbuf[:, j * GB:(j + 1) * GB])
        t0, t2 = g[0:128, 0:128], g[128:256, 128:256]
        t5 = jnp.concatenate([g[256:344, 256:344], jnp.zeros((88, 40), F32)], axis=1)
        second = diag(t2)
        grad_sum += diag(t0) + second + jnp.sum(jnp.where(r[:88] == c[:88], t5, 0.0), axis=0, keepdims=True)
        tail = jnp.concatenate([pltpu.roll(t5[48:88], 40, 1), jnp.zeros((8, 128), F32)], axis=0)
        store_all(j, GROWS, 0, 0, g[128:256, 0:128])
        store_all(j, GROWS, 0, 128, jnp.where(r >= c, t0, t2))
        store_all(j, GROWS, 0, 256, g[256:344, 0:128])
        store_all(j, GROWS, 0, 344, g[256:344, 128:256])
        store_all(j, GROWS, 0, 432, jnp.where(c[:48] < 88, t5[0:48], tail))
        store_all(j, GROWS, 0, 480, jnp.concatenate([second, jnp.zeros((31, 128), F32)], axis=0))
        finish(j)
    t_ref[0:8, :] = jnp.concatenate([act_sum, grad_sum, jnp.zeros((6, 128), F32)], axis=0)
    for copy in outs:
        copy.wait()


def grams(acts, grads, sib_acts, sib_grads):
    shape = jax.ShapeDtypeStruct((NB, 16, HALF, 128), F32)
    vmem = pl.BlockSpec(memory_space=pltpu.VMEM)
    anywhere = pl.BlockSpec(memory_space=pl.ANY)
    rows = acts.shape[0]
    return pl.pallas_call(
        gram_kernel,
        out_shape=(shape, shape, jax.ShapeDtypeStruct((16, 128), F32)),
        in_specs=[anywhere] * 4,
        out_specs=(anywhere, anywhere, vmem),
        scratch_shapes=[pltpu.VMEM((2 * rows, D // 2), acts.dtype), pltpu.VMEM((2 * rows, FF // 2), acts.dtype),
                        pltpu.VMEM(shape.shape, F32), pltpu.VMEM(shape.shape, F32),
                        pltpu.SemaphoreType.DMA((6,)), pltpu.SemaphoreType.DMA((2, 16))],
        compiler_params=pltpu.CompilerParams(vmem_limit_bytes=VLIM),
        name="grams",
    )(acts, grads, sib_acts, sib_grads)


def reduce_kernel(gx, gy, tr, fg_out, fa_out, t_out,
                  ps, pk, pm, pr, rx2, ry2, st, rz, fin, ga, aa, fg, fa, t1, t2, t3, q1, q2, q3, q4, tt,
                  local, s1, r1, s2, r2, s3, r3, s4, rg4, ra4, s5, rg5, ra5, ts, tr_sem):
    dp, own = place()
    core = lax.rem(dp, 2)
    zh = lax.rem(dp // 2, 2)
    y = dp // 4
    x = lax.rem(own, 4)
    zl = own // 4
    z = zh * 4 + zl
    sib = dp + 1 - 2 * core

    def at(ax, ay, az, ac):
        return ((ay * 2 + az // 4) * 2 + ac, lax.rem(az, 4) * 4 + ax)

    xs = [at(lax.rem(x + k, 4), y, z, core) for k in (1, 2, 3)]
    ys = [at(x, lax.rem(y + k, 4), z, core) for k in (1, 2, 3)]
    zs = [at(x, y, lax.rem(z + k, 8), core) for k in range(1, 8)]
    j = 8 * (y % 2) + 4 * ((x + y) % 2) + 2 * (x // 2) + y // 2
    unit = core * 8 + j // 2
    part = lax.rem(j, 2)
    unit_zh = lax.rem(unit // 2, 2)
    unit_zl = unit // 4
    g_on = zh == unit_zh
    a_on = zl == unit_zl
    g_to = [(unit, zl * 4 + lax.rem(x + k, 4)) for k in range(4)]
    a_to = [((lax.rem(y + k // 2, 4) * 2 + zh) * 2 + lax.rem(core + k, 2), unit) for k in range(8)]
    g_self = unit == dp
    a_self = unit == own

    barrier = pltpu.get_barrier_semaphore()

    def greet(device):
        pl.semaphore_signal(barrier, inc=1, device_id=device, device_id_type=MESH)

    for device in xs + ys + zs + [(sib, own)]:
        greet(device)
    for base in (dp, own):
        for i in range(2):
            js = lax.rem(base, 8) * 2 + i
            source = at(*position(js), z, base // 8)

            @pl.when(jnp.logical_or(source[0] != dp, source[1] != own))
            def _():
                greet(source)
    g_count = jnp.where(g_on, 4 - jnp.where(g_self, 1, 0), 0)
    a_count = jnp.where(a_on, 8 - jnp.where(a_self, 1, 0), 0)
    pl.semaphore_wait(barrier, 14 + g_count + a_count)

    def remote(src, dst, ssem, rsem, device):
        return pltpu.make_async_remote_copy(src_ref=src, dst_ref=dst, send_sem=ssem, recv_sem=rsem,
                                            device_id=device, device_id_type=MESH)

    def begin(copies):
        for copy in copies:
            copy.start()
        return copies

    def end(copies):
        for copy in copies:
            copy.wait()

    axes = ((0, gx, x, (xs[0], xs[2])), (1, gy, y, (ys[0], ys[2])))

    def plane(b):
        copies = []
        for a, g, me, (up, down) in axes:
            over, under, opposite = lax.rem(me + 1, 4) * 4, lax.rem(me + 3, 4) * 4, lax.rem(me + 2, 4) * 4
            copies.append(remote(g.at[b, pl.ds(opposite, 2)], pm.at[a, b, 0], s1.at[a, b, 0], r1.at[a, b, 0], up))
            copies.append(remote(g.at[b, pl.ds(opposite + 2, 2)], pm.at[a, b, 1],
                                 s1.at[a, b, 1], r1.at[a, b, 1], down))
            copies.append(pltpu.make_async_copy(g.at[b, pl.ds(over, 2)], pk.at[a, b, 0], local.at[a, b, 0]))
            copies.append(pltpu.make_async_copy(g.at[b, pl.ds(under + 2, 2)], pk.at[a, b, 1], local.at[a, b, 1]))
        for a, g, me, (up, down) in axes:
            over, under = lax.rem(me + 1, 4) * 4, lax.rem(me + 3, 4) * 4
            copies.append(remote(g.at[b, pl.ds(over + 2, 2)], pr.at[a, b, 0, pl.ds(2, 2)],
                                 s1.at[a, b, 2], r1.at[a, b, 2], up))
            copies.append(remote(g.at[b, pl.ds(under, 2)], pr.at[a, b, 1, pl.ds(0, 2)],
                                 s1.at[a, b, 3], r1.at[a, b, 3], down))
            copies.append(pltpu.make_async_copy(g.at[b, pl.ds(me * 4, 4)], ps.at[a, b], local.at[a, b, 2]))
        return begin(copies)

    def plane_pass(b, copies):
        end(copies[:8])
        @pl.loop(0, 8)
        def _(i):
            h, rows = i // 4, pl.ds(pl.multiple_of(lax.rem(i, 4) * CH, 8), CH)
            for a in range(2):
                for d in range(2):
                    pk[a, b, d, h, rows, :] += pm[a, b, d, h, rows, :]
        for a, _, _, to in axes:
            for d in range(2):
                copies.append(remote(pk.at[a, b, d], pr.at[a, b, d, pl.ds(2 * d, 2)],
                                     s1.at[a, b, 4 + d], r1.at[a, b, 4 + d], to[d]))
                copies[-1].start()

    def plane_sum(b, copies):
        end(copies[8:])
        @pl.loop(0, 16)
        def _(i):
            q, rows = i // 4, pl.ds(pl.multiple_of(lax.rem(i, 4) * CH, 8), CH)
            for a in range(2):
                ps[a, b, q, rows, :] += pr[a, b, 0, q, rows, :] + pr[a, b, 1, q, rows, :]

    def cross(b):
        copies = []
        for k in range(3):
            copies.append(remote(ps.at[0, b, lax.rem(y + k + 1, 4)], rx2.at[b, k], s2.at[b, k], r2.at[b, k], ys[k]))
            copies.append(remote(ps.at[1, b, lax.rem(x + k + 1, 4)], ry2.at[b, k],
                                 s2.at[b, 3 + k], r2.at[b, 3 + k], xs[k]))
        return begin(copies)

    def cross_sum(b):
        @pl.loop(0, 4)
        def _(i):
            rows = pl.ds(pl.multiple_of(i * CH, 8), CH)
            st[b, i] = (ps[0, b, y, rows, :] + rx2[b, 0, rows, :]) + (rx2[b, 1, rows, :] + rx2[b, 2, rows, :])
            st[b, 4 + i] = (ps[1, b, x, rows, :] + ry2[b, 0, rows, :]) + (ry2[b, 1, rows, :] + ry2[b, 2, rows, :])

    def along(b):
        return begin([remote(st.at[b, lax.rem(z + k + 1, 8)], rz.at[b, k], s3.at[b, k], r3.at[b, k], zs[k])
                      for k in range(7)])

    def along_sum(b):
        total = st[b, z]
        for k in range(7):
            total += rz[b, k]
        fin[b] = total

    def spread(b):
        for i in range(6):
            if i < 4:
                to = unit_zh * 4 + i
                src, dst, rsem = fin.at[b, pl.ds(0, GROWS)], ga.at[b, z], rg4.at[b, z]
            else:
                to = (i - 4) * 4 + unit_zl
                src, dst, rsem = fin.at[b, pl.ds(GROWS, AROWS)], aa.at[b, z], ra4.at[b, z]

            @pl.when(to == z)
            def _():
                pltpu.make_async_copy(src, dst, rsem).start()

            @pl.when(to != z)
            def _():
                remote(src, dst, s4.at[b, i], rsem, at(x, y, to, core)).start()

    def spread_sent(b):
        for i in range(6):
            to = unit_zh * 4 + i if i < 4 else (i - 4) * 4 + unit_zl
            src = fin.at[b, pl.ds(0, GROWS)] if i < 4 else fin.at[b, pl.ds(GROWS, AROWS)]
            dst, rsem = (ga.at[b, z], rg4.at[b, z]) if i < 4 else (aa.at[b, z], ra4.at[b, z])

            @pl.when(to != z)
            def _():
                remote(src, dst, s4.at[b, i], rsem, at(x, y, to, core)).wait_send()

    def give(b):
        for on, mine, src, all_to, dst, rsem, first in (
                (g_on, g_self, ga.at[b], g_to, fg.at[part, b], rg5.at[b, part], 0),
                (a_on, a_self, aa.at[b], a_to, fa.at[part, b], ra5.at[b, part], 4)):
            @pl.when(on)
            def _():
                for i in range(8):
                    piece = fin.at[b, pl.ds(0, GROWS)] if first == 0 else fin.at[b, pl.ds(GROWS, AROWS)]
                    arrive = (rg4 if first == 0 else ra4).at[b, i]
                    pltpu.make_async_copy(piece, src.at[i], arrive).wait()
                for i, device in enumerate(all_to):
                    if i == 0:
                        @pl.when(mine)
                        def _():
                            pltpu.make_async_copy(src, dst, rsem).start()

                        @pl.when(jnp.logical_not(mine))
                        def _():
                            remote(src, dst, s5.at[b, first], rsem, device).start()
                    else:
                        remote(src, dst, s5.at[b, first + i], rsem, device).start()

    def given(b):
        for on, mine, src, all_to, dst, rsem, first in (
                (g_on, g_self, ga.at[b], g_to, fg.at[part, b], rg5.at[b, part], 0),
                (a_on, a_self, aa.at[b], a_to, fa.at[part, b], ra5.at[b, part], 4)):
            @pl.when(on)
            def _():
                for i, device in enumerate(all_to):
                    copy = remote(src, dst, s5.at[b, first + i], rsem, device)
                    if i == 0:
                        @pl.when(jnp.logical_not(mine))
                        def _():
                            copy.wait_send()
                    else:
                        copy.wait_send()

    def taken(b):
        for i in range(2):
            pltpu.make_async_copy(ga.at[b], fg.at[i, b], rg5.at[b, i]).wait()
            pltpu.make_async_copy(aa.at[b], fa.at[i, b], ra5.at[b, i]).wait()

    batches = range(NB)
    q = begin([remote(tr, q1.at[k], ts.at[k], tr_sem.at[k], xs[k]) for k in range(3)])
    second, third = [], []
    first = [plane(0)]
    plane_pass(0, first[0])
    for b in batches:
        if b + 1 < NB:
            first.append(plane(b + 1))
        plane_sum(b, first[b])
        second.append(cross(b))
        if b + 1 < NB:
            plane_pass(b + 1, first[b + 1])
    end(q)
    t1[...] = (tr[...] + q1[0]) + (q1[1] + q1[2])
    q = begin([remote(t1, q2.at[k], ts.at[3 + k], tr_sem.at[3 + k], ys[k]) for k in range(3)])
    for b in batches:
        end(second[b])
        cross_sum(b)
        third.append(along(b))
    end(q)
    t2[...] = (t1[...] + q2[0]) + (q2[1] + q2[2])
    q = begin([remote(t2, q3.at[k], ts.at[6 + k], tr_sem.at[6 + k], zs[k]) for k in range(7)])
    for b in batches:
        end(third[b])
        along_sum(b)
        spread(b)
    end(q)
    trace = t2[...]
    for k in range(7):
        trace += q3[k]
    t3[...] = trace
    q = begin([remote(t3, q4, ts.at[13], tr_sem.at[13], (sib, own))])
    for b in batches:
        give(b)
    end(q)
    tt[core] = t3[...]
    tt[1 - core] = q4[...]
    t_out[0:8, :] = tt[0, 0:8, :] + tt[1, 0:8, :]
    t_out[8:16, :] = jnp.broadcast_to(tt[own // 8, pl.ds(8 + lax.rem(own, 8), 1), :], (8, 128))
    for b in batches:
        taken(b)
        for i in range(2):
            for k in range(8):
                fg_out[i, k, b * GROWS:(b + 1) * GROWS, :] = fg[i, b, k]
                fa_out[i, k, b * AROWS:(b + 1) * AROWS, :] = fa[i, b, k]
    for b in batches:
        spread_sent(b)
        given(b)


def reduce_all(gx, gy, tr):
    vmem = pl.BlockSpec(memory_space=pltpu.VMEM)
    dma = pltpu.SemaphoreType.DMA
    tile = pltpu.VMEM((16, 128), F32)

    def buf(*shape):
        return pltpu.VMEM(shape + (128,), F32)

    return pl.pallas_call(
        reduce_kernel,
        out_shape=(jax.ShapeDtypeStruct((2, 8, NB * GROWS, 128), F32),
                   jax.ShapeDtypeStruct((2, 8, NB * AROWS, 128), F32),
                   jax.ShapeDtypeStruct((16, 128), F32)),
        in_specs=[pl.BlockSpec(memory_space=pl.ANY)] * 2 + [vmem],
        out_specs=(vmem,) * 3,
        scratch_shapes=[
            buf(2, NB, 4, HALF), buf(2, NB, 2, 2, HALF), buf(2, NB, 2, 2, HALF), buf(2, NB, 2, 4, HALF),
            buf(NB, 3, HALF), buf(NB, 3, HALF), buf(NB, 8, CH), buf(NB, 7, CH), buf(NB, CH),
            buf(NB, 8, GROWS), buf(NB, 8, AROWS), buf(2, NB, 8, GROWS), buf(2, NB, 8, AROWS),
            tile, tile, tile, buf(3, 16), buf(3, 16), buf(7, 16), tile, buf(2, 16),
            dma((2, NB, 3)), dma((2, NB, 6)), dma((2, NB, 6)), dma((NB, 6)), dma((NB, 6)), dma((NB, 7)), dma((NB, 7)),
            dma((NB, 6)), dma((NB, 8)), dma((NB, 8)), dma((NB, 12)), dma((NB, 2)), dma((NB, 2)), dma((14,)), dma((14,)),
        ],
        compiler_params=pltpu.CompilerParams(collective_id=1, has_side_effects=True, vmem_limit_bytes=VLIM),
        name="reduce_all",
    )(gx, gy, tr)


def dot(a, b, ca=1, cb=0):
    return lax.dot_general(a, b, (((ca,), (cb,)), ((), ())), precision=HIGH, preferred_element_type=F32)


def split(v):
    high = v.astype(jnp.bfloat16).astype(F32)
    rest = v - high
    mid = rest.astype(jnp.bfloat16).astype(F32)
    return high, mid, rest - mid


def outer(a, b):
    ah, am, al = split(a)
    bh, bm, bl = split(b)
    left = jnp.concatenate([ah, ah, am, ah, am, al], axis=0).astype(jnp.bfloat16)
    right = jnp.concatenate([bh, bm, bh, bl, bm, bh], axis=0).astype(jnp.bfloat16)
    return lax.dot_general(left, right, (((0,), (0,)), ((), ())), preferred_element_type=F32)


def sweep_four(now, at, row, sub, lane):
    def full(v):
        return jnp.broadcast_to(v, (8, 128))

    four = range(4)
    cols = [full(now[:, at + i:at + i + 1]) for i in four]
    rows = [full(now[row + i:row + i + 1, :]) for i in four]
    m = {(i, j): full(cols[j][row + i:row + i + 1, :]) for i in four for j in range(i + 1)}
    for p in four:
        inv = 1.0 / m[(p, p)]
        line = {i: m[(max(i, p), min(i, p))] * inv for i in four if i != p}
        new = {}
        for i in four:
            for j in range(i + 1):
                if i == p and j == p:
                    new[(i, j)] = -inv
                elif i == p:
                    new[(i, j)] = line[j]
                elif j == p:
                    new[(i, j)] = line[i]
                else:
                    new[(i, j)] = m[(i, j)] - m[(max(i, p), min(i, p))] * line[j]
        m = new
    in_rows = jnp.logical_and(sub >= row, sub < row + 4)
    in_cols = jnp.logical_and(lane >= at, lane < at + 4)
    out = jnp.where(jnp.logical_or(in_rows, in_cols), 0.0, now)
    rows = [jnp.where(in_cols, jnp.where(lane == at + i, -1.0, 0.0), rows[i]) for i in four]
    for i in four:
        col = jnp.where(in_rows, jnp.where(sub == row + i, -1.0, 0.0), cols[i])
        term = m[(i, 0)] * rows[0]
        for j in range(1, 4):
            term = term + m[(max(i, j), min(i, j))] * rows[j]
        out = out + col * term
    return out


def sweep_tiles(refs, panels):
    sub = lax.broadcasted_iota(jnp.int32, (8, 128), 0)
    lane = lax.broadcasted_iota(jnp.int32, (8, 128), 1)
    lane_all = lax.broadcasted_iota(jnp.int32, (128, 128), 1)
    for p in range(panels):
        base = 8 * p
        inside = jnp.logical_and(lane_all >= base, lane_all < base + 8)
        olds = [ref[base:base + 8, :] for ref in refs]
        news = [sweep_four(old, base, 0, sub, lane) for old in olds]
        news = [sweep_four(new, base + 4, 4, sub, lane) for new in news]
        for ref, old, new in zip(refs, olds, news):
            ref[...] = jnp.where(inside, 0.0, ref[...]) - outer(old, new)
            ref[base:base + 8, :] = new


def solve_kernel(fg_ref, fa_ref, t_ref, w_ref, p_ref, g_ref, a_ref, gi_ref, ai_ref):
    act_trace = jnp.sum(t_ref[0:1, :], keepdims=True) / TOKENS
    grad_trace = jnp.sum(t_ref[1:2, :], keepdims=True) / TOKENS
    ratio = jnp.sqrt(act_trace / D / (grad_trace / FF))
    act_damp = ratio * DAMP
    grad_damp = DAMP / ratio
    r = lax.broadcasted_iota(jnp.int32, (128, 128), 0)
    c = lax.broadcasted_iota(jnp.int32, (128, 128), 1)
    last = GB - 256

    def pair(both, second):
        turned = both.T
        first = jnp.where(r >= c, both, turned)
        other = jnp.where(r < c, both, jnp.where(r == c, jnp.broadcast_to(second, (128, 128)), turned))
        return first, other

    def damped(tile, damp):
        return tile / TOKENS + jnp.where(r == c, damp, 0.0)

    zeros = jnp.zeros((128 - last, 128), F32)
    for b in range(2):
        first, second = pair(fg_ref[b, 128:256, :], fg_ref[b, 480:481, :])
        g_ref[b * 6] = damped(first, grad_damp)
        g_ref[b * 6 + 1] = fg_ref[b, 0:128, :] / TOKENS
        g_ref[b * 6 + 2] = damped(second, grad_damp)
        g_ref[b * 6 + 3] = jnp.concatenate([fg_ref[b, 256:344, :] / TOKENS, zeros], axis=0)
        g_ref[b * 6 + 4] = jnp.concatenate([fg_ref[b, 344:432, :] / TOKENS, zeros], axis=0)
        packed = fg_ref[b, 432:480, :]
        low = pltpu.roll(packed[0:40], 88, 1)
        upper = jnp.concatenate([packed, low, jnp.zeros((40, 128), F32)], axis=0)
        corner = jnp.where(jnp.logical_and(r >= 48, c < 48), upper.T, upper)
        inside = jnp.logical_and(r < last, c < last)
        g_ref[b * 6 + 5] = jnp.where(inside, damped(corner, grad_damp), jnp.where(r == c, 1.0, 0.0))
    first, second = pair(fa_ref[128:256, :], t_ref[8:9, :])
    a_ref[0] = damped(first, act_damp)
    a_ref[1] = fa_ref[0:128, :] / TOKENS
    a_ref[2] = damped(second, act_damp)
    gs = [[g_ref.at[b * 6 + t] for t in range(6)] for b in range(2)]
    am = [a_ref.at[t] for t in range(3)]
    sweep_tiles([gs[0][0], gs[1][0], am[0]], 16)
    for m in gs:
        neg = m[0][...]
        a10, a20 = m[1][...], m[3][...]
        v10, v20 = -dot(a10, neg), -dot(a20, neg)
        m[2][...] -= dot(v10, a10, 1, 1)
        m[4][...] -= dot(v20, a10, 1, 1)
        m[5][...] -= dot(v20, a20, 1, 1)
        m[1][...] = v10
        m[3][...] = v20
    a10 = am[1][...]
    v10 = -dot(a10, am[0][...])
    am[2][...] -= dot(v10, a10, 1, 1)
    am[1][...] = v10
    sweep_tiles([gs[0][2], gs[1][2], am[2]], 16)
    for m in gs:
        neg = m[2][...]
        a10, a21 = m[1][...], m[4][...]
        v10, v21 = -dot(neg, a10), -dot(a21, neg)
        m[0][...] -= dot(a10, v10, 0, 0)
        m[3][...] -= dot(a21, v10)
        m[5][...] -= dot(v21, a21, 1, 1)
        m[1][...] = v10
        m[4][...] = v21
    a10 = am[1][...]
    v10 = -dot(am[2][...], a10)
    am[0][...] -= dot(a10, v10, 0, 0)
    am[1][...] = v10
    sweep_tiles([gs[0][5], gs[1][5]], last // 8)
    for m in gs:
        neg = m[5][...]
        a20, a21 = m[3][...], m[4][...]
        v20, v21 = -dot(neg, a20), -dot(neg, a21)
        m[0][...] -= dot(a20, v20, 0, 0)
        m[1][...] -= dot(a21, v20, 0, 0)
        m[2][...] -= dot(a21, v21, 0, 0)
        m[3][...] = v20
        m[4][...] = v21
    ai_ref[0:128, 0:128] = -am[0][...]
    ai_ref[128:256, 0:128] = -am[1][...]
    ai_ref[0:128, 128:256] = -am[1][...].T
    ai_ref[128:256, 128:256] = -am[2][...]
    for b, m in enumerate(gs):
        for t, (i, j) in enumerate(((0, 0), (1, 0), (1, 1), (2, 0), (2, 1), (2, 2))):
            tile = -m[t][...]
            gi_ref[b, i * 128:(i + 1) * 128, j * 128:(j + 1) * 128] = tile
            if i != j:
                gi_ref[b, j * 128:(j + 1) * 128, i * 128:(i + 1) * 128] = tile.T
    for b in range(2):
        w = w_ref[...].astype(F32)[b * GB:(b + 1) * GB]
        w = jnp.concatenate([w, jnp.zeros((384 - GB, 256), F32)], axis=0)
        left = dot(ai_ref[...], w, 1, 1)
        p_ref[:, b * 384:(b + 1) * 384] = dot(left, gi_ref[b]).astype(jnp.bfloat16)


def solve(fg, fa, tr, w):
    vmem = pl.BlockSpec(memory_space=pltpu.VMEM)
    return pl.pallas_call(
        solve_kernel,
        out_shape=jax.ShapeDtypeStruct((256, 768), jnp.bfloat16),
        in_specs=[vmem] * 4,
        out_specs=vmem,
        scratch_shapes=[pltpu.VMEM((12, 128, 128), F32), pltpu.VMEM((3, 128, 128), F32),
                        pltpu.VMEM((2, 384, 384), F32), pltpu.VMEM((256, 256), F32)],
        compiler_params=pltpu.CompilerParams(vmem_limit_bytes=VLIM),
        name="solve",
    )(fg, fa, tr, w)


def gather_kernel(p_ref, o_ref, local, sz, rz, sy, ry, sh, rh, sc, rc):
    dp, own = place()
    core = lax.rem(dp, 2)
    y = dp // 4
    sib = dp + 1 - 2 * core
    zh = lax.rem(dp // 2, 2)
    anti = dp + 2 - 4 * zh
    up = lax.rem(y + 1, 4) * 4 + lax.rem(dp, 4)
    down = lax.rem(y + 3, 4) * 4 + lax.rem(dp, 4)
    barrier = pltpu.get_barrier_semaphore()
    for device in (sib, anti, up, down):
        pl.semaphore_signal(barrier, inc=1, device_id=(device, own), device_id_type=MESH)
    pl.semaphore_wait(barrier, 4)

    def other(d):
        return d + 2 - 4 * lax.rem(d // 2, 2)

    far = lax.rem(y + 2, 4) * 4 + lax.rem(dp, 4)
    waits = []

    def half(ref, h):
        return ref.at[pl.ds(h * 128, 128)]

    def send(d, h, sems, i, device, src=None):
        src = o_ref.at[d] if src is None else src
        copy = pltpu.make_async_remote_copy(
            src_ref=half(src, h), dst_ref=half(o_ref.at[d], h), send_sem=sems[0].at[i], recv_sem=sems[1].at[i],
            device_id=(device, own), device_id_type=MESH)
        copy.start()
        waits.append(copy)

    def arrived(d, h, sems, i):
        dst = half(o_ref.at[d], h)
        pltpu.make_async_remote_copy(src_ref=dst, dst_ref=dst, send_sem=sems[0].at[i], recv_sem=sems[1].at[i],
                                     device_id=(sib, own), device_id_type=MESH).wait_recv()

    zsem, ysem, hsem, csem = (sz, rz), (sy, ry), (sh, rh), (sc, rc)
    for h in range(2):
        send(dp, h, zsem, h, anti, p_ref)
        send(dp, h, ysem, h, up, p_ref)
        send(dp, 1 - h, ysem, 3 - h, down, p_ref)
    for h in range(2):
        send(dp, h, csem, h, sib, p_ref)
    keep = pltpu.make_async_copy(p_ref, o_ref.at[dp], local)
    keep.start()
    arrived(down, 0, ysem, 0)
    send(down, 0, hsem, 0, up)
    arrived(up, 1, ysem, 3)
    send(up, 1, hsem, 1, down)
    send(down, 0, csem, 2, sib)
    send(up, 1, csem, 5, sib)
    arrived(down, 1, ysem, 1)
    send(down, 1, csem, 3, sib)
    arrived(up, 0, ysem, 2)
    send(up, 0, csem, 4, sib)
    arrived(anti, 0, zsem, 0)
    send(anti, 0, ysem, 4, up)
    send(anti, 0, ysem, 6, down)
    send(anti, 0, csem, 6, sib)
    arrived(far, 0, hsem, 0)
    send(far, 0, csem, 8, sib)
    arrived(far, 1, hsem, 1)
    send(far, 1, csem, 9, sib)
    arrived(anti, 1, zsem, 1)
    send(anti, 1, ysem, 5, up)
    send(anti, 1, ysem, 7, down)
    send(anti, 1, csem, 7, sib)
    arrived(other(down), 0, ysem, 4)
    send(other(down), 0, hsem, 2, up)
    send(other(down), 0, csem, 10, sib)
    arrived(other(up), 0, ysem, 6)
    send(other(up), 0, csem, 12, sib)
    arrived(other(up), 1, ysem, 7)
    send(other(up), 1, hsem, 3, down)
    send(other(up), 1, csem, 13, sib)
    arrived(other(down), 1, ysem, 5)
    send(other(down), 1, csem, 11, sib)
    arrived(other(far), 0, hsem, 2)
    send(other(far), 0, csem, 14, sib)
    arrived(other(far), 1, hsem, 3)
    send(other(far), 1, csem, 15, sib)

    def twin(d):
        return d + 1 - 2 * lax.rem(d, 2)

    for i, d in enumerate((dp, down, up, anti, far, other(down), other(up), other(far))):
        for h in range(2):
            arrived(twin(d), h, csem, 2 * i + h)
    keep.wait()
    for copy in waits:
        copy.wait_send()


def gather(p):
    dma = pltpu.SemaphoreType.DMA
    return pl.pallas_call(
        gather_kernel,
        out_shape=jax.ShapeDtypeStruct((16, 256, 768), jnp.bfloat16),
        in_specs=[pl.BlockSpec(memory_space=pl.ANY)],
        out_specs=pl.BlockSpec(memory_space=pl.ANY),
        scratch_shapes=[dma, dma((2,)), dma((2,)), dma((8,)), dma((8,)), dma((4,)), dma((4,)), dma((16,)), dma((16,))],
        compiler_params=pltpu.CompilerParams(collective_id=2, has_side_effects=True),
        name="gather",
    )(p)


def flat_kernel(i_ref, o_ref):
    for d in range(16):
        for b in range(2):
            start = (2 * d + b) * GB
            o_ref[:, start:start + GB] = i_ref[d, :, b * 384:b * 384 + GB]


def flatten(slices):
    rows = 64
    return pl.pallas_call(
        flat_kernel,
        out_shape=jax.ShapeDtypeStruct((256, FF), jnp.bfloat16),
        grid=(256 // rows,),
        in_specs=[pl.BlockSpec((16, rows, 768), lambda i: (0, i, 0))],
        out_specs=pl.BlockSpec((rows, FF), lambda i: (i, 0)),
        compiler_params=pltpu.CompilerParams(vmem_limit_bytes=VLIM),
        name="flatten",
    )(slices)


def shards(acts, grads_out, weight_grad):
    sib_acts, sib_grads = swap(acts, grads_out)
    gx, gy, tr = grams(acts, grads_out, sib_acts, sib_grads)
    fg, fa, tr = reduce_all(gx, gy, tr)
    p = solve(fg.reshape(2, 512, 128), fa.reshape(256, 128), tr, weight_grad.T)
    return flatten(gather(p))


def solution(mesh):
    in_specs = (P(("dp", "owner"), None), P(("dp", "owner"), None), P("owner", "dp"))
    out_specs = P("owner", None)
    return jax.shard_map(shards, mesh=mesh, in_specs=in_specs, out_specs=out_specs, check_vma=False)
```

```python
import functools
import math

import jax
import jax.numpy as jnp
from jax import lax
from jax.experimental import pallas as pl
from jax.experimental.pallas import tpu as pltpu
from jax.sharding import PartitionSpec as P

D = 4096
FF = 11008
AB = 256
GB = 344
TOKENS = 57344
DAMP = math.sqrt(0.03)
MESH = pl.DeviceIdType.MESH
HIGH = lax.Precision.HIGHEST
F32 = jnp.float32
NB = 2
GROWS = 64 // NB
AROWS = 16 // NB
CH = GROWS + AROWS
HALF = 4 * CH
VLIM = 56 * 1024 * 1024
WIN = 7 * 128
WIDTHS = [WIN] * 7 + [WIN - 128]
CUT = (352, 336)


def grad_position(p, part):
    y = p // 2
    return 2 * part + (p + y) % 2, y


def act_position(k, part):
    return k % 4, 2 * part + k // 4


def window(d):
    return 128 * (43 * d // 8)


def place():
    dp = lax.axis_index("dp")
    own = lax.axis_index("owner")
    return dp, own


def swap_kernel(a_ref, g_ref, ao_ref, go_ref, send, recv):
    dp, own = place()
    core = lax.rem(dp, 2)
    sib = dp + 1 - 2 * core
    barrier = pltpu.get_barrier_semaphore()
    pl.semaphore_signal(barrier, inc=1, device_id=(sib, own), device_id_type=MESH)
    pl.semaphore_wait(barrier, 1)
    width = ao_ref.shape[1]
    pieces = [(a_ref.at[:, pl.ds(pl.multiple_of((1 - core) * width, 128), width)], ao_ref)]
    for p in range(8):
        start = pl.multiple_of(window(2 * p + 1 - core), 128)
        pieces.append((g_ref.at[:, pl.ds(start, WIDTHS[p])], go_ref.at[:, pl.ds(p * WIN, WIDTHS[p])]))
    copies = []
    for i, (src, dst) in enumerate(pieces):
        copy = pltpu.make_async_remote_copy(
            src_ref=src, dst_ref=dst, send_sem=send.at[i], recv_sem=recv.at[i],
            device_id=(sib, own), device_id_type=MESH)
        copy.start()
        copies.append(copy)
    for copy in copies:
        copy.wait()


def swap(acts, grads):
    rows = acts.shape[0]
    return pl.pallas_call(
        swap_kernel,
        out_shape=(jax.ShapeDtypeStruct((rows, D // 2), acts.dtype),
                   jax.ShapeDtypeStruct((rows, 8 * WIN), acts.dtype)),
        in_specs=[pl.BlockSpec(memory_space=pl.ANY)] * 2,
        out_specs=(pl.BlockSpec(memory_space=pl.ANY),) * 2,
        scratch_shapes=[pltpu.SemaphoreType.DMA((9,))] * 2,
        compiler_params=pltpu.CompilerParams(collective_id=0, has_side_effects=True),
        name="swap",
    )(acts, grads)


def gram(block):
    return lax.dot_general(block, block, (((0,), (0,)), ((), ())), preferred_element_type=F32)


def gram_kernel(a_ref, g_ref, as_ref, gs_ref, x_out, y_out, t_ref, abuf, gbuf, even, x_ref, y_ref, sems, out_sems):
    core = lax.rem(lax.axis_index("dp"), 2)
    rows = a_ref.shape[0]
    mine, theirs = pl.ds(0, rows), pl.ds(rows, rows)
    width = abuf.shape[1]
    moves = [[(a_ref.at[:, pl.ds(pl.multiple_of(core * width, 128), width)], abuf.at[mine]), (as_ref, abuf.at[theirs])]]
    for lo in (0, 4):
        group = []
        for p in range(lo, lo + 4):
            start = pl.multiple_of(window(2 * p + core), 128)
            group.append((g_ref.at[:, pl.ds(start, WIDTHS[p])], gbuf.at[mine, pl.ds(p * WIN, WIDTHS[p])]))
        span = pl.ds(lo * WIN, 4 * WIN - WIN + WIDTHS[lo + 3])
        group.append((gs_ref.at[:, span], gbuf.at[theirs, span]))
        moves.append(group)
    copies = []
    for i, group in enumerate(moves):
        copies.append([pltpu.make_async_copy(src, dst, sems.at[i, n]) for n, (src, dst) in enumerate(group)])
        for copy in copies[i]:
            copy.start()

    def store_all(where, size, lead, row, value):
        px, py = where
        done = 0
        while done < value.shape[0]:
            at = row + done
            n = min(size - at % size, value.shape[0] - done)
            batch, chunk = at // size // 8, at // size % 8
            rows_at = pl.ds(chunk % 4 * CH + lead + at % size, n)
            if chunk < 4:
                x_ref[batch, px * 4 + py, rows_at, :] = value[done:done + n]
            else:
                y_ref[batch, py * 4 + px, rows_at, :] = value[done:done + n]
            done += n

    outs = []

    def finish(where):
        px, py = where
        for i, (src, dst, at) in enumerate(((x_ref, x_out, px * 4 + py), (y_ref, y_out, py * 4 + px))):
            copy = pltpu.make_async_copy(src.at[:, at], dst.at[:, at], out_sems.at[i, px * 4 + py])
            copy.start()
            outs.append(copy)

    r = lax.broadcasted_iota(jnp.int32, (128, 128), 0)
    c = lax.broadcasted_iota(jnp.int32, (128, 128), 1)

    def diag(tile):
        return jnp.sum(jnp.where(r == c, tile, 0.0), axis=0, keepdims=True)

    act_sum = jnp.zeros((1, 128), F32)
    grad_sum = jnp.zeros((1, 128), F32)
    for copy in copies[0]:
        copy.wait()
    for k in range(8):
        g = gram(abuf[:, k * AB:(k + 1) * AB])
        t0, t2 = g[0:128, 0:128], g[128:256, 128:256]
        second = diag(t2)
        act_sum += diag(t0) + second
        t_ref[8 + k:9 + k, :] = second
        store_all(act_position(k, 0), AROWS, GROWS, 0, g[128:256, 0:128])
        store_all(act_position(k, 1), AROWS, GROWS, 0, jnp.where(r >= c, t0, t2))
    for j in range(16):
        if j in (0, 8):
            for copy in copies[1 + j // 8]:
                copy.wait()
            for odd in range(2):
                @pl.when(core == odd)
                def _():
                    for i in range(j, j + 8):
                        d = i // 2 * 2 + odd
                        start = i // 2 * WIN + 2 * GB * d - window(d) + i % 2 * GB
                        even[i, :, 0:GB] = gbuf[:, start:start + GB]
        block = even[j, :, 0:GB]
        g = lax.dot_general(block, block[:, 0:256], (((0,), (0,)), ((), ())), preferred_element_type=F32)
        t0, t2 = g[0:128, 0:128], g[128:256, 128:256]
        t5 = jnp.concatenate([gram(block[:, 256:GB]), jnp.zeros((88, 40), F32)], axis=1)
        second = diag(t2)
        grad_sum += diag(t0) + second + jnp.sum(jnp.where(r[:88] == c[:88], t5, 0.0), axis=0, keepdims=True)
        tail = jnp.concatenate([pltpu.roll(t5[48:88], 40, 1), jnp.zeros((8, 128), F32)], axis=0)
        where = grad_position(j // 2, j % 2)
        store_all(where, GROWS, 0, 0, g[128:256, 0:128])
        store_all(where, GROWS, 0, 128, jnp.where(r >= c, t0, t2))
        store_all(where, GROWS, 0, 256, g[256:344, 0:128])
        store_all(where, GROWS, 0, 344, g[256:344, 128:256])
        store_all(where, GROWS, 0, 432, jnp.where(c[:48] < 88, t5[0:48], tail))
        store_all(where, GROWS, 0, 480, jnp.concatenate([second, jnp.zeros((31, 128), F32)], axis=0))
        finish(where)
    t_ref[0:8, :] = jnp.concatenate([act_sum, grad_sum, jnp.zeros((6, 128), F32)], axis=0)
    for copy in outs:
        copy.wait()


def grams(acts, grads, sib_acts, sib_grads):
    shape = jax.ShapeDtypeStruct((NB, 16, HALF, 128), F32)
    vmem = pl.BlockSpec(memory_space=pltpu.VMEM)
    anywhere = pl.BlockSpec(memory_space=pl.ANY)
    rows = acts.shape[0]
    return pl.pallas_call(
        gram_kernel,
        out_shape=(shape, shape, jax.ShapeDtypeStruct((16, 128), F32)),
        in_specs=[anywhere] * 4,
        out_specs=(anywhere, anywhere, vmem),
        scratch_shapes=[pltpu.VMEM((2 * rows, D // 2), acts.dtype), pltpu.VMEM((2 * rows, 8 * WIN), acts.dtype),
                        pltpu.VMEM((16, 2 * rows, 384), acts.dtype),
                        pltpu.VMEM(shape.shape, F32), pltpu.VMEM(shape.shape, F32),
                        pltpu.SemaphoreType.DMA((3, 5)), pltpu.SemaphoreType.DMA((2, 16))],
        compiler_params=pltpu.CompilerParams(vmem_limit_bytes=VLIM),
        name="grams",
    )(acts, grads, sib_acts, sib_grads)


def reduce_kernel(gx, gy, tr, fg, fa, t_out,
                  ps, pk, pm, pr, rx2, ry2, st, rz, fin, ga, aa, t1, t2, t3, q1, q2, q3, q4, tt,
                  local, s1, r1, s2, r2, s3, r3, s4, rg4, ra4, s5, rg5, ra5, ts, tr_sem):
    dp, own = place()
    core = lax.rem(dp, 2)
    zh = lax.rem(dp // 2, 2)
    y = dp // 4
    x = lax.rem(own, 4)
    zl = own // 4
    z = zh * 4 + zl
    sib = dp + 1 - 2 * core

    def at(ax, ay, az, ac):
        return ((ay * 2 + az // 4) * 2 + ac, lax.rem(az, 4) * 4 + ax)

    xs = [at(lax.rem(x + k, 4), y, z, core) for k in (1, 2, 3)]
    ys = [at(x, lax.rem(y + k, 4), z, core) for k in (1, 2, 3)]
    zs = [at(x, y, lax.rem(z + k, 8), core) for k in range(1, 8)]
    g_part, a_part = x // 2, y // 2
    unit_zh = lax.rem(x + y, 2)
    unit_zl = 2 * core + lax.rem(y, 2)
    g_on = zh == unit_zh
    a_on = zl == unit_zl
    across = [at(x, lax.rem(y + k, 4), z, 1 - core) for k in range(4)]

    barrier = pltpu.get_barrier_semaphore()
    for device in xs + ys + zs + across:
        pl.semaphore_signal(barrier, inc=1, device_id=device, device_id_type=MESH)
    pl.semaphore_wait(barrier, 17)

    def remote(src, dst, ssem, rsem, device):
        return pltpu.make_async_remote_copy(src_ref=src, dst_ref=dst, send_sem=ssem, recv_sem=rsem,
                                            device_id=device, device_id_type=MESH)

    def begin(copies):
        for copy in copies:
            copy.start()
        return copies

    def end(copies):
        for copy in copies:
            copy.wait()

    axes = ((0, gx, x, (xs[0], xs[2])), (1, gy, y, (ys[0], ys[2])))

    def plane(b):
        copies = []
        for a, g, me, (up, down) in axes:
            over, under, opposite = lax.rem(me + 1, 4) * 4, lax.rem(me + 3, 4) * 4, lax.rem(me + 2, 4) * 4
            copies.append(remote(g.at[b, pl.ds(opposite, 2)], pm.at[a, b, 0], s1.at[a, b, 0], r1.at[a, b, 0], up))
            copies.append(remote(g.at[b, pl.ds(opposite + 2, 2)], pm.at[a, b, 1],
                                 s1.at[a, b, 1], r1.at[a, b, 1], down))
            copies.append(pltpu.make_async_copy(g.at[b, pl.ds(over, 2)], pk.at[a, b, 0], local.at[a, b, 0]))
            copies.append(pltpu.make_async_copy(g.at[b, pl.ds(under + 2, 2)], pk.at[a, b, 1], local.at[a, b, 1]))
        for a, g, me, (up, down) in axes:
            over, under = lax.rem(me + 1, 4) * 4, lax.rem(me + 3, 4) * 4
            copies.append(remote(g.at[b, pl.ds(over + 2, 2)], pr.at[a, b, 0, pl.ds(2, 2)],
                                 s1.at[a, b, 2], r1.at[a, b, 2], up))
            copies.append(remote(g.at[b, pl.ds(under, 2)], pr.at[a, b, 1, pl.ds(0, 2)],
                                 s1.at[a, b, 3], r1.at[a, b, 3], down))
            copies.append(pltpu.make_async_copy(g.at[b, pl.ds(me * 4, 4)], ps.at[a, b], local.at[a, b, 2]))
        return begin(copies)

    def plane_pass(b, copies):
        end(copies[:8])
        @pl.loop(0, 8)
        def _(i):
            h, rows = i // 4, pl.ds(pl.multiple_of(lax.rem(i, 4) * CH, 8), CH)
            for a in range(2):
                for d in range(2):
                    pk[a, b, d, h, rows, :] += pm[a, b, d, h, rows, :]
        for a, _, _, to in axes:
            for d in range(2):
                copies.append(remote(pk.at[a, b, d], pr.at[a, b, d, pl.ds(2 * d, 2)],
                                     s1.at[a, b, 4 + d], r1.at[a, b, 4 + d], to[d]))
                copies[-1].start()

    def plane_sum(b, copies):
        end(copies[8:])
        @pl.loop(0, 16)
        def _(i):
            q, rows = i // 4, pl.ds(pl.multiple_of(lax.rem(i, 4) * CH, 8), CH)
            for a in range(2):
                ps[a, b, q, rows, :] += pr[a, b, 0, q, rows, :] + pr[a, b, 1, q, rows, :]

    def cross(b):
        copies = []
        for k in range(3):
            copies.append(remote(ps.at[0, b, lax.rem(y + k + 1, 4)], rx2.at[b, k], s2.at[b, k], r2.at[b, k], ys[k]))
            copies.append(remote(ps.at[1, b, lax.rem(x + k + 1, 4)], ry2.at[b, k],
                                 s2.at[b, 3 + k], r2.at[b, 3 + k], xs[k]))
        return begin(copies)

    def cross_sum(b):
        @pl.loop(0, 4)
        def _(i):
            rows = pl.ds(pl.multiple_of(i * CH, 8), CH)
            st[b, i] = (ps[0, b, y, rows, :] + rx2[b, 0, rows, :]) + (rx2[b, 1, rows, :] + rx2[b, 2, rows, :])
            st[b, 4 + i] = (ps[1, b, x, rows, :] + ry2[b, 0, rows, :]) + (ry2[b, 1, rows, :] + ry2[b, 2, rows, :])

    def along(b):
        return begin([remote(st.at[b, lax.rem(z + k + 1, 8)], rz.at[b, k], s3.at[b, k], r3.at[b, k], zs[k])
                      for k in range(7)])

    def along_sum(b):
        total = st[b, z]
        for k in range(7):
            total += rz[b, k]
        fin[b] = total

    def spread(b):
        for i in range(6):
            if i < 4:
                to = unit_zh * 4 + i
                src, dst, rsem = fin.at[b, pl.ds(0, GROWS)], ga.at[b, z], rg4.at[b, z]
            else:
                to = (i - 4) * 4 + unit_zl
                src, dst, rsem = fin.at[b, pl.ds(GROWS, AROWS)], aa.at[b, z], ra4.at[b, z]

            @pl.when(to == z)
            def _():
                pltpu.make_async_copy(src, dst, rsem).start()

            @pl.when(to != z)
            def _():
                remote(src, dst, s4.at[b, i], rsem, at(x, y, to, core)).start()

    def spread_sent(b):
        for i in range(6):
            to = unit_zh * 4 + i if i < 4 else (i - 4) * 4 + unit_zl
            src = fin.at[b, pl.ds(0, GROWS)] if i < 4 else fin.at[b, pl.ds(GROWS, AROWS)]
            dst, rsem = (ga.at[b, z], rg4.at[b, z]) if i < 4 else (aa.at[b, z], ra4.at[b, z])

            @pl.when(to != z)
            def _():
                remote(src, dst, s4.at[b, i], rsem, at(x, y, to, core)).wait_send()

    def parts(b):
        return ((g_on, ga.at[b], xs, fg.at[g_part, b], rg5.at[b, g_part], 0),
                (a_on, aa.at[b], ys + across, fa.at[a_part, b], ra5.at[b, a_part], 3))

    def give(b):
        for on, src, to, dst, rsem, first in parts(b):
            @pl.when(on)
            def _():
                for i in range(8):
                    piece = fin.at[b, pl.ds(0, GROWS)] if first == 0 else fin.at[b, pl.ds(GROWS, AROWS)]
                    arrive = (rg4 if first == 0 else ra4).at[b, i]
                    pltpu.make_async_copy(piece, src.at[i], arrive).wait()
                for i, device in enumerate(to):
                    remote(src, dst, s5.at[b, first + i], rsem, device).start()
                pltpu.make_async_copy(src, dst, rsem).start()

    def given(b):
        for on, src, to, dst, rsem, first in parts(b):
            @pl.when(on)
            def _():
                for i, device in enumerate(to):
                    remote(src, dst, s5.at[b, first + i], rsem, device).wait_send()

    def taken(b):
        for i in range(2):
            pltpu.make_async_copy(ga.at[b], fg.at[i, b], rg5.at[b, i]).wait()
            pltpu.make_async_copy(aa.at[b], fa.at[i, b], ra5.at[b, i]).wait()

    batches = range(NB)
    q = begin([remote(tr, q1.at[k], ts.at[k], tr_sem.at[k], xs[k]) for k in range(3)])
    second, third = [], []
    first = [plane(0)]
    plane_pass(0, first[0])
    for b in batches:
        if b + 1 < NB:
            first.append(plane(b + 1))
        plane_sum(b, first[b])
        second.append(cross(b))
        if b + 1 < NB:
            plane_pass(b + 1, first[b + 1])
    end(q)
    t1[...] = (tr[...] + q1[0]) + (q1[1] + q1[2])
    q = begin([remote(t1, q2.at[k], ts.at[3 + k], tr_sem.at[3 + k], ys[k]) for k in range(3)])
    for b in batches:
        end(second[b])
        cross_sum(b)
        third.append(along(b))
    end(q)
    t2[...] = (t1[...] + q2[0]) + (q2[1] + q2[2])
    q = begin([remote(t2, q3.at[k], ts.at[6 + k], tr_sem.at[6 + k], zs[k]) for k in range(7)])
    for b in batches:
        end(third[b])
        along_sum(b)
        spread(b)
    end(q)
    trace = t2[...]
    for k in range(7):
        trace += q3[k]
    t3[...] = trace
    q = begin([remote(t3, q4, ts.at[13], tr_sem.at[13], (sib, own))])
    for b in batches:
        give(b)
    end(q)
    tt[core] = t3[...]
    tt[1 - core] = q4[...]
    t_out[0:8, :] = tt[0, 0:8, :] + tt[1, 0:8, :]
    t_out[8:16, :] = jnp.broadcast_to(tt[own // 8, pl.ds(8 + lax.rem(own, 8), 1), :], (8, 128))
    for b in batches:
        taken(b)
    for b in batches:
        spread_sent(b)
        given(b)


def reduce_all(gx, gy, tr):
    vmem = pl.BlockSpec(memory_space=pltpu.VMEM)
    dma = pltpu.SemaphoreType.DMA
    tile = pltpu.VMEM((16, 128), F32)

    def buf(*shape):
        return pltpu.VMEM(shape + (128,), F32)

    return pl.pallas_call(
        reduce_kernel,
        out_shape=(jax.ShapeDtypeStruct((2, NB, 8, GROWS, 128), F32),
                   jax.ShapeDtypeStruct((2, NB, 8, AROWS, 128), F32),
                   jax.ShapeDtypeStruct((16, 128), F32)),
        in_specs=[pl.BlockSpec(memory_space=pl.ANY)] * 2 + [vmem],
        out_specs=(vmem,) * 3,
        scratch_shapes=[
            buf(2, NB, 4, HALF), buf(2, NB, 2, 2, HALF), buf(2, NB, 2, 2, HALF), buf(2, NB, 2, 4, HALF),
            buf(NB, 3, HALF), buf(NB, 3, HALF), buf(NB, 8, CH), buf(NB, 7, CH), buf(NB, CH),
            buf(NB, 8, GROWS), buf(NB, 8, AROWS),
            tile, tile, tile, buf(3, 16), buf(3, 16), buf(7, 16), tile, buf(2, 16),
            dma((2, NB, 3)), dma((2, NB, 6)), dma((2, NB, 6)), dma((NB, 6)), dma((NB, 6)), dma((NB, 7)), dma((NB, 7)),
            dma((NB, 6)), dma((NB, 8)), dma((NB, 8)), dma((NB, 10)), dma((NB, 2)), dma((NB, 2)), dma((14,)), dma((14,)),
        ],
        compiler_params=pltpu.CompilerParams(collective_id=1, has_side_effects=True, vmem_limit_bytes=VLIM),
        name="reduce_all",
    )(gx, gy, tr)


def dot(a, b, ca=1, cb=0):
    return lax.dot_general(a, b, (((ca,), (cb,)), ((), ())), precision=HIGH, preferred_element_type=F32)


def split(v):
    high = v.astype(jnp.bfloat16).astype(F32)
    rest = v - high
    mid = rest.astype(jnp.bfloat16).astype(F32)
    return high, mid, rest - mid


def outer(a, b):
    ah, am, al = split(a)
    bh, bm, bl = split(b)
    left = jnp.concatenate([ah, ah, am, ah, am, al], axis=0).astype(jnp.bfloat16)
    right = jnp.concatenate([bh, bm, bh, bl, bm, bh], axis=0).astype(jnp.bfloat16)
    return lax.dot_general(left, right, (((0,), (0,)), ((), ())), preferred_element_type=F32)


def sweep_four(now, at, row, sub, lane):
    def full(v):
        return jnp.broadcast_to(v, (8, 128))

    four = range(4)
    cols = [full(now[:, at + i:at + i + 1]) for i in four]
    rows = [full(now[row + i:row + i + 1, :]) for i in four]
    m = {(i, j): full(cols[j][row + i:row + i + 1, :]) for i in four for j in range(i + 1)}
    for p in four:
        inv = 1.0 / m[(p, p)]
        line = {i: m[(max(i, p), min(i, p))] * inv for i in four if i != p}
        new = {}
        for i in four:
            for j in range(i + 1):
                if i == p and j == p:
                    new[(i, j)] = -inv
                elif i == p:
                    new[(i, j)] = line[j]
                elif j == p:
                    new[(i, j)] = line[i]
                else:
                    new[(i, j)] = m[(i, j)] - m[(max(i, p), min(i, p))] * line[j]
        m = new
    in_rows = jnp.logical_and(sub >= row, sub < row + 4)
    in_cols = jnp.logical_and(lane >= at, lane < at + 4)
    out = jnp.where(jnp.logical_or(in_rows, in_cols), 0.0, now)
    rows = [jnp.where(in_cols, jnp.where(lane == at + i, -1.0, 0.0), rows[i]) for i in four]
    for i in four:
        col = jnp.where(in_rows, jnp.where(sub == row + i, -1.0, 0.0), cols[i])
        term = m[(i, 0)] * rows[0]
        for j in range(1, 4):
            term = term + m[(max(i, j), min(i, j))] * rows[j]
        out = out + col * term
    return out


def sweep_tiles(refs, panels):
    sub = lax.broadcasted_iota(jnp.int32, (8, 128), 0)
    lane = lax.broadcasted_iota(jnp.int32, (8, 128), 1)
    lane_all = lax.broadcasted_iota(jnp.int32, (128, 128), 1)
    for p in range(panels):
        base = 8 * p
        inside = jnp.logical_and(lane_all >= base, lane_all < base + 8)
        olds = [ref[base:base + 8, :] for ref in refs]
        news = [sweep_four(old, base, 0, sub, lane) for old in olds]
        news = [sweep_four(new, base + 4, 4, sub, lane) for new in news]
        for ref, old, new in zip(refs, olds, news):
            ref[...] = jnp.where(inside, 0.0, ref[...]) - outer(old, new)
            ref[base:base + 8, :] = new


def solve_kernel(fg_ref, fa_ref, t_ref, w_ref, p_ref, g_ref, a_ref, gi_ref, ai_ref):
    act_trace = jnp.sum(t_ref[0:1, :], keepdims=True) / TOKENS
    grad_trace = jnp.sum(t_ref[1:2, :], keepdims=True) / TOKENS
    ratio = jnp.sqrt(act_trace / D / (grad_trace / FF))
    act_damp = ratio * DAMP
    grad_damp = DAMP / ratio
    r = lax.broadcasted_iota(jnp.int32, (128, 128), 0)
    c = lax.broadcasted_iota(jnp.int32, (128, 128), 1)
    last = GB - 256

    def pair(both, second):
        turned = both.T
        first = jnp.where(r >= c, both, turned)
        other = jnp.where(r < c, both, jnp.where(r == c, jnp.broadcast_to(second, (128, 128)), turned))
        return first, other

    def damped(tile, damp):
        return tile / TOKENS + jnp.where(r == c, damp, 0.0)

    zeros = jnp.zeros((128 - last, 128), F32)
    for b in range(2):
        first, second = pair(fg_ref[b, 128:256, :], fg_ref[b, 480:481, :])
        g_ref[b * 6] = damped(first, grad_damp)
        g_ref[b * 6 + 1] = fg_ref[b, 0:128, :] / TOKENS
        g_ref[b * 6 + 2] = damped(second, grad_damp)
        g_ref[b * 6 + 3] = jnp.concatenate([fg_ref[b, 256:344, :] / TOKENS, zeros], axis=0)
        g_ref[b * 6 + 4] = jnp.concatenate([fg_ref[b, 344:432, :] / TOKENS, zeros], axis=0)
        packed = fg_ref[b, 432:480, :]
        low = pltpu.roll(packed[0:40], 88, 1)
        upper = jnp.concatenate([packed, low, jnp.zeros((40, 128), F32)], axis=0)
        corner = jnp.where(jnp.logical_and(r >= 48, c < 48), upper.T, upper)
        inside = jnp.logical_and(r < last, c < last)
        g_ref[b * 6 + 5] = jnp.where(inside, damped(corner, grad_damp), jnp.where(r == c, 1.0, 0.0))
    first, second = pair(fa_ref[128:256, :], t_ref[8:9, :])
    a_ref[0] = damped(first, act_damp)
    a_ref[1] = fa_ref[0:128, :] / TOKENS
    a_ref[2] = damped(second, act_damp)
    gs = [[g_ref.at[b * 6 + t] for t in range(6)] for b in range(2)]
    am = [a_ref.at[t] for t in range(3)]
    sweep_tiles([gs[0][0], gs[1][0], am[0]], 16)
    for m in gs:
        neg = m[0][...]
        a10, a20 = m[1][...], m[3][...]
        v10, v20 = -dot(a10, neg), -dot(a20, neg)
        m[2][...] -= dot(v10, a10, 1, 1)
        m[4][...] -= dot(v20, a10, 1, 1)
        m[5][...] -= dot(v20, a20, 1, 1)
        m[1][...] = v10
        m[3][...] = v20
    a10 = am[1][...]
    v10 = -dot(a10, am[0][...])
    am[2][...] -= dot(v10, a10, 1, 1)
    am[1][...] = v10
    sweep_tiles([gs[0][2], gs[1][2], am[2]], 16)
    for m in gs:
        neg = m[2][...]
        a10, a21 = m[1][...], m[4][...]
        v10, v21 = -dot(neg, a10), -dot(a21, neg)
        m[0][...] -= dot(a10, v10, 0, 0)
        m[3][...] -= dot(a21, v10)
        m[5][...] -= dot(v21, a21, 1, 1)
        m[1][...] = v10
        m[4][...] = v21
    a10 = am[1][...]
    v10 = -dot(am[2][...], a10)
    am[0][...] -= dot(a10, v10, 0, 0)
    am[1][...] = v10
    sweep_tiles([gs[0][5], gs[1][5]], last // 8)
    for m in gs:
        neg = m[5][...]
        a20, a21 = m[3][...], m[4][...]
        v20, v21 = -dot(neg, a20), -dot(neg, a21)
        m[0][...] -= dot(a20, v20, 0, 0)
        m[1][...] -= dot(a21, v20, 0, 0)
        m[2][...] -= dot(a21, v21, 0, 0)
        m[3][...] = v20
        m[4][...] = v21
    ai_ref[0:128, 0:128] = -am[0][...]
    ai_ref[128:256, 0:128] = -am[1][...]
    ai_ref[0:128, 128:256] = -am[1][...].T
    ai_ref[128:256, 128:256] = -am[2][...]
    for b, m in enumerate(gs):
        for t, (i, j) in enumerate(((0, 0), (1, 0), (1, 1), (2, 0), (2, 1), (2, 2))):
            tile = -m[t][...]
            gi_ref[b, i * 128:(i + 1) * 128, j * 128:(j + 1) * 128] = tile
            if i != j:
                gi_ref[b, j * 128:(j + 1) * 128, i * 128:(i + 1) * 128] = tile.T
    out = []
    for b in range(2):
        w = w_ref[...].astype(F32)[b * GB:(b + 1) * GB]
        w = jnp.concatenate([w, jnp.zeros((384 - GB, 256), F32)], axis=0)
        out.append(dot(gi_ref[b], dot(w, ai_ref[...]))[0:GB])
    p_ref[...] = jnp.concatenate(out, axis=0).astype(jnp.bfloat16)


def solve(fg, fa, tr, w):
    vmem = pl.BlockSpec(memory_space=pltpu.VMEM)
    return pl.pallas_call(
        solve_kernel,
        out_shape=jax.ShapeDtypeStruct((2 * GB, 256), jnp.bfloat16),
        in_specs=[vmem] * 4,
        out_specs=vmem,
        scratch_shapes=[pltpu.VMEM((12, 128, 128), F32), pltpu.VMEM((3, 128, 128), F32),
                        pltpu.VMEM((2, 384, 384), F32), pltpu.VMEM((256, 256), F32)],
        compiler_params=pltpu.CompilerParams(vmem_limit_bytes=VLIM),
        name="solve",
    )(fg, fa, tr, w)


def gather_kernel(p_ref, o_ref, local, sz, rz, sy, ry, sh, rh, sc, rc):
    dp, own = place()
    core = lax.rem(dp, 2)
    y = dp // 4
    sib = dp + 1 - 2 * core
    zh = lax.rem(dp // 2, 2)
    anti = dp + 2 - 4 * zh
    up = lax.rem(y + 1, 4) * 4 + lax.rem(dp, 4)
    down = lax.rem(y + 3, 4) * 4 + lax.rem(dp, 4)
    barrier = pltpu.get_barrier_semaphore()
    for device in (sib, anti, up, down):
        pl.semaphore_signal(barrier, inc=1, device_id=(device, own), device_id_type=MESH)
    pl.semaphore_wait(barrier, 4)

    def other(d):
        return d + 2 - 4 * lax.rem(d // 2, 2)

    far = lax.rem(y + 2, 4) * 4 + lax.rem(dp, 4)
    waits = []

    def half(ref, h):
        return ref.at[pl.ds(h * CUT[0], CUT[h])]

    def send(d, h, sems, i, device, src=None):
        src = o_ref.at[d] if src is None else src
        copy = pltpu.make_async_remote_copy(
            src_ref=half(src, h), dst_ref=half(o_ref.at[d], h), send_sem=sems[0].at[i], recv_sem=sems[1].at[i],
            device_id=(device, own), device_id_type=MESH)
        copy.start()
        waits.append(copy)

    def arrived(d, h, sems, i):
        dst = half(o_ref.at[d], h)
        pltpu.make_async_remote_copy(src_ref=dst, dst_ref=dst, send_sem=sems[0].at[i], recv_sem=sems[1].at[i],
                                     device_id=(sib, own), device_id_type=MESH).wait_recv()

    zsem, ysem, hsem, csem = (sz, rz), (sy, ry), (sh, rh), (sc, rc)
    for h in range(2):
        send(dp, h, zsem, h, anti, p_ref)
        send(dp, h, ysem, h, up, p_ref)
        send(dp, 1 - h, ysem, 3 - h, down, p_ref)
    for h in range(2):
        send(dp, h, csem, h, sib, p_ref)
    keep = pltpu.make_async_copy(p_ref, o_ref.at[dp], local)
    keep.start()
    arrived(down, 0, ysem, 0)
    send(down, 0, hsem, 0, up)
    arrived(up, 1, ysem, 3)
    send(up, 1, hsem, 1, down)
    send(down, 0, csem, 2, sib)
    send(up, 1, csem, 5, sib)
    arrived(down, 1, ysem, 1)
    send(down, 1, csem, 3, sib)
    arrived(up, 0, ysem, 2)
    send(up, 0, csem, 4, sib)
    arrived(anti, 0, zsem, 0)
    send(anti, 0, ysem, 4, up)
    send(anti, 0, ysem, 6, down)
    send(anti, 0, csem, 6, sib)
    arrived(far, 0, hsem, 0)
    send(far, 0, csem, 8, sib)
    arrived(far, 1, hsem, 1)
    send(far, 1, csem, 9, sib)
    arrived(anti, 1, zsem, 1)
    send(anti, 1, ysem, 5, up)
    send(anti, 1, ysem, 7, down)
    send(anti, 1, csem, 7, sib)
    arrived(other(down), 0, ysem, 4)
    send(other(down), 0, hsem, 2, up)
    send(other(down), 0, csem, 10, sib)
    arrived(other(up), 0, ysem, 6)
    send(other(up), 0, csem, 12, sib)
    arrived(other(up), 1, ysem, 7)
    send(other(up), 1, hsem, 3, down)
    send(other(up), 1, csem, 13, sib)
    arrived(other(down), 1, ysem, 5)
    send(other(down), 1, csem, 11, sib)
    arrived(other(far), 0, hsem, 2)
    send(other(far), 0, csem, 14, sib)
    arrived(other(far), 1, hsem, 3)
    send(other(far), 1, csem, 15, sib)

    def twin(d):
        return d + 1 - 2 * lax.rem(d, 2)

    for i, d in enumerate((dp, down, up, anti, far, other(down), other(up), other(far))):
        for h in range(2):
            arrived(twin(d), h, csem, 2 * i + h)
    keep.wait()
    for copy in waits:
        copy.wait_send()


def gather(p):
    dma = pltpu.SemaphoreType.DMA
    return pl.pallas_call(
        gather_kernel,
        out_shape=jax.ShapeDtypeStruct((16, 2 * GB, 256), jnp.bfloat16),
        in_specs=[pl.BlockSpec(memory_space=pl.ANY)],
        out_specs=pl.BlockSpec(memory_space=pl.ANY),
        scratch_shapes=[dma, dma((2,)), dma((2,)), dma((8,)), dma((8,)), dma((4,)), dma((4,)), dma((16,)), dma((16,))],
        compiler_params=pltpu.CompilerParams(collective_id=2, has_side_effects=True),
        name="gather",
    )(p)


def turn_kernel(i_ref, o_ref):
    for k in range(i_ref.shape[0] // 128):
        o_ref[:, k * 128:(k + 1) * 128] = i_ref[k * 128:(k + 1) * 128, :].T


def turn(slices):
    step = FF // 2
    return pl.pallas_call(
        turn_kernel,
        out_shape=jax.ShapeDtypeStruct((256, FF), jnp.bfloat16),
        grid=(2, 2),
        in_specs=[pl.BlockSpec((step, 128), lambda i, j: (j, i))],
        out_specs=pl.BlockSpec((128, step), lambda i, j: (i, j)),
        compiler_params=pltpu.CompilerParams(vmem_limit_bytes=VLIM),
        name="turn",
    )(slices)


def shards(acts, grads_out, weight_grad):
    sib_acts, sib_grads = swap(acts, grads_out)
    gx, gy, tr = grams(acts, grads_out, sib_acts, sib_grads)
    fg, fa, tr = reduce_all(gx, gy, tr)
    p = solve(fg.reshape(2, 512, 128), fa.reshape(256, 128), tr, weight_grad.T)
    return turn(gather(p).reshape(FF, 256))


def solution(mesh):
    in_specs = (P(("dp", "owner"), None), P(("dp", "owner"), None), P("owner", "dp"))
    out_specs = P("owner", None)
    return jax.shard_map(shards, mesh=mesh, in_specs=in_specs, out_specs=out_specs, check_vma=False)
```

```python
import functools
import math

import jax
import jax.numpy as jnp
from jax import lax
from jax.experimental import pallas as pl
from jax.experimental.pallas import tpu as pltpu
from jax.sharding import PartitionSpec as P

D = 4096
FF = 11008
AB = 256
GB = 344
TOKENS = 57344
DAMP = math.sqrt(0.03)
MESH = pl.DeviceIdType.MESH
F32 = jnp.float32
NB = 2
GROWS = 64 // NB
AROWS = 16 // NB
CH = GROWS + AROWS
HALF = 4 * CH
VLIM = 56 * 1024 * 1024
WIN = 7 * 128
WIDTHS = [WIN] * 7 + [WIN - 128]
CUT = (352, 336)


def grad_position(p, part, core):
    y = p // 2
    return 2 * part + (p + y + core) % 2, y


def act_position(k, part):
    return k % 4, 2 * part + k // 4


def window(d):
    return 128 * (43 * d // 8)


def place():
    dp = lax.axis_index("dp")
    own = lax.axis_index("owner")
    return dp, own


def swap_kernel(a_ref, g_ref, ao_ref, go_ref, send, recv):
    dp, own = place()
    core = lax.rem(dp, 2)
    sib = dp + 1 - 2 * core
    barrier = pltpu.get_barrier_semaphore()
    pl.semaphore_signal(barrier, inc=1, device_id=(sib, own), device_id_type=MESH)
    pl.semaphore_wait(barrier, 1)
    width = ao_ref.shape[1]
    pieces = [(a_ref.at[:, pl.ds(pl.multiple_of((1 - core) * width, 128), width)], ao_ref)]
    for p in range(8):
        start = pl.multiple_of(window(2 * p + 1 - core), 128)
        pieces.append((g_ref.at[:, pl.ds(start, WIDTHS[p])], go_ref.at[:, pl.ds(p * WIN, WIDTHS[p])]))
    copies = []
    for i, (src, dst) in enumerate(pieces):
        copy = pltpu.make_async_remote_copy(
            src_ref=src, dst_ref=dst, send_sem=send.at[i], recv_sem=recv.at[i],
            device_id=(sib, own), device_id_type=MESH)
        copy.start()
        copies.append(copy)
    for copy in copies:
        copy.wait()


def swap(acts, grads):
    rows = acts.shape[0]
    return pl.pallas_call(
        swap_kernel,
        out_shape=(jax.ShapeDtypeStruct((rows, D // 2), acts.dtype),
                   jax.ShapeDtypeStruct((rows, 8 * WIN), acts.dtype)),
        in_specs=[pl.BlockSpec(memory_space=pl.ANY)] * 2,
        out_specs=(pl.BlockSpec(memory_space=pl.ANY),) * 2,
        scratch_shapes=[pltpu.SemaphoreType.DMA((9,))] * 2,
        compiler_params=pltpu.CompilerParams(collective_id=0, has_side_effects=True),
        name="swap",
    )(acts, grads)


def gram(block):
    return lax.dot_general(block, block, (((0,), (0,)), ((), ())), preferred_element_type=F32)


def gram_kernel(a_ref, g_ref, as_ref, gs_ref, x_out, y_out, t_ref, abuf, gbuf, even, x_ref, y_ref, sems, out_sems):
    core = lax.rem(lax.axis_index("dp"), 2)
    rows = a_ref.shape[0]
    mine, theirs = pl.ds(0, rows), pl.ds(rows, rows)
    width = abuf.shape[1]
    moves = [[(a_ref.at[:, pl.ds(pl.multiple_of(core * width, 128), width)], abuf.at[mine]), (as_ref, abuf.at[theirs])]]
    for lo in (0, 4):
        group = []
        for p in range(lo, lo + 4):
            start = pl.multiple_of(window(2 * p + core), 128)
            group.append((g_ref.at[:, pl.ds(start, WIDTHS[p])], gbuf.at[mine, pl.ds(p * WIN, WIDTHS[p])]))
        span = pl.ds(lo * WIN, 4 * WIN - WIN + WIDTHS[lo + 3])
        group.append((gs_ref.at[:, span], gbuf.at[theirs, span]))
        moves.append(group)
    copies = []
    for i, group in enumerate(moves):
        copies.append([pltpu.make_async_copy(src, dst, sems.at[i, n]) for n, (src, dst) in enumerate(group)])
        for copy in copies[i]:
            copy.start()

    def store_all(where, size, lead, row, value):
        px, py = where
        done = 0
        while done < value.shape[0]:
            at = row + done
            n = min(size - at % size, value.shape[0] - done)
            batch, chunk = at // size // 8, at // size % 8
            rows_at = pl.ds(chunk % 4 * CH + lead + at % size, n)
            if chunk < 4:
                x_ref[batch, px * 4 + py, rows_at, :] = value[done:done + n]
            else:
                y_ref[batch, py * 4 + px, rows_at, :] = value[done:done + n]
            done += n

    outs = []

    def finish(where):
        px, py = where
        for i, (src, dst, at) in enumerate(((x_ref, x_out, px * 4 + py), (y_ref, y_out, py * 4 + px))):
            copy = pltpu.make_async_copy(src.at[:, at], dst.at[:, at], out_sems.at[i, px * 4 + py])
            copy.start()
            outs.append(copy)

    r = lax.broadcasted_iota(jnp.int32, (128, 128), 0)
    c = lax.broadcasted_iota(jnp.int32, (128, 128), 1)

    def diag(tile):
        return jnp.sum(jnp.where(r == c, tile, 0.0), axis=0, keepdims=True)

    act_sum = jnp.zeros((1, 128), F32)
    grad_sum = jnp.zeros((1, 128), F32)
    for copy in copies[0]:
        copy.wait()
    for k in range(8):
        g = gram(abuf[:, k * AB:(k + 1) * AB])
        t0, t2 = g[0:128, 0:128], g[128:256, 128:256]
        second = diag(t2)
        act_sum += diag(t0) + second
        t_ref[8 + k:9 + k, :] = second
        store_all(act_position(k, 0), AROWS, GROWS, 0, g[128:256, 0:128])
        store_all(act_position(k, 1), AROWS, GROWS, 0, jnp.where(r >= c, t0, t2))
    for j in range(16):
        if j in (0, 8):
            for copy in copies[1 + j // 8]:
                copy.wait()
            for odd in range(2):
                @pl.when(core == odd)
                def _():
                    for i in range(j, j + 8):
                        d = i // 2 * 2 + odd
                        start = i // 2 * WIN + 2 * GB * d - window(d) + i % 2 * GB
                        even[i, :, 0:GB] = gbuf[:, start:start + GB]
        block = even[j, :, 0:GB]
        g = lax.dot_general(block, block[:, 0:256], (((0,), (0,)), ((), ())), preferred_element_type=F32)
        t0, t2 = g[0:128, 0:128], g[128:256, 128:256]
        t5 = jnp.concatenate([gram(block[:, 256:GB]), jnp.zeros((88, 40), F32)], axis=1)
        second = diag(t2)
        grad_sum += diag(t0) + second + jnp.sum(jnp.where(r[:88] == c[:88], t5, 0.0), axis=0, keepdims=True)
        tail = jnp.concatenate([pltpu.roll(t5[48:88], 40, 1), jnp.zeros((8, 128), F32)], axis=0)
        where = grad_position(j // 2, j % 2, core)
        store_all(where, GROWS, 0, 0, g[128:256, 0:128])
        store_all(where, GROWS, 0, 128, jnp.where(r >= c, t0, t2))
        store_all(where, GROWS, 0, 256, g[256:344, 0:128])
        store_all(where, GROWS, 0, 344, g[256:344, 128:256])
        store_all(where, GROWS, 0, 432, jnp.where(c[:48] < 88, t5[0:48], tail))
        store_all(where, GROWS, 0, 480, jnp.concatenate([second, jnp.zeros((31, 128), F32)], axis=0))
        finish(where)
    t_ref[0:8, :] = jnp.concatenate([act_sum, grad_sum, jnp.zeros((6, 128), F32)], axis=0)
    for copy in outs:
        copy.wait()


def grams(acts, grads, sib_acts, sib_grads):
    shape = jax.ShapeDtypeStruct((NB, 16, HALF, 128), F32)
    vmem = pl.BlockSpec(memory_space=pltpu.VMEM)
    anywhere = pl.BlockSpec(memory_space=pl.ANY)
    rows = acts.shape[0]
    return pl.pallas_call(
        gram_kernel,
        out_shape=(shape, shape, jax.ShapeDtypeStruct((16, 128), F32)),
        in_specs=[anywhere] * 4,
        out_specs=(anywhere, anywhere, vmem),
        scratch_shapes=[pltpu.VMEM((2 * rows, D // 2), acts.dtype), pltpu.VMEM((2 * rows, 8 * WIN), acts.dtype),
                        pltpu.VMEM((16, 2 * rows, 384), acts.dtype),
                        pltpu.VMEM(shape.shape, F32), pltpu.VMEM(shape.shape, F32),
                        pltpu.SemaphoreType.DMA((3, 5)), pltpu.SemaphoreType.DMA((2, 16))],
        compiler_params=pltpu.CompilerParams(vmem_limit_bytes=VLIM),
        name="grams",
    )(acts, grads, sib_acts, sib_grads)


def reduce_kernel(gx, gy, tr, fg, fa, t_out,
                  ps, pk, pm, pr, rx2, ry2, st, rz, fin, ga, aa, t1, t2, t3, q1, q2, q3, q4, tt,
                  local, s1, r1, s2, r2, s3, r3, s4, rg4, ra4, s5, rg5, ra5, ts, tr_sem):
    dp, own = place()
    core = lax.rem(dp, 2)
    zh = lax.rem(dp // 2, 2)
    y = dp // 4
    x = lax.rem(own, 4)
    zl = own // 4
    z = zh * 4 + zl
    sib = dp + 1 - 2 * core

    def at(ax, ay, az, ac):
        return ((ay * 2 + az // 4) * 2 + ac, lax.rem(az, 4) * 4 + ax)

    xs = [at(lax.rem(x + k, 4), y, z, core) for k in (1, 2, 3)]
    ys = [at(x, lax.rem(y + k, 4), z, core) for k in (1, 2, 3)]
    zs = [at(x, y, lax.rem(z + k, 8), core) for k in range(1, 8)]
    g_part, a_part = x // 2, y // 2
    unit_zh = lax.rem(x + y + core, 2)
    unit_zl = 2 * core + lax.rem(y, 2)
    g_on = zh == unit_zh
    a_on = zl == unit_zl
    across = [at(x, lax.rem(y + k, 4), z, 1 - core) for k in range(4)]

    barrier = pltpu.get_barrier_semaphore()
    for device in xs + ys + zs + across:
        pl.semaphore_signal(barrier, inc=1, device_id=device, device_id_type=MESH)
    pl.semaphore_wait(barrier, 17)

    def remote(src, dst, ssem, rsem, device):
        return pltpu.make_async_remote_copy(src_ref=src, dst_ref=dst, send_sem=ssem, recv_sem=rsem,
                                            device_id=device, device_id_type=MESH)

    def begin(copies):
        for copy in copies:
            copy.start()
        return copies

    def end(copies):
        for copy in copies:
            copy.wait()

    axes = ((0, gx, x, (xs[0], xs[2])), (1, gy, y, (ys[0], ys[2])))

    def plane(b):
        copies = []
        for a, g, me, (up, down) in axes:
            over, under, opposite = lax.rem(me + 1, 4) * 4, lax.rem(me + 3, 4) * 4, lax.rem(me + 2, 4) * 4
            copies.append(remote(g.at[b, pl.ds(opposite, 2)], pm.at[a, b, 0], s1.at[a, b, 0], r1.at[a, b, 0], up))
            copies.append(remote(g.at[b, pl.ds(opposite + 2, 2)], pm.at[a, b, 1],
                                 s1.at[a, b, 1], r1.at[a, b, 1], down))
            copies.append(pltpu.make_async_copy(g.at[b, pl.ds(over, 2)], pk.at[a, b, 0], local.at[a, b, 0]))
            copies.append(pltpu.make_async_copy(g.at[b, pl.ds(under + 2, 2)], pk.at[a, b, 1], local.at[a, b, 1]))
        for a, g, me, (up, down) in axes:
            over, under = lax.rem(me + 1, 4) * 4, lax.rem(me + 3, 4) * 4
            copies.append(remote(g.at[b, pl.ds(over + 2, 2)], pr.at[a, b, 0, pl.ds(2, 2)],
                                 s1.at[a, b, 2], r1.at[a, b, 2], up))
            copies.append(remote(g.at[b, pl.ds(under, 2)], pr.at[a, b, 1, pl.ds(0, 2)],
                                 s1.at[a, b, 3], r1.at[a, b, 3], down))
            copies.append(pltpu.make_async_copy(g.at[b, pl.ds(me * 4, 4)], ps.at[a, b], local.at[a, b, 2]))
        return begin(copies)

    def plane_pass(b, copies):
        end(copies[:8])
        @pl.loop(0, 8)
        def _(i):
            h, rows = i // 4, pl.ds(pl.multiple_of(lax.rem(i, 4) * CH, 8), CH)
            for a in range(2):
                for d in range(2):
                    pk[a, b, d, h, rows, :] += pm[a, b, d, h, rows, :]
        for a, _, _, to in axes:
            for d in range(2):
                copies.append(remote(pk.at[a, b, d], pr.at[a, b, d, pl.ds(2 * d, 2)],
                                     s1.at[a, b, 4 + d], r1.at[a, b, 4 + d], to[d]))
                copies[-1].start()

    def plane_sum(b, copies):
        end(copies[8:])
        @pl.loop(0, 16)
        def _(i):
            q, rows = i // 4, pl.ds(pl.multiple_of(lax.rem(i, 4) * CH, 8), CH)
            for a in range(2):
                ps[a, b, q, rows, :] += pr[a, b, 0, q, rows, :] + pr[a, b, 1, q, rows, :]

    def cross(b):
        copies = []
        for k in range(3):
            copies.append(remote(ps.at[0, b, lax.rem(y + k + 1, 4)], rx2.at[b, k], s2.at[b, k], r2.at[b, k], ys[k]))
            copies.append(remote(ps.at[1, b, lax.rem(x + k + 1, 4)], ry2.at[b, k],
                                 s2.at[b, 3 + k], r2.at[b, 3 + k], xs[k]))
        return begin(copies)

    def cross_sum(b):
        @pl.loop(0, 4)
        def _(i):
            rows = pl.ds(pl.multiple_of(i * CH, 8), CH)
            st[b, i] = (ps[0, b, y, rows, :] + rx2[b, 0, rows, :]) + (rx2[b, 1, rows, :] + rx2[b, 2, rows, :])
            st[b, 4 + i] = (ps[1, b, x, rows, :] + ry2[b, 0, rows, :]) + (ry2[b, 1, rows, :] + ry2[b, 2, rows, :])

    def along(b):
        return begin([remote(st.at[b, lax.rem(z + k + 1, 8)], rz.at[b, k], s3.at[b, k], r3.at[b, k], zs[k])
                      for k in range(7)])

    def along_sum(b):
        total = st[b, z]
        for k in range(7):
            total += rz[b, k]
        fin[b] = total

    def spread(b):
        for i in range(6):
            if i < 4:
                to = unit_zh * 4 + i
                src, dst, rsem = fin.at[b, pl.ds(0, GROWS)], ga.at[b, z], rg4.at[b, z]
            else:
                to = (i - 4) * 4 + unit_zl
                src, dst, rsem = fin.at[b, pl.ds(GROWS, AROWS)], aa.at[b, z], ra4.at[b, z]

            @pl.when(to == z)
            def _():
                pltpu.make_async_copy(src, dst, rsem).start()

            @pl.when(to != z)
            def _():
                remote(src, dst, s4.at[b, i], rsem, at(x, y, to, core)).start()

    def spread_sent(b):
        for i in range(6):
            to = unit_zh * 4 + i if i < 4 else (i - 4) * 4 + unit_zl
            src = fin.at[b, pl.ds(0, GROWS)] if i < 4 else fin.at[b, pl.ds(GROWS, AROWS)]
            dst, rsem = (ga.at[b, z], rg4.at[b, z]) if i < 4 else (aa.at[b, z], ra4.at[b, z])

            @pl.when(to != z)
            def _():
                remote(src, dst, s4.at[b, i], rsem, at(x, y, to, core)).wait_send()

    def parts(b):
        return ((g_on, ga.at[b], xs, fg.at[g_part, b], rg5.at[b, g_part], 0),
                (a_on, aa.at[b], ys + across, fa.at[a_part, b], ra5.at[b, a_part], 3))

    def give(b):
        for on, src, to, dst, rsem, first in parts(b):
            @pl.when(on)
            def _():
                for i in range(8):
                    piece = fin.at[b, pl.ds(0, GROWS)] if first == 0 else fin.at[b, pl.ds(GROWS, AROWS)]
                    arrive = (rg4 if first == 0 else ra4).at[b, i]
                    pltpu.make_async_copy(piece, src.at[i], arrive).wait()
                for i, device in enumerate(to):
                    remote(src, dst, s5.at[b, first + i], rsem, device).start()
                pltpu.make_async_copy(src, dst, rsem).start()

    def given(b):
        for on, src, to, dst, rsem, first in parts(b):
            @pl.when(on)
            def _():
                for i, device in enumerate(to):
                    remote(src, dst, s5.at[b, first + i], rsem, device).wait_send()

    def taken(b):
        for i in range(2):
            pltpu.make_async_copy(ga.at[b], fg.at[i, b], rg5.at[b, i]).wait()
            pltpu.make_async_copy(aa.at[b], fa.at[i, b], ra5.at[b, i]).wait()

    batches = range(NB)
    q = begin([remote(tr, q1.at[k], ts.at[k], tr_sem.at[k], xs[k]) for k in range(3)])
    first, second, third = {}, {}, {}
    first[0] = plane(0)
    plane_pass(0, first[0])
    first[1] = plane(1)
    plane_sum(0, first[0])
    second[0] = cross(0)
    end(q)
    t1[...] = (tr[...] + q1[0]) + (q1[1] + q1[2])
    q = begin([remote(t1, q2.at[k], ts.at[3 + k], tr_sem.at[3 + k], ys[k]) for k in range(3)])
    plane_pass(1, first[1])
    end(second[0])
    cross_sum(0)
    third[0] = along(0)
    end(q)
    t2[...] = (t1[...] + q2[0]) + (q2[1] + q2[2])
    q = begin([remote(t2, q3.at[k], ts.at[6 + k], tr_sem.at[6 + k], zs[k]) for k in range(7)])
    plane_sum(1, first[1])
    second[1] = cross(1)
    end(third[0])
    along_sum(0)
    spread(0)
    end(q)
    trace = t2[...]
    for k in range(7):
        trace += q3[k]
    t3[...] = trace
    q = begin([remote(t3, q4, ts.at[13], tr_sem.at[13], (sib, own))])
    end(second[1])
    cross_sum(1)
    third[1] = along(1)
    give(0)
    end(third[1])
    along_sum(1)
    spread(1)
    give(1)
    end(q)
    tt[core] = t3[...]
    tt[1 - core] = q4[...]
    t_out[0:8, :] = tt[0, 0:8, :] + tt[1, 0:8, :]
    t_out[8:16, :] = jnp.broadcast_to(tt[own // 8, pl.ds(8 + lax.rem(own, 8), 1), :], (8, 128))
    for b in batches:
        taken(b)
    for b in batches:
        spread_sent(b)
        given(b)


def reduce_all(gx, gy, tr):
    vmem = pl.BlockSpec(memory_space=pltpu.VMEM)
    dma = pltpu.SemaphoreType.DMA
    tile = pltpu.VMEM((16, 128), F32)

    def buf(*shape):
        return pltpu.VMEM(shape + (128,), F32)

    return pl.pallas_call(
        reduce_kernel,
        out_shape=(jax.ShapeDtypeStruct((2, NB, 8, GROWS, 128), F32),
                   jax.ShapeDtypeStruct((2, NB, 8, AROWS, 128), F32),
                   jax.ShapeDtypeStruct((16, 128), F32)),
        in_specs=[pl.BlockSpec(memory_space=pl.ANY)] * 2 + [vmem],
        out_specs=(vmem,) * 3,
        scratch_shapes=[
            buf(2, NB, 4, HALF), buf(2, NB, 2, 2, HALF), buf(2, NB, 2, 2, HALF), buf(2, NB, 2, 4, HALF),
            buf(NB, 3, HALF), buf(NB, 3, HALF), buf(NB, 8, CH), buf(NB, 7, CH), buf(NB, CH),
            buf(NB, 8, GROWS), buf(NB, 8, AROWS),
            tile, tile, tile, buf(3, 16), buf(3, 16), buf(7, 16), tile, buf(2, 16),
            dma((2, NB, 3)), dma((2, NB, 6)), dma((2, NB, 6)), dma((NB, 6)), dma((NB, 6)), dma((NB, 7)), dma((NB, 7)),
            dma((NB, 6)), dma((NB, 8)), dma((NB, 8)), dma((NB, 10)), dma((NB, 2)), dma((NB, 2)), dma((14,)), dma((14,)),
        ],
        compiler_params=pltpu.CompilerParams(collective_id=1, has_side_effects=True, vmem_limit_bytes=VLIM),
        name="reduce_all",
    )(gx, gy, tr)


def split(v):
    high = v.astype(jnp.bfloat16).astype(F32)
    rest = v - high
    mid = rest.astype(jnp.bfloat16).astype(F32)
    return high, mid, rest - mid


def dot(a, b, ca=1, cb=0):
    ah, am, al = split(a)
    bh, bm, bl = split(b)
    left = jnp.concatenate([ah, ah, am, ah, am, al], axis=ca).astype(jnp.bfloat16)
    right = jnp.concatenate([bh, bm, bh, bl, bm, bh], axis=cb).astype(jnp.bfloat16)
    return lax.dot_general(left, right, (((ca,), (cb,)), ((), ())), preferred_element_type=F32)


def sweep_four(now, at, row, sub, lane):
    def full(v):
        return jnp.broadcast_to(v, (8, 128))

    four = range(4)
    cols = [full(now[:, at + i:at + i + 1]) for i in four]
    rows = [full(now[row + i:row + i + 1, :]) for i in four]
    m = {(i, j): full(cols[j][row + i:row + i + 1, :]) for i in four for j in range(i + 1)}
    for p in four:
        inv = 1.0 / m[(p, p)]
        line = {i: m[(max(i, p), min(i, p))] * inv for i in four if i != p}
        new = {}
        for i in four:
            for j in range(i + 1):
                if i == p and j == p:
                    new[(i, j)] = -inv
                elif i == p:
                    new[(i, j)] = line[j]
                elif j == p:
                    new[(i, j)] = line[i]
                else:
                    new[(i, j)] = m[(i, j)] - m[(max(i, p), min(i, p))] * line[j]
        m = new
    in_rows = jnp.logical_and(sub >= row, sub < row + 4)
    in_cols = jnp.logical_and(lane >= at, lane < at + 4)
    out = jnp.where(jnp.logical_or(in_rows, in_cols), 0.0, now)
    rows = [jnp.where(in_cols, jnp.where(lane == at + i, -1.0, 0.0), rows[i]) for i in four]
    for i in four:
        col = jnp.where(in_rows, jnp.where(sub == row + i, -1.0, 0.0), cols[i])
        term = m[(i, 0)] * rows[0]
        for j in range(1, 4):
            term = term + m[(max(i, j), min(i, j))] * rows[j]
        out = out + col * term
    return out


def sweep_tiles(refs, panels, others=()):
    others = list(others)
    sub = lax.broadcasted_iota(jnp.int32, (8, 128), 0)
    lane = lax.broadcasted_iota(jnp.int32, (8, 128), 1)
    lane_all = lax.broadcasted_iota(jnp.int32, (128, 128), 1)
    for p in range(panels):
        base = 8 * p
        inside = jnp.logical_and(lane_all >= base, lane_all < base + 8)
        olds = [ref[base:base + 8, :] for ref in refs]
        news = [sweep_four(old, base, 0, sub, lane) for old in olds]
        news = [sweep_four(new, base + 4, 4, sub, lane) for new in news]
        for ref, old, new in zip(refs, olds, news):
            ref[...] = jnp.where(inside, 0.0, ref[...]) - dot(old, new, 0, 0)
            ref[base:base + 8, :] = new
        count = -(-len(others) // (panels - p))
        for step in others[:count]:
            step()
        others = others[count:]


def solve_kernel(fg_ref, fa_ref, t_ref, w_ref, p_ref, g_ref, a_ref, l_ref, x_ref, ai_ref):
    act_trace = jnp.sum(t_ref[0:1, :], keepdims=True) / TOKENS
    grad_trace = jnp.sum(t_ref[1:2, :], keepdims=True) / TOKENS
    ratio = jnp.sqrt(act_trace / D / (grad_trace / FF))
    act_damp = ratio * DAMP
    grad_damp = DAMP / ratio
    r = lax.broadcasted_iota(jnp.int32, (128, 128), 0)
    c = lax.broadcasted_iota(jnp.int32, (128, 128), 1)
    last = GB - 256

    def pair(both, second):
        turned = both.T
        first = jnp.where(r >= c, both, turned)
        other = jnp.where(r < c, both, jnp.where(r == c, jnp.broadcast_to(second, (128, 128)), turned))
        return first, other

    def damped(tile, damp):
        return tile / TOKENS + jnp.where(r == c, damp, 0.0)

    zeros = jnp.zeros((128 - last, 128), F32)
    for b in range(2):
        first, second = pair(fg_ref[b, 128:256, :], fg_ref[b, 480:481, :])
        g_ref[b * 6] = damped(first, grad_damp)
        g_ref[b * 6 + 1] = fg_ref[b, 0:128, :] / TOKENS
        g_ref[b * 6 + 2] = damped(second, grad_damp)
        g_ref[b * 6 + 3] = jnp.concatenate([fg_ref[b, 256:344, :] / TOKENS, zeros], axis=0)
        g_ref[b * 6 + 4] = jnp.concatenate([fg_ref[b, 344:432, :] / TOKENS, zeros], axis=0)
        packed = fg_ref[b, 432:480, :]
        low = pltpu.roll(packed[0:40], 88, 1)
        upper = jnp.concatenate([packed, low, jnp.zeros((40, 128), F32)], axis=0)
        corner = jnp.where(jnp.logical_and(r >= 48, c < 48), upper.T, upper)
        inside = jnp.logical_and(r < last, c < last)
        g_ref[b * 6 + 5] = jnp.where(inside, damped(corner, grad_damp), jnp.where(r == c, 1.0, 0.0))
    first, second = pair(fa_ref[128:256, :], t_ref[8:9, :])
    a_ref[0] = damped(first, act_damp)
    a_ref[1] = fa_ref[0:128, :] / TOKENS
    a_ref[2] = damped(second, act_damp)
    gs = [[g_ref.at[b * 6 + t] for t in range(6)] for b in range(2)]
    am = [a_ref.at[t] for t in range(3)]
    sweep_tiles([gs[0][0], gs[1][0], am[0]], 16)
    for m in gs + [am]:
        a10 = m[1][...]
        l10 = -dot(a10, m[0][...])
        m[2][...] -= dot(l10, a10, 1, 1)
        l_ref[0 if m is gs[0] else 1 if m is gs[1] else 2] = l10

    def row_two(b):
        m = gs[b]
        a20 = m[3][...]

        def lower():
            l_ref[3 + b] = -dot(a20, m[0][...])

        def side():
            m[4][...] -= dot(l_ref[3 + b], m[1][...], 1, 1)

        def corner():
            m[5][...] -= dot(l_ref[3 + b], a20, 1, 1)
        return [lower, side, corner]

    steps = [step for pair_of in zip(row_two(0), row_two(1)) for step in pair_of]
    sweep_tiles([gs[0][2], gs[1][2], am[2]], 16, steps)
    for b, m in enumerate(gs):
        a21 = m[4][...]
        l21 = -dot(a21, m[2][...])
        m[5][...] -= dot(l21, a21, 1, 1)
        l_ref[5 + b] = l21

    def act_cross():
        v10 = -dot(am[2][...], l_ref[2])
        ai_ref[128:256, 0:128] = -v10
        ai_ref[0:128, 128:256] = -v10.T
        ai_ref[128:256, 128:256] = -am[2][...]

    def act_first():
        ai_ref[0:128, 0:128] = -am[0][...] - dot(l_ref[2], ai_ref[128:256, 0:128], 0, 0)

    def right_side(b):
        w = w_ref[...].astype(F32)[b * GB:(b + 1) * GB]
        w = jnp.concatenate([w, jnp.zeros((384 - GB, 256), F32)], axis=0).astype(jnp.bfloat16)
        pieces = jnp.concatenate(split(ai_ref[...]), axis=0).astype(jnp.bfloat16)
        x_ref[b] = jnp.dot(jnp.concatenate([w, w, w], axis=1), pieces, preferred_element_type=F32)

    def through(b):
        x = [x_ref.at[b, pl.ds(128 * i, 128)] for i in range(3)]
        l10, l20, l21 = l_ref.at[b], l_ref.at[3 + b], l_ref.at[5 + b]
        m = gs[b]

        def one():
            x[1][...] -= dot(l10[...], x[0][...])

        def two():
            x[2][...] -= dot(l20[...], x[0][...])

        def three():
            x[2][...] -= dot(l21[...], x[1][...])

        def four():
            x[1][...] = -dot(m[2][...], x[1][...])

        def five():
            x[0][...] = -dot(m[0][...], x[0][...])

        def six():
            x[0][...] -= dot(l10[...], x[1][...], 0, 0)

        def seven():
            l20[...] -= dot(l21[...], l10[...])
        return [one, two, three, four, five, six, seven]

    steps = [act_cross, act_first, lambda: right_side(0), lambda: right_side(1)]
    steps += [step for pair_of in zip(through(0), through(1)) for step in pair_of]
    sweep_tiles([gs[0][5], gs[1][5]], last // 8, steps)
    out = []
    for b, m in enumerate(gs):
        y2 = -dot(m[5][...], x_ref[b, 256:384])
        out += [x_ref[b, 0:128] - dot(l_ref[3 + b], y2, 0, 0),
                x_ref[b, 128:256] - dot(l_ref[5 + b], y2, 0, 0), y2[0:last]]
    p_ref[...] = jnp.concatenate(out, axis=0).astype(jnp.bfloat16)


def solve(fg, fa, tr, w):
    vmem = pl.BlockSpec(memory_space=pltpu.VMEM)
    return pl.pallas_call(
        solve_kernel,
        out_shape=jax.ShapeDtypeStruct((2 * GB, 256), jnp.bfloat16),
        in_specs=[vmem] * 4,
        out_specs=vmem,
        scratch_shapes=[pltpu.VMEM((12, 128, 128), F32), pltpu.VMEM((3, 128, 128), F32),
                        pltpu.VMEM((7, 128, 128), F32), pltpu.VMEM((2, 384, 256), F32),
                        pltpu.VMEM((256, 256), F32)],
        compiler_params=pltpu.CompilerParams(vmem_limit_bytes=VLIM),
        name="solve",
    )(fg, fa, tr, w)


def gather_kernel(p_ref, o_ref, local, sz, rz, sy, ry, sh, rh, sc, rc):
    dp, own = place()
    core = lax.rem(dp, 2)
    y = dp // 4
    sib = dp + 1 - 2 * core
    zh = lax.rem(dp // 2, 2)
    anti = dp + 2 - 4 * zh
    up = lax.rem(y + 1, 4) * 4 + lax.rem(dp, 4)
    down = lax.rem(y + 3, 4) * 4 + lax.rem(dp, 4)
    barrier = pltpu.get_barrier_semaphore()
    for device in (sib, anti, up, down):
        pl.semaphore_signal(barrier, inc=1, device_id=(device, own), device_id_type=MESH)
    pl.semaphore_wait(barrier, 4)

    def other(d):
        return d + 2 - 4 * lax.rem(d // 2, 2)

    far = lax.rem(y + 2, 4) * 4 + lax.rem(dp, 4)
    waits = []

    def half(ref, h):
        return ref.at[pl.ds(h * CUT[0], CUT[h])]

    def send(d, h, sems, i, device, src=None):
        src = o_ref.at[d] if src is None else src
        copy = pltpu.make_async_remote_copy(
            src_ref=half(src, h), dst_ref=half(o_ref.at[d], h), send_sem=sems[0].at[i], recv_sem=sems[1].at[i],
            device_id=(device, own), device_id_type=MESH)
        copy.start()
        waits.append(copy)

    def arrived(d, h, sems, i):
        dst = half(o_ref.at[d], h)
        pltpu.make_async_remote_copy(src_ref=dst, dst_ref=dst, send_sem=sems[0].at[i], recv_sem=sems[1].at[i],
                                     device_id=(sib, own), device_id_type=MESH).wait_recv()

    zsem, ysem, hsem, csem = (sz, rz), (sy, ry), (sh, rh), (sc, rc)
    for h in range(2):
        send(dp, h, zsem, h, anti, p_ref)
        send(dp, h, ysem, h, up, p_ref)
        send(dp, 1 - h, ysem, 3 - h, down, p_ref)
    for h in range(2):
        send(dp, h, csem, h, sib, p_ref)
    keep = pltpu.make_async_copy(p_ref, o_ref.at[dp], local)
    keep.start()
    arrived(down, 0, ysem, 0)
    send(down, 0, hsem, 0, up)
    arrived(up, 1, ysem, 3)
    send(up, 1, hsem, 1, down)
    send(down, 0, csem, 2, sib)
    send(up, 1, csem, 5, sib)
    arrived(down, 1, ysem, 1)
    send(down, 1, csem, 3, sib)
    arrived(up, 0, ysem, 2)
    send(up, 0, csem, 4, sib)
    arrived(anti, 0, zsem, 0)
    send(anti, 0, ysem, 4, up)
    send(anti, 0, ysem, 6, down)
    send(anti, 0, csem, 6, sib)
    arrived(far, 0, hsem, 0)
    send(far, 0, csem, 8, sib)
    arrived(far, 1, hsem, 1)
    send(far, 1, csem, 9, sib)
    arrived(anti, 1, zsem, 1)
    send(anti, 1, ysem, 5, up)
    send(anti, 1, ysem, 7, down)
    send(anti, 1, csem, 7, sib)
    arrived(other(down), 0, ysem, 4)
    send(other(down), 0, hsem, 2, up)
    send(other(down), 0, csem, 10, sib)
    arrived(other(up), 0, ysem, 6)
    send(other(up), 0, csem, 12, sib)
    arrived(other(up), 1, ysem, 7)
    send(other(up), 1, hsem, 3, down)
    send(other(up), 1, csem, 13, sib)
    arrived(other(down), 1, ysem, 5)
    send(other(down), 1, csem, 11, sib)
    arrived(other(far), 0, hsem, 2)
    send(other(far), 0, csem, 14, sib)
    arrived(other(far), 1, hsem, 3)
    send(other(far), 1, csem, 15, sib)

    def twin(d):
        return d + 1 - 2 * lax.rem(d, 2)

    for i, d in enumerate((dp, down, up, anti, far, other(down), other(up), other(far))):
        for h in range(2):
            arrived(twin(d), h, csem, 2 * i + h)
    keep.wait()
    for copy in waits:
        copy.wait_send()


def gather(p):
    dma = pltpu.SemaphoreType.DMA
    return pl.pallas_call(
        gather_kernel,
        out_shape=jax.ShapeDtypeStruct((16, 2 * GB, 256), jnp.bfloat16),
        in_specs=[pl.BlockSpec(memory_space=pl.ANY)],
        out_specs=pl.BlockSpec(memory_space=pl.ANY),
        scratch_shapes=[dma, dma((2,)), dma((2,)), dma((8,)), dma((8,)), dma((4,)), dma((4,)), dma((16,)), dma((16,))],
        compiler_params=pltpu.CompilerParams(collective_id=2, has_side_effects=True),
        name="gather",
    )(p)


def turn_kernel(i_ref, o_ref):
    for k in range(i_ref.shape[0] // 128):
        o_ref[:, k * 128:(k + 1) * 128] = i_ref[k * 128:(k + 1) * 128, :].T


def turn(slices):
    step = FF // 2
    return pl.pallas_call(
        turn_kernel,
        out_shape=jax.ShapeDtypeStruct((256, FF), jnp.bfloat16),
        grid=(2, 2),
        in_specs=[pl.BlockSpec((step, 128), lambda i, j: (j, i))],
        out_specs=pl.BlockSpec((128, step), lambda i, j: (i, j)),
        compiler_params=pltpu.CompilerParams(vmem_limit_bytes=VLIM),
        name="turn",
    )(slices)


def shards(acts, grads_out, weight_grad):
    sib_acts, sib_grads = swap(acts, grads_out)
    gx, gy, tr = grams(acts, grads_out, sib_acts, sib_grads)
    fg, fa, tr = reduce_all(gx, gy, tr)
    p = solve(fg.reshape(2, 512, 128), fa.reshape(256, 128), tr, weight_grad.T)
    return turn(gather(p).reshape(FF, 256))


def solution(mesh):
    in_specs = (P(("dp", "owner"), None), P(("dp", "owner"), None), P("owner", "dp"))
    out_specs = P("owner", None)
    return jax.shard_map(shards, mesh=mesh, in_specs=in_specs, out_specs=out_specs, check_vma=False)
```

```python
import functools
import math

import jax
import jax.numpy as jnp
from jax import lax
from jax.experimental import pallas as pl
from jax.experimental.pallas import tpu as pltpu
from jax.sharding import PartitionSpec as P

D = 4096
FF = 11008
AB = 256
GB = 344
TOKENS = 57344
DAMP = math.sqrt(0.03)
MESH = pl.DeviceIdType.MESH
F32 = jnp.float32
NB = 2
GROWS = 64 // NB
AROWS = 16 // NB
CH = GROWS + AROWS
HALF = 4 * CH
VLIM = 56 * 1024 * 1024
WIN = 7 * 128
WIDTHS = [WIN] * 7 + [WIN - 128]
CUT = (352, 336)


def grad_position(p, part, core):
    y = p // 2
    return 2 * part + (p + y + core) % 2, y


def act_position(k, part):
    return k % 4, 2 * part + k // 4


def window(d):
    return 128 * (43 * d // 8)


def place():
    dp = lax.axis_index("dp")
    own = lax.axis_index("owner")
    return dp, own


def gram(block):
    return lax.dot_general(block, block, (((0,), (0,)), ((), ())), preferred_element_type=F32)


def fetch(a_ref, g_ref, abuf, gbuf, core, sibling, sems, send, recv):
    rows = a_ref.shape[0]
    mine, theirs = pl.ds(0, rows), pl.ds(rows, rows)
    width = abuf.shape[1]

    def half(c):
        return a_ref.at[:, pl.ds(pl.multiple_of(c * width, 128), width)]

    def columns(p, c):
        return g_ref.at[:, pl.ds(pl.multiple_of(window(2 * p + c), 128), WIDTHS[p])]

    here = [[(half(core), abuf.at[mine])], [], []]
    away = [[(half(1 - core), abuf.at[theirs])], [], []]
    for p in range(8):
        at = pl.ds(p * WIN, WIDTHS[p])
        here[1 + p // 4].append((columns(p, core), gbuf.at[mine, at]))
        away[1 + p // 4].append((columns(p, 1 - core), gbuf.at[theirs, at]))
    here = [[pltpu.make_async_copy(src, dst, sems.at[i, n]) for n, (src, dst) in enumerate(group)]
            for i, group in enumerate(here)]
    away = [[pltpu.make_async_remote_copy(src_ref=src, dst_ref=dst, send_sem=send.at[i, n], recv_sem=recv.at[i, n],
                                          device_id=sibling, device_id_type=MESH)
             for n, (src, dst) in enumerate(group)] for i, group in enumerate(away)]
    for group in here:
        for copy in group:
            copy.start()
    return here, away


def gram_step(copies, core, abuf, gbuf, even, x_ref, y_ref, t_ref):
    def store_all(where, size, lead, row, value):
        px, py = where
        done = 0
        while done < value.shape[0]:
            at = row + done
            n = min(size - at % size, value.shape[0] - done)
            batch, chunk = at // size // 8, at // size % 8
            rows_at = pl.ds(chunk % 4 * CH + lead + at % size, n)
            if chunk < 4:
                x_ref[batch, px * 4 + py, rows_at, :] = value[done:done + n]
            else:
                y_ref[batch, py * 4 + px, rows_at, :] = value[done:done + n]
            done += n

    r = lax.broadcasted_iota(jnp.int32, (128, 128), 0)
    c = lax.broadcasted_iota(jnp.int32, (128, 128), 1)

    def diag(tile):
        return jnp.sum(jnp.where(r == c, tile, 0.0), axis=0, keepdims=True)

    act_sum = jnp.zeros((1, 128), F32)
    grad_sum = jnp.zeros((1, 128), F32)
    for copy in copies[0]:
        copy.wait()
    for k in range(8):
        g = gram(abuf[:, k * AB:(k + 1) * AB])
        t0, t2 = g[0:128, 0:128], g[128:256, 128:256]
        second = diag(t2)
        act_sum += diag(t0) + second
        t_ref[8 + k:9 + k, :] = second
        store_all(act_position(k, 0), AROWS, GROWS, 0, g[128:256, 0:128])
        store_all(act_position(k, 1), AROWS, GROWS, 0, jnp.where(r >= c, t0, t2))
    for j in range(16):
        if j in (0, 8):
            for copy in copies[1 + j // 8]:
                copy.wait()
            for odd in range(2):
                @pl.when(core == odd)
                def _():
                    for i in range(j, j + 8):
                        d = i // 2 * 2 + odd
                        start = i // 2 * WIN + 2 * GB * d - window(d) + i % 2 * GB
                        even[i, :, 0:GB] = gbuf[:, start:start + GB]
        block = even[j, :, 0:GB]
        g = lax.dot_general(block, block[:, 0:256], (((0,), (0,)), ((), ())), preferred_element_type=F32)
        t0, t2 = g[0:128, 0:128], g[128:256, 128:256]
        t5 = jnp.concatenate([gram(block[:, 256:GB]), jnp.zeros((88, 40), F32)], axis=1)
        second = diag(t2)
        grad_sum += diag(t0) + second + jnp.sum(jnp.where(r[:88] == c[:88], t5, 0.0), axis=0, keepdims=True)
        tail = jnp.concatenate([pltpu.roll(t5[48:88], 40, 1), jnp.zeros((8, 128), F32)], axis=0)
        where = grad_position(j // 2, j % 2, core)
        store_all(where, GROWS, 0, 0, g[128:256, 0:128])
        store_all(where, GROWS, 0, 128, jnp.where(r >= c, t0, t2))
        store_all(where, GROWS, 0, 256, g[256:344, 0:128])
        store_all(where, GROWS, 0, 344, g[256:344, 128:256])
        store_all(where, GROWS, 0, 432, jnp.where(c[:48] < 88, t5[0:48], tail))
        store_all(where, GROWS, 0, 480, jnp.concatenate([second, jnp.zeros((31, 128), F32)], axis=0))
    t_ref[0:8, :] = jnp.concatenate([act_sum, grad_sum, jnp.zeros((6, 128), F32)], axis=0)


def reduce_kernel(a_ref, g_ref, fg, fa, t_out,
                  abuf, gbuf, even, gx, gy, tr, ps, pk, pm, pr, rx2, ry2, st, rz, fin, ga, aa, t1, t2, t3, q1, q2, q3, q4, tt,
                  local, s0, r0, s1, r1, s2, r2, s3, r3, s4, rg4, ra4, s5, rg5, ra5, ts, tr_sem):
    dp, own = place()
    core = lax.rem(dp, 2)
    zh = lax.rem(dp // 2, 2)
    y = dp // 4
    x = lax.rem(own, 4)
    zl = own // 4
    z = zh * 4 + zl
    sib = dp + 1 - 2 * core

    def at(ax, ay, az, ac):
        return ((ay * 2 + az // 4) * 2 + ac, lax.rem(az, 4) * 4 + ax)

    xs = [at(lax.rem(x + k, 4), y, z, core) for k in (1, 2, 3)]
    ys = [at(x, lax.rem(y + k, 4), z, core) for k in (1, 2, 3)]
    zs = [at(x, y, lax.rem(z + k, 8), core) for k in range(1, 8)]
    g_part, a_part = x // 2, y // 2
    unit_zh = lax.rem(x + y + core, 2)
    unit_zl = 2 * core + lax.rem(y, 2)
    g_on = zh == unit_zh
    a_on = zl == unit_zl
    across = [at(x, lax.rem(y + k, 4), z, 1 - core) for k in range(4)]

    here, away = fetch(a_ref, g_ref, abuf, gbuf, core, (sib, own), local, s0, r0)
    barrier = pltpu.get_barrier_semaphore()
    for device in xs + ys + zs + across:
        pl.semaphore_signal(barrier, inc=1, device_id=device, device_id_type=MESH)
    pl.semaphore_wait(barrier, 17)
    for group in away:
        for copy in group:
            copy.start()
    gram_step([h + a for h, a in zip(here, away)], core, abuf, gbuf, even, gx, gy, tr)

    def remote(src, dst, ssem, rsem, device):
        return pltpu.make_async_remote_copy(src_ref=src, dst_ref=dst, send_sem=ssem, recv_sem=rsem,
                                            device_id=device, device_id_type=MESH)

    def begin(copies):
        for copy in copies:
            copy.start()
        return copies

    def end(copies):
        for copy in copies:
            copy.wait()

    axes = ((0, gx, x, (xs[0], xs[2])), (1, gy, y, (ys[0], ys[2])))

    def plane(b):
        copies = []
        for a, g, me, (up, down) in axes:
            opposite = lax.rem(me + 2, 4) * 4
            copies.append(remote(g.at[b, pl.ds(opposite, 2)], pm.at[a, b, 0], s1.at[a, b, 0], r1.at[a, b, 0], up))
            copies.append(remote(g.at[b, pl.ds(opposite + 2, 2)], pm.at[a, b, 1],
                                 s1.at[a, b, 1], r1.at[a, b, 1], down))
        for a, g, me, (up, down) in axes:
            over, under = lax.rem(me + 1, 4) * 4, lax.rem(me + 3, 4) * 4
            copies.append(remote(g.at[b, pl.ds(over + 2, 2)], pr.at[a, b, 0, pl.ds(2, 2)],
                                 s1.at[a, b, 2], r1.at[a, b, 2], up))
            copies.append(remote(g.at[b, pl.ds(under, 2)], pr.at[a, b, 1, pl.ds(0, 2)],
                                 s1.at[a, b, 3], r1.at[a, b, 3], down))
        return begin(copies)

    def plane_pass(b, copies):
        end(copies[:4])
        @pl.loop(0, 8)
        def _(i):
            h, rows = i // 4, pl.ds(pl.multiple_of(lax.rem(i, 4) * CH, 8), CH)
            for a, g, me, _ in axes:
                over, under = lax.rem(me + 1, 4) * 4, lax.rem(me + 3, 4) * 4
                pk[a, b, 0, h, rows, :] = g[b, over + h, rows, :] + pm[a, b, 0, h, rows, :]
                pk[a, b, 1, h, rows, :] = g[b, under + 2 + h, rows, :] + pm[a, b, 1, h, rows, :]
        for a, _, _, to in axes:
            for d in range(2):
                copies.append(remote(pk.at[a, b, d], pr.at[a, b, d, pl.ds(2 * d, 2)],
                                     s1.at[a, b, 4 + d], r1.at[a, b, 4 + d], to[d]))
                copies[-1].start()

    def plane_sum(b, copies):
        end(copies[4:])
        @pl.loop(0, 16)
        def _(i):
            q, rows = i // 4, pl.ds(pl.multiple_of(lax.rem(i, 4) * CH, 8), CH)
            for a, g, me, _ in axes:
                ps[a, b, q, rows, :] = g[b, me * 4 + q, rows, :] + (pr[a, b, 0, q, rows, :] + pr[a, b, 1, q, rows, :])

    def cross(b):
        copies = []
        for k in range(3):
            copies.append(remote(ps.at[0, b, lax.rem(y + k + 1, 4)], rx2.at[b, k], s2.at[b, k], r2.at[b, k], ys[k]))
            copies.append(remote(ps.at[1, b, lax.rem(x + k + 1, 4)], ry2.at[b, k],
                                 s2.at[b, 3 + k], r2.at[b, 3 + k], xs[k]))
        return begin(copies)

    def cross_sum(b):
        @pl.loop(0, 4)
        def _(i):
            rows = pl.ds(pl.multiple_of(i * CH, 8), CH)
            st[b, i] = (ps[0, b, y, rows, :] + rx2[b, 0, rows, :]) + (rx2[b, 1, rows, :] + rx2[b, 2, rows, :])
            st[b, 4 + i] = (ps[1, b, x, rows, :] + ry2[b, 0, rows, :]) + (ry2[b, 1, rows, :] + ry2[b, 2, rows, :])

    def along(b):
        return begin([remote(st.at[b, lax.rem(z + k + 1, 8)], rz.at[b, k], s3.at[b, k], r3.at[b, k], zs[k])
                      for k in range(7)])

    def along_sum(b):
        total = st[b, z]
        for k in range(7):
            total += rz[b, k]
        fin[b] = total

    def spread(b):
        for i in range(6):
            if i < 4:
                to = unit_zh * 4 + i
                src, dst, rsem = fin.at[b, pl.ds(0, GROWS)], ga.at[b, z], rg4.at[b, z]
            else:
                to = (i - 4) * 4 + unit_zl
                src, dst, rsem = fin.at[b, pl.ds(GROWS, AROWS)], aa.at[b, z], ra4.at[b, z]

            @pl.when(to == z)
            def _():
                pltpu.make_async_copy(src, dst, rsem).start()

            @pl.when(to != z)
            def _():
                remote(src, dst, s4.at[b, i], rsem, at(x, y, to, core)).start()

    def spread_sent(b):
        for i in range(6):
            to = unit_zh * 4 + i if i < 4 else (i - 4) * 4 + unit_zl
            src = fin.at[b, pl.ds(0, GROWS)] if i < 4 else fin.at[b, pl.ds(GROWS, AROWS)]
            dst, rsem = (ga.at[b, z], rg4.at[b, z]) if i < 4 else (aa.at[b, z], ra4.at[b, z])

            @pl.when(to != z)
            def _():
                remote(src, dst, s4.at[b, i], rsem, at(x, y, to, core)).wait_send()

    def parts(b):
        return ((g_on, ga.at[b], xs, fg.at[g_part, b], rg5.at[b, g_part], 0),
                (a_on, aa.at[b], ys + across, fa.at[a_part, b], ra5.at[b, a_part], 3))

    def give(b):
        for on, src, to, dst, rsem, first in parts(b):
            @pl.when(on)
            def _():
                for i in range(8):
                    piece = fin.at[b, pl.ds(0, GROWS)] if first == 0 else fin.at[b, pl.ds(GROWS, AROWS)]
                    arrive = (rg4 if first == 0 else ra4).at[b, i]
                    pltpu.make_async_copy(piece, src.at[i], arrive).wait()
                for i, device in enumerate(to):
                    remote(src, dst, s5.at[b, first + i], rsem, device).start()
                pltpu.make_async_copy(src, dst, rsem).start()

    def given(b):
        for on, src, to, dst, rsem, first in parts(b):
            @pl.when(on)
            def _():
                for i, device in enumerate(to):
                    remote(src, dst, s5.at[b, first + i], rsem, device).wait_send()

    def taken(b):
        for i in range(2):
            pltpu.make_async_copy(ga.at[b], fg.at[i, b], rg5.at[b, i]).wait()
            pltpu.make_async_copy(aa.at[b], fa.at[i, b], ra5.at[b, i]).wait()

    batches = range(NB)
    q = begin([remote(tr, q1.at[k], ts.at[k], tr_sem.at[k], xs[k]) for k in range(3)])
    first, second, third = {}, {}, {}
    first[0] = plane(0)
    plane_pass(0, first[0])
    first[1] = plane(1)
    plane_sum(0, first[0])
    second[0] = cross(0)
    end(q)
    t1[...] = (tr[...] + q1[0]) + (q1[1] + q1[2])
    q = begin([remote(t1, q2.at[k], ts.at[3 + k], tr_sem.at[3 + k], ys[k]) for k in range(3)])
    plane_pass(1, first[1])
    end(second[0])
    cross_sum(0)
    third[0] = along(0)
    end(q)
    t2[...] = (t1[...] + q2[0]) + (q2[1] + q2[2])
    q = begin([remote(t2, q3.at[k], ts.at[6 + k], tr_sem.at[6 + k], zs[k]) for k in range(7)])
    plane_sum(1, first[1])
    second[1] = cross(1)
    end(third[0])
    along_sum(0)
    spread(0)
    end(q)
    trace = t2[...]
    for k in range(7):
        trace += q3[k]
    t3[...] = trace
    q = begin([remote(t3, q4, ts.at[13], tr_sem.at[13], (sib, own))])
    end(second[1])
    cross_sum(1)
    third[1] = along(1)
    give(0)
    end(third[1])
    along_sum(1)
    spread(1)
    give(1)
    end(q)
    tt[core] = t3[...]
    tt[1 - core] = q4[...]
    t_out[0:8, :] = tt[0, 0:8, :] + tt[1, 0:8, :]
    t_out[8:16, :] = jnp.broadcast_to(tt[own // 8, pl.ds(8 + lax.rem(own, 8), 1), :], (8, 128))
    for b in batches:
        taken(b)
    for b in batches:
        spread_sent(b)
        given(b)


def reduce_all(acts, grads):
    rows = acts.shape[0]
    vmem = pl.BlockSpec(memory_space=pltpu.VMEM)
    dma = pltpu.SemaphoreType.DMA
    tile = pltpu.VMEM((16, 128), F32)

    def buf(*shape):
        return pltpu.VMEM(shape + (128,), F32)

    return pl.pallas_call(
        reduce_kernel,
        out_shape=(jax.ShapeDtypeStruct((2, NB, 8, GROWS, 128), F32),
                   jax.ShapeDtypeStruct((2, NB, 8, AROWS, 128), F32),
                   jax.ShapeDtypeStruct((16, 128), F32)),
        in_specs=[pl.BlockSpec(memory_space=pl.ANY)] * 2,
        out_specs=(vmem,) * 3,
        scratch_shapes=[
            pltpu.VMEM((2 * rows, D // 2), acts.dtype), pltpu.VMEM((2 * rows, 8 * WIN), acts.dtype),
            pltpu.VMEM((16, 2 * rows, 384), acts.dtype),
            buf(NB, 16, HALF), buf(NB, 16, HALF), tile,
            buf(2, NB, 4, HALF), buf(2, NB, 2, 2, HALF), buf(2, NB, 2, 2, HALF), buf(2, NB, 2, 4, HALF),
            buf(NB, 3, HALF), buf(NB, 3, HALF), buf(NB, 8, CH), buf(NB, 7, CH), buf(NB, CH),
            buf(NB, 8, GROWS), buf(NB, 8, AROWS),
            tile, tile, tile, buf(3, 16), buf(3, 16), buf(7, 16), tile, buf(2, 16),
            dma((3, 4)), dma((3, 4)), dma((3, 4)), dma((2, NB, 6)), dma((2, NB, 6)), dma((NB, 6)), dma((NB, 6)), dma((NB, 7)), dma((NB, 7)),
            dma((NB, 6)), dma((NB, 8)), dma((NB, 8)), dma((NB, 10)), dma((NB, 2)), dma((NB, 2)), dma((14,)), dma((14,)),
        ],
        compiler_params=pltpu.CompilerParams(collective_id=1, has_side_effects=True, vmem_limit_bytes=VLIM),
        name="reduce_all",
    )(acts, grads)


def split(v):
    high = v.astype(jnp.bfloat16).astype(F32)
    rest = v - high
    mid = rest.astype(jnp.bfloat16).astype(F32)
    return high, mid, rest - mid


def dot(a, b, ca=1, cb=0):
    ah, am, al = split(a)
    bh, bm, bl = split(b)
    left = jnp.concatenate([ah, ah, am, ah, am, al], axis=ca).astype(jnp.bfloat16)
    right = jnp.concatenate([bh, bm, bh, bl, bm, bh], axis=cb).astype(jnp.bfloat16)
    return lax.dot_general(left, right, (((ca,), (cb,)), ((), ())), preferred_element_type=F32)


def sweep_four(now, at, row, sub, lane):
    def full(v):
        return jnp.broadcast_to(v, (8, 128))

    four = range(4)
    cols = [full(now[:, at + i:at + i + 1]) for i in four]
    rows = [full(now[row + i:row + i + 1, :]) for i in four]
    m = {(i, j): full(cols[j][row + i:row + i + 1, :]) for i in four for j in range(i + 1)}
    for p in four:
        inv = 1.0 / m[(p, p)]
        line = {i: m[(max(i, p), min(i, p))] * inv for i in four if i != p}
        new = {}
        for i in four:
            for j in range(i + 1):
                if i == p and j == p:
                    new[(i, j)] = -inv
                elif i == p:
                    new[(i, j)] = line[j]
                elif j == p:
                    new[(i, j)] = line[i]
                else:
                    new[(i, j)] = m[(i, j)] - m[(max(i, p), min(i, p))] * line[j]
        m = new
    in_rows = jnp.logical_and(sub >= row, sub < row + 4)
    in_cols = jnp.logical_and(lane >= at, lane < at + 4)
    out = jnp.where(jnp.logical_or(in_rows, in_cols), 0.0, now)
    rows = [jnp.where(in_cols, jnp.where(lane == at + i, -1.0, 0.0), rows[i]) for i in four]
    for i in four:
        col = jnp.where(in_rows, jnp.where(sub == row + i, -1.0, 0.0), cols[i])
        term = m[(i, 0)] * rows[0]
        for j in range(1, 4):
            term = term + m[(max(i, j), min(i, j))] * rows[j]
        out = out + col * term
    return out


def sweep_tiles(refs, panels, others=()):
    others = list(others)
    sub = lax.broadcasted_iota(jnp.int32, (8, 128), 0)
    lane = lax.broadcasted_iota(jnp.int32, (8, 128), 1)
    lane_all = lax.broadcasted_iota(jnp.int32, (128, 128), 1)
    for p in range(panels):
        base = 8 * p
        inside = jnp.logical_and(lane_all >= base, lane_all < base + 8)
        olds = [ref[base:base + 8, :] for ref in refs]
        news = [sweep_four(old, base, 0, sub, lane) for old in olds]
        news = [sweep_four(new, base + 4, 4, sub, lane) for new in news]
        for ref, old, new in zip(refs, olds, news):
            ref[...] = jnp.where(inside, 0.0, ref[...]) - dot(old, new, 0, 0)
            ref[base:base + 8, :] = new
        count = -(-len(others) // (panels - p))
        for step in others[:count]:
            step()
        others = others[count:]


def solve_kernel(fg_ref, fa_ref, t_ref, w_ref, p_ref, g_ref, a_ref, l_ref, x_ref, ai_ref):
    act_trace = jnp.sum(t_ref[0:1, :], keepdims=True) / TOKENS
    grad_trace = jnp.sum(t_ref[1:2, :], keepdims=True) / TOKENS
    ratio = jnp.sqrt(act_trace / D / (grad_trace / FF))
    act_damp = ratio * DAMP
    grad_damp = DAMP / ratio
    r = lax.broadcasted_iota(jnp.int32, (128, 128), 0)
    c = lax.broadcasted_iota(jnp.int32, (128, 128), 1)
    last = GB - 256

    def pair(both, second):
        turned = both.T
        first = jnp.where(r >= c, both, turned)
        other = jnp.where(r < c, both, jnp.where(r == c, jnp.broadcast_to(second, (128, 128)), turned))
        return first, other

    def damped(tile, damp):
        return tile / TOKENS + jnp.where(r == c, damp, 0.0)

    zeros = jnp.zeros((128 - last, 128), F32)
    for b in range(2):
        first, second = pair(fg_ref[b, 128:256, :], fg_ref[b, 480:481, :])
        g_ref[b * 6] = damped(first, grad_damp)
        g_ref[b * 6 + 1] = fg_ref[b, 0:128, :] / TOKENS
        g_ref[b * 6 + 2] = damped(second, grad_damp)
        g_ref[b * 6 + 3] = jnp.concatenate([fg_ref[b, 256:344, :] / TOKENS, zeros], axis=0)
        g_ref[b * 6 + 4] = jnp.concatenate([fg_ref[b, 344:432, :] / TOKENS, zeros], axis=0)
        packed = fg_ref[b, 432:480, :]
        low = pltpu.roll(packed[0:40], 88, 1)
        upper = jnp.concatenate([packed, low, jnp.zeros((40, 128), F32)], axis=0)
        corner = jnp.where(jnp.logical_and(r >= 48, c < 48), upper.T, upper)
        inside = jnp.logical_and(r < last, c < last)
        g_ref[b * 6 + 5] = jnp.where(inside, damped(corner, grad_damp), jnp.where(r == c, 1.0, 0.0))
    first, second = pair(fa_ref[128:256, :], t_ref[8:9, :])
    a_ref[0] = damped(first, act_damp)
    a_ref[1] = fa_ref[0:128, :] / TOKENS
    a_ref[2] = damped(second, act_damp)
    gs = [[g_ref.at[b * 6 + t] for t in range(6)] for b in range(2)]
    am = [a_ref.at[t] for t in range(3)]
    sweep_tiles([gs[0][0], gs[1][0], am[0]], 16)
    for m in gs + [am]:
        a10 = m[1][...]
        l10 = -dot(a10, m[0][...])
        m[2][...] -= dot(l10, a10, 1, 1)
        l_ref[0 if m is gs[0] else 1 if m is gs[1] else 2] = l10

    def row_two(b):
        m = gs[b]
        a20 = m[3][...]

        def lower():
            l_ref[3 + b] = -dot(a20, m[0][...])

        def side():
            m[4][...] -= dot(l_ref[3 + b], m[1][...], 1, 1)

        def corner():
            m[5][...] -= dot(l_ref[3 + b], a20, 1, 1)
        return [lower, side, corner]

    steps = [step for pair_of in zip(row_two(0), row_two(1)) for step in pair_of]
    sweep_tiles([gs[0][2], gs[1][2], am[2]], 16, steps)
    for b, m in enumerate(gs):
        a21 = m[4][...]
        l21 = -dot(a21, m[2][...])
        m[5][...] -= dot(l21, a21, 1, 1)
        l_ref[5 + b] = l21

    def act_cross():
        v10 = -dot(am[2][...], l_ref[2])
        ai_ref[128:256, 0:128] = -v10
        ai_ref[0:128, 128:256] = -v10.T
        ai_ref[128:256, 128:256] = -am[2][...]

    def act_first():
        ai_ref[0:128, 0:128] = -am[0][...] - dot(l_ref[2], ai_ref[128:256, 0:128], 0, 0)

    def right_side(b):
        w = w_ref[...].astype(F32)[b * GB:(b + 1) * GB]
        w = jnp.concatenate([w, jnp.zeros((384 - GB, 256), F32)], axis=0).astype(jnp.bfloat16)
        pieces = jnp.concatenate(split(ai_ref[...]), axis=0).astype(jnp.bfloat16)
        x_ref[b] = jnp.dot(jnp.concatenate([w, w, w], axis=1), pieces, preferred_element_type=F32)

    def through(b):
        x = [x_ref.at[b, pl.ds(128 * i, 128)] for i in range(3)]
        l10, l20, l21 = l_ref.at[b], l_ref.at[3 + b], l_ref.at[5 + b]
        m = gs[b]

        def one():
            x[1][...] -= dot(l10[...], x[0][...])

        def two():
            x[2][...] -= dot(l20[...], x[0][...])

        def three():
            x[2][...] -= dot(l21[...], x[1][...])

        def four():
            x[1][...] = -dot(m[2][...], x[1][...])

        def five():
            x[0][...] = -dot(m[0][...], x[0][...])

        def six():
            x[0][...] -= dot(l10[...], x[1][...], 0, 0)

        def seven():
            l20[...] -= dot(l21[...], l10[...])
        return [one, two, three, four, five, six, seven]

    steps = [act_cross, act_first, lambda: right_side(0), lambda: right_side(1)]
    steps += [step for pair_of in zip(through(0), through(1)) for step in pair_of]
    sweep_tiles([gs[0][5], gs[1][5]], last // 8, steps)
    out = []
    for b, m in enumerate(gs):
        y2 = -dot(m[5][...], x_ref[b, 256:384])
        out += [x_ref[b, 0:128] - dot(l_ref[3 + b], y2, 0, 0),
                x_ref[b, 128:256] - dot(l_ref[5 + b], y2, 0, 0), y2[0:last]]
    p_ref[...] = jnp.concatenate(out, axis=0).astype(jnp.bfloat16)


def solve(fg, fa, tr, w):
    vmem = pl.BlockSpec(memory_space=pltpu.VMEM)
    return pl.pallas_call(
        solve_kernel,
        out_shape=jax.ShapeDtypeStruct((2 * GB, 256), jnp.bfloat16),
        in_specs=[vmem] * 4,
        out_specs=vmem,
        scratch_shapes=[pltpu.VMEM((12, 128, 128), F32), pltpu.VMEM((3, 128, 128), F32),
                        pltpu.VMEM((7, 128, 128), F32), pltpu.VMEM((2, 384, 256), F32),
                        pltpu.VMEM((256, 256), F32)],
        compiler_params=pltpu.CompilerParams(vmem_limit_bytes=VLIM),
        name="solve",
    )(fg, fa, tr, w)


def gather_kernel(p_ref, o_ref, local, sz, rz, sy, ry, sh, rh, sc, rc):
    dp, own = place()
    core = lax.rem(dp, 2)
    y = dp // 4
    sib = dp + 1 - 2 * core
    zh = lax.rem(dp // 2, 2)
    anti = dp + 2 - 4 * zh
    up = lax.rem(y + 1, 4) * 4 + lax.rem(dp, 4)
    down = lax.rem(y + 3, 4) * 4 + lax.rem(dp, 4)
    barrier = pltpu.get_barrier_semaphore()
    for device in (sib, anti, up, down):
        pl.semaphore_signal(barrier, inc=1, device_id=(device, own), device_id_type=MESH)
    pl.semaphore_wait(barrier, 4)

    def other(d):
        return d + 2 - 4 * lax.rem(d // 2, 2)

    far = lax.rem(y + 2, 4) * 4 + lax.rem(dp, 4)
    waits = []

    def half(ref, h):
        return ref.at[pl.ds(h * CUT[0], CUT[h])]

    def send(d, h, sems, i, device, src=None):
        src = o_ref.at[d] if src is None else src
        copy = pltpu.make_async_remote_copy(
            src_ref=half(src, h), dst_ref=half(o_ref.at[d], h), send_sem=sems[0].at[i], recv_sem=sems[1].at[i],
            device_id=(device, own), device_id_type=MESH)
        copy.start()
        waits.append(copy)

    def arrived(d, h, sems, i):
        dst = half(o_ref.at[d], h)
        pltpu.make_async_remote_copy(src_ref=dst, dst_ref=dst, send_sem=sems[0].at[i], recv_sem=sems[1].at[i],
                                     device_id=(sib, own), device_id_type=MESH).wait_recv()

    zsem, ysem, hsem, csem = (sz, rz), (sy, ry), (sh, rh), (sc, rc)
    for h in range(2):
        send(dp, h, zsem, h, anti, p_ref)
        send(dp, h, ysem, h, up, p_ref)
        send(dp, 1 - h, ysem, 3 - h, down, p_ref)
    for h in range(2):
        send(dp, h, csem, h, sib, p_ref)
    keep = pltpu.make_async_copy(p_ref, o_ref.at[dp], local)
    keep.start()
    arrived(down, 0, ysem, 0)
    send(down, 0, hsem, 0, up)
    arrived(up, 1, ysem, 3)
    send(up, 1, hsem, 1, down)
    send(down, 0, csem, 2, sib)
    send(up, 1, csem, 5, sib)
    arrived(down, 1, ysem, 1)
    send(down, 1, csem, 3, sib)
    arrived(up, 0, ysem, 2)
    send(up, 0, csem, 4, sib)
    arrived(anti, 0, zsem, 0)
    send(anti, 0, ysem, 4, up)
    send(anti, 0, ysem, 6, down)
    send(anti, 0, csem, 6, sib)
    arrived(far, 0, hsem, 0)
    send(far, 0, csem, 8, sib)
    arrived(far, 1, hsem, 1)
    send(far, 1, csem, 9, sib)
    arrived(anti, 1, zsem, 1)
    send(anti, 1, ysem, 5, up)
    send(anti, 1, ysem, 7, down)
    send(anti, 1, csem, 7, sib)
    arrived(other(down), 0, ysem, 4)
    send(other(down), 0, hsem, 2, up)
    send(other(down), 0, csem, 10, sib)
    arrived(other(up), 0, ysem, 6)
    send(other(up), 0, csem, 12, sib)
    arrived(other(up), 1, ysem, 7)
    send(other(up), 1, hsem, 3, down)
    send(other(up), 1, csem, 13, sib)
    arrived(other(down), 1, ysem, 5)
    send(other(down), 1, csem, 11, sib)
    arrived(other(far), 0, hsem, 2)
    send(other(far), 0, csem, 14, sib)
    arrived(other(far), 1, hsem, 3)
    send(other(far), 1, csem, 15, sib)

    def twin(d):
        return d + 1 - 2 * lax.rem(d, 2)

    for i, d in enumerate((dp, down, up, anti, far, other(down), other(up), other(far))):
        for h in range(2):
            arrived(twin(d), h, csem, 2 * i + h)
    keep.wait()
    for copy in waits:
        copy.wait_send()


def gather(p):
    dma = pltpu.SemaphoreType.DMA
    return pl.pallas_call(
        gather_kernel,
        out_shape=jax.ShapeDtypeStruct((16, 2 * GB, 256), jnp.bfloat16),
        in_specs=[pl.BlockSpec(memory_space=pl.ANY)],
        out_specs=pl.BlockSpec(memory_space=pl.ANY),
        scratch_shapes=[dma, dma((2,)), dma((2,)), dma((8,)), dma((8,)), dma((4,)), dma((4,)), dma((16,)), dma((16,))],
        compiler_params=pltpu.CompilerParams(collective_id=2, has_side_effects=True),
        name="gather",
    )(p)


def turn_kernel(i_ref, o_ref):
    for k in range(i_ref.shape[0] // 128):
        o_ref[:, k * 128:(k + 1) * 128] = i_ref[k * 128:(k + 1) * 128, :].T


def turn(slices):
    step = FF // 2
    return pl.pallas_call(
        turn_kernel,
        out_shape=jax.ShapeDtypeStruct((256, FF), jnp.bfloat16),
        grid=(2, 2),
        in_specs=[pl.BlockSpec((step, 128), lambda i, j: (j, i))],
        out_specs=pl.BlockSpec((128, step), lambda i, j: (i, j)),
        compiler_params=pltpu.CompilerParams(vmem_limit_bytes=VLIM),
        name="turn",
    )(slices)


def shards(acts, grads_out, weight_grad):
    fg, fa, tr = reduce_all(acts, grads_out)
    p = solve(fg.reshape(2, 512, 128), fa.reshape(256, 128), tr, weight_grad.T)
    return turn(gather(p).reshape(FF, 256))


def solution(mesh):
    in_specs = (P(("dp", "owner"), None), P(("dp", "owner"), None), P("owner", "dp"))
    out_specs = P("owner", None)
    return jax.shard_map(shards, mesh=mesh, in_specs=in_specs, out_specs=out_specs, check_vma=False)
```

```python
import functools
import math

import jax
import jax.numpy as jnp
from jax import lax
from jax.experimental import pallas as pl
from jax.experimental.pallas import tpu as pltpu
from jax.sharding import PartitionSpec as P

D = 4096
FF = 11008
AB = 256
GB = 344
TOKENS = 57344
DAMP = math.sqrt(0.03)
MESH = pl.DeviceIdType.MESH
F32 = jnp.float32
NB = 2
GROWS = 64 // NB
AROWS = 16 // NB
CH = GROWS + AROWS
HALF = 4 * CH
VLIM = 56 * 1024 * 1024
WIN = 7 * 128
WIDTHS = [WIN] * 7 + [WIN - 128]
CUT = (352, 336)


def grad_position(p, part, core):
    y = p // 2
    return 2 * part + (p + y + core) % 2, y


def act_position(k, part):
    return k % 4, 2 * part + k // 4


def window(d):
    return 128 * (43 * d // 8)


def place():
    dp = lax.axis_index("dp")
    own = lax.axis_index("owner")
    return dp, own


def gram(block):
    return lax.dot_general(block, block, (((0,), (0,)), ((), ())), preferred_element_type=F32)


def fetch(a_ref, g_ref, abuf, gbuf, core, sibling, sems, send, recv):
    rows = a_ref.shape[0]
    mine, theirs = pl.ds(0, rows), pl.ds(rows, rows)
    width = abuf.shape[1]

    def half(c):
        return a_ref.at[:, pl.ds(pl.multiple_of(c * width, 128), width)]

    def columns(p, c):
        return g_ref.at[:, pl.ds(pl.multiple_of(window(2 * p + c), 128), WIDTHS[p])]

    here = [[(half(core), abuf.at[mine])], [], []]
    away = [[(half(1 - core), abuf.at[theirs])], [], []]
    for p in range(8):
        at = pl.ds(p * WIN, WIDTHS[p])
        here[1 + p // 4].append((columns(p, core), gbuf.at[mine, at]))
        away[1 + p // 4].append((columns(p, 1 - core), gbuf.at[theirs, at]))
    here = [[pltpu.make_async_copy(src, dst, sems.at[i, n]) for n, (src, dst) in enumerate(group)]
            for i, group in enumerate(here)]
    away = [[pltpu.make_async_remote_copy(src_ref=src, dst_ref=dst, send_sem=send.at[i, n], recv_sem=recv.at[i, n],
                                          device_id=sibling, device_id_type=MESH)
             for n, (src, dst) in enumerate(group)] for i, group in enumerate(away)]
    for group in here:
        for copy in group:
            copy.start()
    return here, away


def gram_step(copies, core, abuf, gbuf, even, x_ref, y_ref, t_ref):
    def store_all(where, size, lead, row, value):
        px, py = where
        done = 0
        while done < value.shape[0]:
            at = row + done
            n = min(size - at % size, value.shape[0] - done)
            batch, chunk = at // size // 8, at // size % 8
            rows_at = pl.ds(chunk % 4 * CH + lead + at % size, n)
            if chunk < 4:
                x_ref[batch, px * 4 + py, rows_at, :] = value[done:done + n]
            else:
                y_ref[batch, py * 4 + px, rows_at, :] = value[done:done + n]
            done += n

    r = lax.broadcasted_iota(jnp.int32, (128, 128), 0)
    c = lax.broadcasted_iota(jnp.int32, (128, 128), 1)

    def diag(tile):
        return jnp.sum(jnp.where(r == c, tile, 0.0), axis=0, keepdims=True)

    act_sum = jnp.zeros((1, 128), F32)
    grad_sum = jnp.zeros((1, 128), F32)
    for copy in copies[0]:
        copy.wait()
    for k in range(8):
        g = gram(abuf[:, k * AB:(k + 1) * AB])
        t0, t2 = g[0:128, 0:128], g[128:256, 128:256]
        second = diag(t2)
        act_sum += diag(t0) + second
        t_ref[8 + k:9 + k, :] = second
        store_all(act_position(k, 0), AROWS, GROWS, 0, g[128:256, 0:128])
        store_all(act_position(k, 1), AROWS, GROWS, 0, jnp.where(r >= c, t0, t2))
    for j in range(16):
        if j in (0, 8):
            for copy in copies[1 + j // 8]:
                copy.wait()
            for odd in range(2):
                @pl.when(core == odd)
                def _():
                    for i in range(j, j + 8):
                        d = i // 2 * 2 + odd
                        start = i // 2 * WIN + 2 * GB * d - window(d) + i % 2 * GB
                        even[i, :, 0:GB] = gbuf[:, start:start + GB]
        g = gram(even[j, :, 0:256])
        t0, t2 = g[0:128, 0:128], g[128:256, 128:256]
        second = diag(t2)
        grad_sum += diag(t0) + second
        where = grad_position(j // 2, j % 2, core)
        store_all(where, GROWS, 0, 0, g[128:256, 0:128])
        store_all(where, GROWS, 0, 128, jnp.where(r >= c, t0, t2))
        store_all(where, GROWS, 0, 480, jnp.concatenate([second, jnp.zeros((31, 128), F32)], axis=0))

    def rest():
        corner_sum = grad_sum
        for j in range(16):
            low = lax.dot_general(even[j, :, 256:GB], even[j, :, 0:GB], (((0,), (0,)), ((), ())),
                                  preferred_element_type=F32)
            t5 = jnp.concatenate([low[:, 256:GB], jnp.zeros((88, 40), F32)], axis=1)
            corner_sum += jnp.sum(jnp.where(r[:88] == c[:88], t5, 0.0), axis=0, keepdims=True)
            tail = jnp.concatenate([pltpu.roll(t5[48:88], 40, 1), jnp.zeros((8, 128), F32)], axis=0)
            where = grad_position(j // 2, j % 2, core)
            store_all(where, GROWS, 0, 256, low[:, 0:128])
            store_all(where, GROWS, 0, 344, low[:, 128:256])
            store_all(where, GROWS, 0, 432, jnp.where(c[:48] < 88, t5[0:48], tail))
        t_ref[0:8, :] = jnp.concatenate([act_sum, corner_sum, jnp.zeros((6, 128), F32)], axis=0)

    return rest


def reduce_kernel(a_ref, g_ref, fg, fa, t_out,
                  abuf, gbuf, even, gx, gy, tr, ps, pk, pm, pr, rx2, ry2, st, rz, fin, ga, aa, t1, t2, t3, q1, q2, q3, q4, tt,
                  local, s0, r0, s1, r1, s2, r2, s3, r3, s4, rg4, ra4, s5, rg5, ra5, ts, tr_sem):
    dp, own = place()
    core = lax.rem(dp, 2)
    zh = lax.rem(dp // 2, 2)
    y = dp // 4
    x = lax.rem(own, 4)
    zl = own // 4
    z = zh * 4 + zl
    sib = dp + 1 - 2 * core

    def at(ax, ay, az, ac):
        return ((ay * 2 + az // 4) * 2 + ac, lax.rem(az, 4) * 4 + ax)

    xs = [at(lax.rem(x + k, 4), y, z, core) for k in (1, 2, 3)]
    ys = [at(x, lax.rem(y + k, 4), z, core) for k in (1, 2, 3)]
    zs = [at(x, y, lax.rem(z + k, 8), core) for k in range(1, 8)]
    g_part, a_part = x // 2, y // 2
    unit_zh = lax.rem(x + y + core, 2)
    unit_zl = 2 * core + lax.rem(y, 2)
    g_on = zh == unit_zh
    a_on = zl == unit_zl
    across = [at(x, lax.rem(y + k, 4), z, 1 - core) for k in range(4)]

    here, away = fetch(a_ref, g_ref, abuf, gbuf, core, (sib, own), local, s0, r0)
    barrier = pltpu.get_barrier_semaphore()
    for device in xs + ys + zs + across:
        pl.semaphore_signal(barrier, inc=1, device_id=device, device_id_type=MESH)
    pl.semaphore_wait(barrier, 17)
    for group in away:
        for copy in group:
            copy.start()
    rest = gram_step([h + a for h, a in zip(here, away)], core, abuf, gbuf, even, gx, gy, tr)

    def remote(src, dst, ssem, rsem, device):
        return pltpu.make_async_remote_copy(src_ref=src, dst_ref=dst, send_sem=ssem, recv_sem=rsem,
                                            device_id=device, device_id_type=MESH)

    def begin(copies):
        for copy in copies:
            copy.start()
        return copies

    def end(copies):
        for copy in copies:
            copy.wait()

    axes = ((0, gx, x, (xs[0], xs[2])), (1, gy, y, (ys[0], ys[2])))

    def plane(b):
        copies = []
        for a, g, me, (up, down) in axes:
            opposite = lax.rem(me + 2, 4) * 4
            copies.append(remote(g.at[b, pl.ds(opposite, 2)], pm.at[a, b, 0], s1.at[a, b, 0], r1.at[a, b, 0], up))
            copies.append(remote(g.at[b, pl.ds(opposite + 2, 2)], pm.at[a, b, 1],
                                 s1.at[a, b, 1], r1.at[a, b, 1], down))
        for a, g, me, (up, down) in axes:
            over, under = lax.rem(me + 1, 4) * 4, lax.rem(me + 3, 4) * 4
            copies.append(remote(g.at[b, pl.ds(over + 2, 2)], pr.at[a, b, 0, pl.ds(2, 2)],
                                 s1.at[a, b, 2], r1.at[a, b, 2], up))
            copies.append(remote(g.at[b, pl.ds(under, 2)], pr.at[a, b, 1, pl.ds(0, 2)],
                                 s1.at[a, b, 3], r1.at[a, b, 3], down))
        return begin(copies)

    def plane_pass(b, copies):
        end(copies[:4])
        @pl.loop(0, 8)
        def _(i):
            h, rows = i // 4, pl.ds(pl.multiple_of(lax.rem(i, 4) * CH, 8), CH)
            for a, g, me, _ in axes:
                over, under = lax.rem(me + 1, 4) * 4, lax.rem(me + 3, 4) * 4
                pk[a, b, 0, h, rows, :] = g[b, over + h, rows, :] + pm[a, b, 0, h, rows, :]
                pk[a, b, 1, h, rows, :] = g[b, under + 2 + h, rows, :] + pm[a, b, 1, h, rows, :]
        for a, _, _, to in axes:
            for d in range(2):
                copies.append(remote(pk.at[a, b, d], pr.at[a, b, d, pl.ds(2 * d, 2)],
                                     s1.at[a, b, 4 + d], r1.at[a, b, 4 + d], to[d]))
                copies[-1].start()

    def plane_sum(b, copies):
        end(copies[4:])
        @pl.loop(0, 16)
        def _(i):
            q, rows = i // 4, pl.ds(pl.multiple_of(lax.rem(i, 4) * CH, 8), CH)
            for a, g, me, _ in axes:
                ps[a, b, q, rows, :] = g[b, me * 4 + q, rows, :] + (pr[a, b, 0, q, rows, :] + pr[a, b, 1, q, rows, :])

    def cross(b):
        copies = []
        for k in range(3):
            copies.append(remote(ps.at[0, b, lax.rem(y + k + 1, 4)], rx2.at[b, k], s2.at[b, k], r2.at[b, k], ys[k]))
            copies.append(remote(ps.at[1, b, lax.rem(x + k + 1, 4)], ry2.at[b, k],
                                 s2.at[b, 3 + k], r2.at[b, 3 + k], xs[k]))
        return begin(copies)

    def cross_sum(b):
        @pl.loop(0, 4)
        def _(i):
            rows = pl.ds(pl.multiple_of(i * CH, 8), CH)
            st[b, i] = (ps[0, b, y, rows, :] + rx2[b, 0, rows, :]) + (rx2[b, 1, rows, :] + rx2[b, 2, rows, :])
            st[b, 4 + i] = (ps[1, b, x, rows, :] + ry2[b, 0, rows, :]) + (ry2[b, 1, rows, :] + ry2[b, 2, rows, :])

    def along(b):
        return begin([remote(st.at[b, lax.rem(z + k + 1, 8)], rz.at[b, k], s3.at[b, k], r3.at[b, k], zs[k])
                      for k in range(7)])

    def along_sum(b):
        total = st[b, z]
        for k in range(7):
            total += rz[b, k]
        fin[b] = total

    def spread(b):
        for i in range(6):
            if i < 4:
                to = unit_zh * 4 + i
                src, dst, rsem = fin.at[b, pl.ds(0, GROWS)], ga.at[b, z], rg4.at[b, z]
            else:
                to = (i - 4) * 4 + unit_zl
                src, dst, rsem = fin.at[b, pl.ds(GROWS, AROWS)], aa.at[b, z], ra4.at[b, z]

            @pl.when(to == z)
            def _():
                pltpu.make_async_copy(src, dst, rsem).start()

            @pl.when(to != z)
            def _():
                remote(src, dst, s4.at[b, i], rsem, at(x, y, to, core)).start()

    def spread_sent(b):
        for i in range(6):
            to = unit_zh * 4 + i if i < 4 else (i - 4) * 4 + unit_zl
            src = fin.at[b, pl.ds(0, GROWS)] if i < 4 else fin.at[b, pl.ds(GROWS, AROWS)]
            dst, rsem = (ga.at[b, z], rg4.at[b, z]) if i < 4 else (aa.at[b, z], ra4.at[b, z])

            @pl.when(to != z)
            def _():
                remote(src, dst, s4.at[b, i], rsem, at(x, y, to, core)).wait_send()

    def parts(b):
        return ((g_on, ga.at[b], xs, fg.at[g_part, b], rg5.at[b, g_part], 0),
                (a_on, aa.at[b], ys + across, fa.at[a_part, b], ra5.at[b, a_part], 3))

    def give(b):
        for on, src, to, dst, rsem, first in parts(b):
            @pl.when(on)
            def _():
                for i in range(8):
                    piece = fin.at[b, pl.ds(0, GROWS)] if first == 0 else fin.at[b, pl.ds(GROWS, AROWS)]
                    arrive = (rg4 if first == 0 else ra4).at[b, i]
                    pltpu.make_async_copy(piece, src.at[i], arrive).wait()
                for i, device in enumerate(to):
                    remote(src, dst, s5.at[b, first + i], rsem, device).start()
                pltpu.make_async_copy(src, dst, rsem).start()

    def given(b):
        for on, src, to, dst, rsem, first in parts(b):
            @pl.when(on)
            def _():
                for i, device in enumerate(to):
                    remote(src, dst, s5.at[b, first + i], rsem, device).wait_send()

    def taken(b):
        for i in range(2):
            pltpu.make_async_copy(ga.at[b], fg.at[i, b], rg5.at[b, i]).wait()
            pltpu.make_async_copy(aa.at[b], fa.at[i, b], ra5.at[b, i]).wait()

    batches = range(NB)
    first, second, third = {}, {}, {}
    first[0] = plane(0)
    rest()
    q = begin([remote(tr, q1.at[k], ts.at[k], tr_sem.at[k], xs[k]) for k in range(3)])
    plane_pass(0, first[0])
    first[1] = plane(1)
    plane_sum(0, first[0])
    second[0] = cross(0)
    end(q)
    t1[...] = (tr[...] + q1[0]) + (q1[1] + q1[2])
    q = begin([remote(t1, q2.at[k], ts.at[3 + k], tr_sem.at[3 + k], ys[k]) for k in range(3)])
    plane_pass(1, first[1])
    end(second[0])
    cross_sum(0)
    third[0] = along(0)
    end(q)
    t2[...] = (t1[...] + q2[0]) + (q2[1] + q2[2])
    q = begin([remote(t2, q3.at[k], ts.at[6 + k], tr_sem.at[6 + k], zs[k]) for k in range(7)])
    plane_sum(1, first[1])
    second[1] = cross(1)
    end(third[0])
    along_sum(0)
    spread(0)
    end(q)
    trace = t2[...]
    for k in range(7):
        trace += q3[k]
    t3[...] = trace
    q = begin([remote(t3, q4, ts.at[13], tr_sem.at[13], (sib, own))])
    end(second[1])
    cross_sum(1)
    third[1] = along(1)
    give(0)
    end(third[1])
    along_sum(1)
    spread(1)
    give(1)
    end(q)
    tt[core] = t3[...]
    tt[1 - core] = q4[...]
    t_out[0:8, :] = tt[0, 0:8, :] + tt[1, 0:8, :]
    t_out[8:16, :] = jnp.broadcast_to(tt[own // 8, pl.ds(8 + lax.rem(own, 8), 1), :], (8, 128))
    for b in batches:
        taken(b)
    for b in batches:
        spread_sent(b)
        given(b)


def reduce_all(acts, grads):
    rows = acts.shape[0]
    vmem = pl.BlockSpec(memory_space=pltpu.VMEM)
    dma = pltpu.SemaphoreType.DMA
    tile = pltpu.VMEM((16, 128), F32)

    def buf(*shape):
        return pltpu.VMEM(shape + (128,), F32)

    return pl.pallas_call(
        reduce_kernel,
        out_shape=(jax.ShapeDtypeStruct((2, NB, 8, GROWS, 128), F32),
                   jax.ShapeDtypeStruct((2, NB, 8, AROWS, 128), F32),
                   jax.ShapeDtypeStruct((16, 128), F32)),
        in_specs=[pl.BlockSpec(memory_space=pl.ANY)] * 2,
        out_specs=(vmem,) * 3,
        scratch_shapes=[
            pltpu.VMEM((2 * rows, D // 2), acts.dtype), pltpu.VMEM((2 * rows, 8 * WIN), acts.dtype),
            pltpu.VMEM((16, 2 * rows, 384), acts.dtype),
            buf(NB, 16, HALF), buf(NB, 16, HALF), tile,
            buf(2, NB, 4, HALF), buf(2, NB, 2, 2, HALF), buf(2, NB, 2, 2, HALF), buf(2, NB, 2, 4, HALF),
            buf(NB, 3, HALF), buf(NB, 3, HALF), buf(NB, 8, CH), buf(NB, 7, CH), buf(NB, CH),
            buf(NB, 8, GROWS), buf(NB, 8, AROWS),
            tile, tile, tile, buf(3, 16), buf(3, 16), buf(7, 16), tile, buf(2, 16),
            dma((3, 4)), dma((3, 4)), dma((3, 4)), dma((2, NB, 6)), dma((2, NB, 6)), dma((NB, 6)), dma((NB, 6)), dma((NB, 7)), dma((NB, 7)),
            dma((NB, 6)), dma((NB, 8)), dma((NB, 8)), dma((NB, 10)), dma((NB, 2)), dma((NB, 2)), dma((14,)), dma((14,)),
        ],
        compiler_params=pltpu.CompilerParams(collective_id=1, has_side_effects=True, vmem_limit_bytes=VLIM),
        name="reduce_all",
    )(acts, grads)


def split(v):
    high = v.astype(jnp.bfloat16).astype(F32)
    rest = v - high
    mid = rest.astype(jnp.bfloat16).astype(F32)
    return high, mid, rest - mid


def dot(a, b, ca=1, cb=0):
    ah, am, al = split(a)
    bh, bm, bl = split(b)
    left = jnp.concatenate([ah, ah, am, ah, am, al], axis=ca).astype(jnp.bfloat16)
    right = jnp.concatenate([bh, bm, bh, bl, bm, bh], axis=cb).astype(jnp.bfloat16)
    return lax.dot_general(left, right, (((ca,), (cb,)), ((), ())), preferred_element_type=F32)


def sweep_four(now, at, row, sub, lane):
    def full(v):
        return jnp.broadcast_to(v, (8, 128))

    four = range(4)
    cols = [full(now[:, at + i:at + i + 1]) for i in four]
    rows = [full(now[row + i:row + i + 1, :]) for i in four]
    m = {(i, j): full(cols[j][row + i:row + i + 1, :]) for i in four for j in range(i + 1)}
    for p in four:
        inv = 1.0 / m[(p, p)]
        line = {i: m[(max(i, p), min(i, p))] * inv for i in four if i != p}
        new = {}
        for i in four:
            for j in range(i + 1):
                if i == p and j == p:
                    new[(i, j)] = -inv
                elif i == p:
                    new[(i, j)] = line[j]
                elif j == p:
                    new[(i, j)] = line[i]
                else:
                    new[(i, j)] = m[(i, j)] - m[(max(i, p), min(i, p))] * line[j]
        m = new
    in_rows = jnp.logical_and(sub >= row, sub < row + 4)
    in_cols = jnp.logical_and(lane >= at, lane < at + 4)
    out = jnp.where(jnp.logical_or(in_rows, in_cols), 0.0, now)
    rows = [jnp.where(in_cols, jnp.where(lane == at + i, -1.0, 0.0), rows[i]) for i in four]
    terms = []
    for i in four:
        col = jnp.where(in_rows, jnp.where(sub == row + i, -1.0, 0.0), cols[i])
        t = [m[(max(i, j), min(i, j))] * rows[j] for j in four]
        terms.append(col * ((t[0] + t[1]) + (t[2] + t[3])))
    return (out + terms[0]) + (terms[1] + (terms[2] + terms[3]))


def sweep_tiles(refs, panels, others=()):
    others = list(others)
    sub = lax.broadcasted_iota(jnp.int32, (8, 128), 0)
    lane = lax.broadcasted_iota(jnp.int32, (8, 128), 1)
    lane_all = lax.broadcasted_iota(jnp.int32, (128, 128), 1)
    for p in range(panels):
        base = 8 * p
        inside = jnp.logical_and(lane_all >= base, lane_all < base + 8)
        olds = [ref[base:base + 8, :] for ref in refs]
        news = [sweep_four(old, base, 0, sub, lane) for old in olds]
        news = [sweep_four(new, base + 4, 4, sub, lane) for new in news]
        for ref, old, new in zip(refs, olds, news):
            ref[...] = jnp.where(inside, 0.0, ref[...]) - dot(old, new, 0, 0)
            ref[base:base + 8, :] = new
        count = -(-len(others) // (panels - p))
        for step in others[:count]:
            step()
        others = others[count:]


def solve_kernel(fg_ref, fa_ref, t_ref, w_ref, p_ref, g_ref, a_ref, l_ref, x_ref, ai_ref):
    act_trace = jnp.sum(t_ref[0:1, :], keepdims=True) / TOKENS
    grad_trace = jnp.sum(t_ref[1:2, :], keepdims=True) / TOKENS
    ratio = jnp.sqrt(act_trace / D / (grad_trace / FF))
    act_damp = ratio * DAMP
    grad_damp = DAMP / ratio
    r = lax.broadcasted_iota(jnp.int32, (128, 128), 0)
    c = lax.broadcasted_iota(jnp.int32, (128, 128), 1)
    last = GB - 256

    def pair(both, second):
        turned = both.T
        first = jnp.where(r >= c, both, turned)
        other = jnp.where(r < c, both, jnp.where(r == c, jnp.broadcast_to(second, (128, 128)), turned))
        return first, other

    def damped(tile, damp):
        return tile / TOKENS + jnp.where(r == c, damp, 0.0)

    zeros = jnp.zeros((128 - last, 128), F32)
    for b in range(2):
        first, second = pair(fg_ref[b, 128:256, :], fg_ref[b, 480:481, :])
        g_ref[b * 6] = damped(first, grad_damp)
        g_ref[b * 6 + 1] = fg_ref[b, 0:128, :] / TOKENS
        g_ref[b * 6 + 2] = damped(second, grad_damp)
        g_ref[b * 6 + 3] = jnp.concatenate([fg_ref[b, 256:344, :] / TOKENS, zeros], axis=0)
        g_ref[b * 6 + 4] = jnp.concatenate([fg_ref[b, 344:432, :] / TOKENS, zeros], axis=0)
        packed = fg_ref[b, 432:480, :]
        low = pltpu.roll(packed[0:40], 88, 1)
        upper = jnp.concatenate([packed, low, jnp.zeros((40, 128), F32)], axis=0)
        corner = jnp.where(jnp.logical_and(r >= 48, c < 48), upper.T, upper)
        inside = jnp.logical_and(r < last, c < last)
        g_ref[b * 6 + 5] = jnp.where(inside, damped(corner, grad_damp), jnp.where(r == c, 1.0, 0.0))
    first, second = pair(fa_ref[128:256, :], t_ref[8:9, :])
    a_ref[0] = damped(first, act_damp)
    a_ref[1] = fa_ref[0:128, :] / TOKENS
    a_ref[2] = damped(second, act_damp)
    gs = [[g_ref.at[b * 6 + t] for t in range(6)] for b in range(2)]
    am = [a_ref.at[t] for t in range(3)]
    sweep_tiles([gs[0][0], gs[1][0], am[0]], 16)
    for m in gs + [am]:
        a10 = m[1][...]
        l10 = -dot(a10, m[0][...])
        m[2][...] -= dot(l10, a10, 1, 1)
        l_ref[0 if m is gs[0] else 1 if m is gs[1] else 2] = l10

    def row_two(b):
        m = gs[b]
        a20 = m[3][...]

        def lower():
            l_ref[3 + b] = -dot(a20, m[0][...])

        def side():
            m[4][...] -= dot(l_ref[3 + b], m[1][...], 1, 1)

        def corner():
            m[5][...] -= dot(l_ref[3 + b], a20, 1, 1)
        return [lower, side, corner]

    steps = [step for pair_of in zip(row_two(0), row_two(1)) for step in pair_of]
    sweep_tiles([gs[0][2], gs[1][2], am[2]], 16, steps)
    for b, m in enumerate(gs):
        a21 = m[4][...]
        l21 = -dot(a21, m[2][...])
        m[5][...] -= dot(l21, a21, 1, 1)
        l_ref[5 + b] = l21

    def act_cross():
        v10 = -dot(am[2][...], l_ref[2])
        ai_ref[128:256, 0:128] = -v10
        ai_ref[0:128, 128:256] = -v10.T
        ai_ref[128:256, 128:256] = -am[2][...]

    def act_first():
        ai_ref[0:128, 0:128] = -am[0][...] - dot(l_ref[2], ai_ref[128:256, 0:128], 0, 0)

    def right_side(b):
        w = w_ref[...].astype(F32)[b * GB:(b + 1) * GB]
        w = jnp.concatenate([w, jnp.zeros((384 - GB, 256), F32)], axis=0).astype(jnp.bfloat16)
        pieces = jnp.concatenate(split(ai_ref[...]), axis=0).astype(jnp.bfloat16)
        x_ref[b] = jnp.dot(jnp.concatenate([w, w, w], axis=1), pieces, preferred_element_type=F32)

    def through(b):
        x = [x_ref.at[b, pl.ds(128 * i, 128)] for i in range(3)]
        l10, l20, l21 = l_ref.at[b], l_ref.at[3 + b], l_ref.at[5 + b]
        m = gs[b]

        def one():
            x[1][...] -= dot(l10[...], x[0][...])

        def two():
            x[2][...] -= dot(l20[...], x[0][...])

        def three():
            x[2][...] -= dot(l21[...], x[1][...])

        def four():
            x[1][...] = -dot(m[2][...], x[1][...])

        def five():
            x[0][...] = -dot(m[0][...], x[0][...])

        def six():
            x[0][...] -= dot(l10[...], x[1][...], 0, 0)

        def seven():
            l20[...] -= dot(l21[...], l10[...])
        return [one, two, three, four, five, six, seven]

    steps = [act_cross, act_first, lambda: right_side(0), lambda: right_side(1)]
    steps += [step for pair_of in zip(through(0), through(1)) for step in pair_of]
    sweep_tiles([gs[0][5], gs[1][5]], last // 8, steps)
    out = []
    for b, m in enumerate(gs):
        y2 = -dot(m[5][...], x_ref[b, 256:384])
        out += [x_ref[b, 0:128] - dot(l_ref[3 + b], y2, 0, 0),
                x_ref[b, 128:256] - dot(l_ref[5 + b], y2, 0, 0), y2[0:last]]
    p_ref[...] = jnp.concatenate(out, axis=0).astype(jnp.bfloat16)


def solve(fg, fa, tr, w):
    vmem = pl.BlockSpec(memory_space=pltpu.VMEM)
    return pl.pallas_call(
        solve_kernel,
        out_shape=jax.ShapeDtypeStruct((2 * GB, 256), jnp.bfloat16),
        in_specs=[vmem] * 4,
        out_specs=vmem,
        scratch_shapes=[pltpu.VMEM((12, 128, 128), F32), pltpu.VMEM((3, 128, 128), F32),
                        pltpu.VMEM((7, 128, 128), F32), pltpu.VMEM((2, 384, 256), F32),
                        pltpu.VMEM((256, 256), F32)],
        compiler_params=pltpu.CompilerParams(vmem_limit_bytes=VLIM),
        name="solve",
    )(fg, fa, tr, w)


def gather_kernel(p_ref, o_ref, local, sz, rz, sy, ry, sh, rh, sc, rc):
    dp, own = place()
    core = lax.rem(dp, 2)
    y = dp // 4
    sib = dp + 1 - 2 * core
    zh = lax.rem(dp // 2, 2)
    anti = dp + 2 - 4 * zh
    up = lax.rem(y + 1, 4) * 4 + lax.rem(dp, 4)
    down = lax.rem(y + 3, 4) * 4 + lax.rem(dp, 4)
    barrier = pltpu.get_barrier_semaphore()
    for device in (sib, anti, up, down):
        pl.semaphore_signal(barrier, inc=1, device_id=(device, own), device_id_type=MESH)
    pl.semaphore_wait(barrier, 4)

    def other(d):
        return d + 2 - 4 * lax.rem(d // 2, 2)

    far = lax.rem(y + 2, 4) * 4 + lax.rem(dp, 4)
    waits = []

    def half(ref, h):
        return ref.at[pl.ds(h * CUT[0], CUT[h])]

    def send(d, h, sems, i, device, src=None):
        src = o_ref.at[d] if src is None else src
        copy = pltpu.make_async_remote_copy(
            src_ref=half(src, h), dst_ref=half(o_ref.at[d], h), send_sem=sems[0].at[i], recv_sem=sems[1].at[i],
            device_id=(device, own), device_id_type=MESH)
        copy.start()
        waits.append(copy)

    def arrived(d, h, sems, i):
        dst = half(o_ref.at[d], h)
        pltpu.make_async_remote_copy(src_ref=dst, dst_ref=dst, send_sem=sems[0].at[i], recv_sem=sems[1].at[i],
                                     device_id=(sib, own), device_id_type=MESH).wait_recv()

    zsem, ysem, hsem, csem = (sz, rz), (sy, ry), (sh, rh), (sc, rc)
    for h in range(2):
        send(dp, h, zsem, h, anti, p_ref)
        send(dp, h, ysem, h, up, p_ref)
        send(dp, 1 - h, ysem, 3 - h, down, p_ref)
    for h in range(2):
        send(dp, h, csem, h, sib, p_ref)
    keep = pltpu.make_async_copy(p_ref, o_ref.at[dp], local)
    keep.start()
    arrived(down, 0, ysem, 0)
    send(down, 0, hsem, 0, up)
    arrived(up, 1, ysem, 3)
    send(up, 1, hsem, 1, down)
    send(down, 0, csem, 2, sib)
    send(up, 1, csem, 5, sib)
    arrived(down, 1, ysem, 1)
    send(down, 1, csem, 3, sib)
    arrived(up, 0, ysem, 2)
    send(up, 0, csem, 4, sib)
    arrived(anti, 0, zsem, 0)
    send(anti, 0, ysem, 4, up)
    send(anti, 0, ysem, 6, down)
    send(anti, 0, csem, 6, sib)
    arrived(far, 0, hsem, 0)
    send(far, 0, csem, 8, sib)
    arrived(far, 1, hsem, 1)
    send(far, 1, csem, 9, sib)
    arrived(anti, 1, zsem, 1)
    send(anti, 1, ysem, 5, up)
    send(anti, 1, ysem, 7, down)
    send(anti, 1, csem, 7, sib)
    arrived(other(down), 0, ysem, 4)
    send(other(down), 0, hsem, 2, up)
    send(other(down), 0, csem, 10, sib)
    arrived(other(up), 0, ysem, 6)
    send(other(up), 0, csem, 12, sib)
    arrived(other(up), 1, ysem, 7)
    send(other(up), 1, hsem, 3, down)
    send(other(up), 1, csem, 13, sib)
    arrived(other(down), 1, ysem, 5)
    send(other(down), 1, csem, 11, sib)
    arrived(other(far), 0, hsem, 2)
    send(other(far), 0, csem, 14, sib)
    arrived(other(far), 1, hsem, 3)
    send(other(far), 1, csem, 15, sib)

    def twin(d):
        return d + 1 - 2 * lax.rem(d, 2)

    for i, d in enumerate((dp, down, up, anti, far, other(down), other(up), other(far))):
        for h in range(2):
            arrived(twin(d), h, csem, 2 * i + h)
    keep.wait()
    for copy in waits:
        copy.wait_send()


def gather(p):
    dma = pltpu.SemaphoreType.DMA
    return pl.pallas_call(
        gather_kernel,
        out_shape=jax.ShapeDtypeStruct((16, 2 * GB, 256), jnp.bfloat16),
        in_specs=[pl.BlockSpec(memory_space=pl.ANY)],
        out_specs=pl.BlockSpec(memory_space=pl.ANY),
        scratch_shapes=[dma, dma((2,)), dma((2,)), dma((8,)), dma((8,)), dma((4,)), dma((4,)), dma((16,)), dma((16,))],
        compiler_params=pltpu.CompilerParams(collective_id=2, has_side_effects=True),
        name="gather",
    )(p)


def turn_kernel(i_ref, o_ref, ibuf, obuf, isem, osem):
    tiles = FF // 128
    parts = isem.shape[0]
    cuts = [tiles * k // parts * 128 for k in range(parts + 1)]
    ins = [pltpu.make_async_copy(i_ref.at[pl.ds(a, b - a)], ibuf.at[pl.ds(a, b - a)], isem.at[k])
           for k, (a, b) in enumerate(zip(cuts, cuts[1:]))]
    outs = [pltpu.make_async_copy(obuf.at[:, pl.ds(a, b - a)], o_ref.at[:, pl.ds(a, b - a)], osem.at[k])
            for k, (a, b) in enumerate(zip(cuts, cuts[1:]))]
    for copy in ins:
        copy.start()
    for k in range(parts):
        ins[k].wait()
        for at in range(cuts[k], cuts[k + 1], 128):
            for half in (0, 128):
                obuf[half:half + 128, at:at + 128] = ibuf[at:at + 128, half:half + 128].T
        outs[k].start()
    for copy in outs:
        copy.wait()


def turn(slices):
    anywhere = pl.BlockSpec(memory_space=pl.ANY)
    return pl.pallas_call(
        turn_kernel,
        out_shape=jax.ShapeDtypeStruct((256, FF), jnp.bfloat16),
        in_specs=[anywhere],
        out_specs=anywhere,
        scratch_shapes=[pltpu.VMEM((FF, 256), jnp.bfloat16), pltpu.VMEM((256, FF), jnp.bfloat16),
                        pltpu.SemaphoreType.DMA((4,)), pltpu.SemaphoreType.DMA((4,))],
        compiler_params=pltpu.CompilerParams(vmem_limit_bytes=VLIM),
        name="turn",
    )(slices)


def shards(acts, grads_out, weight_grad):
    fg, fa, tr = reduce_all(acts, grads_out)
    p = solve(fg.reshape(2, 512, 128), fa.reshape(256, 128), tr, weight_grad.T)
    return turn(gather(p).reshape(FF, 256))


def solution(mesh):
    in_specs = (P(("dp", "owner"), None), P(("dp", "owner"), None), P("owner", "dp"))
    out_specs = P("owner", None)
    return jax.shard_map(shards, mesh=mesh, in_specs=in_specs, out_specs=out_specs, check_vma=False)
```

```python
import functools
import math

import jax
import jax.numpy as jnp
from jax import lax
from jax.experimental import pallas as pl
from jax.experimental.pallas import tpu as pltpu
from jax.sharding import PartitionSpec as P

D = 4096
FF = 11008
AB = 256
GB = 344
TOKENS = 57344
DAMP = math.sqrt(0.03)
MESH = pl.DeviceIdType.MESH
F32 = jnp.float32
GROWS = (32, 16, 16)
AROWS = (8, 8, 0)
NB = len(GROWS)
CHS = tuple(g + a for g, a in zip(GROWS, AROWS))
GBASE = tuple(8 * sum(GROWS[:b]) for b in range(NB))
ABASE = tuple(8 * sum(AROWS[:b]) for b in range(NB))
CH = max(CHS)
HALF = 4 * CH
VLIM = 56 * 1024 * 1024
WIN = 7 * 128
WIDTHS = [WIN] * 7 + [WIN - 128]
CUT = (352, 336)


def grad_position(p, part, core):
    y = p // 2
    return 2 * part + (p + y + core) % 2, y


def act_position(k, part):
    return k % 4, 2 * part + k // 4


def window(d):
    return 128 * (43 * d // 8)


def place():
    dp = lax.axis_index("dp")
    own = lax.axis_index("owner")
    return dp, own


def gram(block):
    return lax.dot_general(block, block, (((0,), (0,)), ((), ())), preferred_element_type=F32)


def fetch(a_ref, g_ref, abuf, gbuf, core, sibling, sems, send, recv):
    rows = a_ref.shape[0]
    mine, theirs = pl.ds(0, rows), pl.ds(rows, rows)
    width = abuf.shape[1]

    def half(c):
        return a_ref.at[:, pl.ds(pl.multiple_of(c * width, 128), width)]

    def columns(p, c):
        return g_ref.at[:, pl.ds(pl.multiple_of(window(2 * p + c), 128), WIDTHS[p])]

    here = [[(half(core), abuf.at[mine])], [], []]
    away = [[(half(1 - core), abuf.at[theirs])], [], []]
    for p in range(8):
        at = pl.ds(p * WIN, WIDTHS[p])
        here[1 + p // 4].append((columns(p, core), gbuf.at[mine, at]))
        away[1 + p // 4].append((columns(p, 1 - core), gbuf.at[theirs, at]))
    here = [[pltpu.make_async_copy(src, dst, sems.at[i, n]) for n, (src, dst) in enumerate(group)]
            for i, group in enumerate(here)]
    away = [[pltpu.make_async_remote_copy(src_ref=src, dst_ref=dst, send_sem=send.at[i, n], recv_sem=recv.at[i, n],
                                          device_id=sibling, device_id_type=MESH)
             for n, (src, dst) in enumerate(group)] for i, group in enumerate(away)]
    for group in here:
        for copy in group:
            copy.start()
    return here, away


def gram_step(copies, core, abuf, gbuf, even, x_ref, y_ref, t_ref):
    def store_all(where, sizes, bases, row, value):
        px, py = where
        done = 0
        while done < value.shape[0]:
            at = row + done
            batch = max(b for b in range(NB) if bases[b] <= at and sizes[b])
            size = sizes[batch]
            chunk, left = divmod(at - bases[batch], size)
            n = min(size - left, value.shape[0] - done)
            lead = 0 if sizes is GROWS else GROWS[batch]
            rows_at = pl.ds(chunk % 4 * CHS[batch] + lead + left, n)
            if chunk < 4:
                x_ref[batch, px * 4 + py, rows_at, :] = value[done:done + n]
            else:
                y_ref[batch, py * 4 + px, rows_at, :] = value[done:done + n]
            done += n

    r = lax.broadcasted_iota(jnp.int32, (128, 128), 0)
    c = lax.broadcasted_iota(jnp.int32, (128, 128), 1)

    def diag(tile):
        return jnp.sum(jnp.where(r == c, tile, 0.0), axis=0, keepdims=True)

    act_sum = jnp.zeros((1, 128), F32)
    grad_sum = jnp.zeros((1, 128), F32)
    for copy in copies[0]:
        copy.wait()
    for k in range(8):
        g = gram(abuf[:, k * AB:(k + 1) * AB])
        t0, t2 = g[0:128, 0:128], g[128:256, 128:256]
        second = diag(t2)
        act_sum += diag(t0) + second
        t_ref[8 + k:9 + k, :] = second
        store_all(act_position(k, 0), AROWS, ABASE, 0, g[128:256, 0:128])
        store_all(act_position(k, 1), AROWS, ABASE, 0, jnp.where(r >= c, t0, t2))
    for j in range(16):
        if j in (0, 8):
            for copy in copies[1 + j // 8]:
                copy.wait()
            for odd in range(2):
                @pl.when(core == odd)
                def _():
                    for i in range(j, j + 8):
                        d = i // 2 * 2 + odd
                        start = i // 2 * WIN + 2 * GB * d - window(d) + i % 2 * GB
                        even[i, :, 0:GB] = gbuf[:, start:start + GB]
        g = gram(even[j, :, 0:256])
        t0, t2 = g[0:128, 0:128], g[128:256, 128:256]
        second = diag(t2)
        grad_sum += diag(t0) + second
        where = grad_position(j // 2, j % 2, core)
        store_all(where, GROWS, GBASE, 0, g[128:256, 0:128])
        store_all(where, GROWS, GBASE, 128, jnp.where(r >= c, t0, t2))
        store_all(where, GROWS, GBASE, 480, jnp.concatenate([second, jnp.zeros((31, 128), F32)], axis=0))

    def rest():
        corner_sum = grad_sum
        for j in range(16):
            low = lax.dot_general(even[j, :, 256:GB], even[j, :, 0:GB], (((0,), (0,)), ((), ())),
                                  preferred_element_type=F32)
            t5 = jnp.concatenate([low[:, 256:GB], jnp.zeros((88, 40), F32)], axis=1)
            corner_sum += jnp.sum(jnp.where(r[:88] == c[:88], t5, 0.0), axis=0, keepdims=True)
            tail = jnp.concatenate([pltpu.roll(t5[48:88], 40, 1), jnp.zeros((8, 128), F32)], axis=0)
            where = grad_position(j // 2, j % 2, core)
            store_all(where, GROWS, GBASE, 256, low[:, 0:128])
            store_all(where, GROWS, GBASE, 344, low[:, 128:256])
            store_all(where, GROWS, GBASE, 432, jnp.where(c[:48] < 88, t5[0:48], tail))
        t_ref[0:8, :] = jnp.concatenate([act_sum, corner_sum, jnp.zeros((6, 128), F32)], axis=0)

    return rest


def reduce_kernel(a_ref, g_ref, fg, fa, t_out,
                  abuf, gbuf, even, gx, gy, tr, ps, pk, pm, pr, rx2, ry2, st, rz, fin, ga, aa, t1, t2, t3, q1, q2, q3, q4, tt,
                  local, s0, r0, s1, r1, s2, r2, s3, r3, s4, rg4, ra4, s5, rg5, ra5, ts, tr_sem):
    dp, own = place()
    core = lax.rem(dp, 2)
    zh = lax.rem(dp // 2, 2)
    y = dp // 4
    x = lax.rem(own, 4)
    zl = own // 4
    z = zh * 4 + zl
    sib = dp + 1 - 2 * core

    def at(ax, ay, az, ac):
        return ((ay * 2 + az // 4) * 2 + ac, lax.rem(az, 4) * 4 + ax)

    xs = [at(lax.rem(x + k, 4), y, z, core) for k in (1, 2, 3)]
    ys = [at(x, lax.rem(y + k, 4), z, core) for k in (1, 2, 3)]
    zs = [at(x, y, lax.rem(z + k, 8), core) for k in range(1, 8)]
    g_part, a_part = x // 2, y // 2
    unit_zh = lax.rem(x + y + core, 2)
    unit_zl = 2 * core + lax.rem(y, 2)
    g_on = zh == unit_zh
    a_on = zl == unit_zl
    across = [at(x, lax.rem(y + k, 4), z, 1 - core) for k in range(4)]

    here, away = fetch(a_ref, g_ref, abuf, gbuf, core, (sib, own), local, s0, r0)
    barrier = pltpu.get_barrier_semaphore()
    for device in xs + ys + zs + across:
        pl.semaphore_signal(barrier, inc=1, device_id=device, device_id_type=MESH)
    pl.semaphore_wait(barrier, 17)
    for group in away:
        for copy in group:
            copy.start()
    rest = gram_step([h + a for h, a in zip(here, away)], core, abuf, gbuf, even, gx, gy, tr)

    def remote(src, dst, ssem, rsem, device):
        return pltpu.make_async_remote_copy(src_ref=src, dst_ref=dst, send_sem=ssem, recv_sem=rsem,
                                            device_id=device, device_id_type=MESH)

    def begin(copies):
        for copy in copies:
            copy.start()
        return copies

    def end(copies):
        for copy in copies:
            copy.wait()

    axes = ((0, gx, x, (xs[0], xs[2])), (1, gy, y, (ys[0], ys[2])))

    def high(b):
        return pl.ds(0, 4 * CHS[b])

    def chunk_rows(b, i):
        return pl.ds(pl.multiple_of(i * CHS[b], 8), CHS[b])

    def plane(b):
        copies = []
        two, rows = pl.ds(0, 2), high(b)
        for a, g, me, (up, down) in axes:
            opposite = lax.rem(me + 2, 4) * 4
            copies.append(remote(g.at[b, pl.ds(opposite, 2), rows], pm.at[a, b, 0, two, rows],
                                 s1.at[a, b, 0], r1.at[a, b, 0], up))
            copies.append(remote(g.at[b, pl.ds(opposite + 2, 2), rows], pm.at[a, b, 1, two, rows],
                                 s1.at[a, b, 1], r1.at[a, b, 1], down))
        for a, g, me, (up, down) in axes:
            over, under = lax.rem(me + 1, 4) * 4, lax.rem(me + 3, 4) * 4
            copies.append(remote(g.at[b, pl.ds(over + 2, 2), rows], pr.at[a, b, 0, pl.ds(2, 2), rows],
                                 s1.at[a, b, 2], r1.at[a, b, 2], up))
            copies.append(remote(g.at[b, pl.ds(under, 2), rows], pr.at[a, b, 1, two, rows],
                                 s1.at[a, b, 3], r1.at[a, b, 3], down))
        return begin(copies)

    def plane_pass(b, copies):
        end(copies[:4])
        @pl.loop(0, 8)
        def _(i):
            h, rows = i // 4, chunk_rows(b, lax.rem(i, 4))
            for a, g, me, _ in axes:
                over, under = lax.rem(me + 1, 4) * 4, lax.rem(me + 3, 4) * 4
                pk[a, b, 0, h, rows, :] = g[b, over + h, rows, :] + pm[a, b, 0, h, rows, :]
                pk[a, b, 1, h, rows, :] = g[b, under + 2 + h, rows, :] + pm[a, b, 1, h, rows, :]
        for a, _, _, to in axes:
            for d in range(2):
                copies.append(remote(pk.at[a, b, d, pl.ds(0, 2), high(b)], pr.at[a, b, d, pl.ds(2 * d, 2), high(b)],
                                     s1.at[a, b, 4 + d], r1.at[a, b, 4 + d], to[d]))
                copies[-1].start()

    def plane_sum(b, copies):
        end(copies[4:])
        @pl.loop(0, 16)
        def _(i):
            q, rows = i // 4, chunk_rows(b, lax.rem(i, 4))
            for a, g, me, _ in axes:
                ps[a, b, q, rows, :] = g[b, me * 4 + q, rows, :] + (pr[a, b, 0, q, rows, :] + pr[a, b, 1, q, rows, :])

    def cross(b):
        copies = []
        rows = high(b)
        for k in range(3):
            copies.append(remote(ps.at[0, b, lax.rem(y + k + 1, 4), rows], rx2.at[b, k, rows],
                                 s2.at[b, k], r2.at[b, k], ys[k]))
            copies.append(remote(ps.at[1, b, lax.rem(x + k + 1, 4), rows], ry2.at[b, k, rows],
                                 s2.at[b, 3 + k], r2.at[b, 3 + k], xs[k]))
        return begin(copies)

    def cross_sum(b):
        n = CHS[b]
        @pl.loop(0, 4)
        def _(i):
            rows = chunk_rows(b, i)
            st[b, i, 0:n, :] = (ps[0, b, y, rows, :] + rx2[b, 0, rows, :]) + (rx2[b, 1, rows, :] + rx2[b, 2, rows, :])
            st[b, 4 + i, 0:n, :] = ((ps[1, b, x, rows, :] + ry2[b, 0, rows, :])
                                    + (ry2[b, 1, rows, :] + ry2[b, 2, rows, :]))

    def along(b):
        rows = pl.ds(0, CHS[b])
        return begin([remote(st.at[b, lax.rem(z + k + 1, 8), rows], rz.at[b, k, rows], s3.at[b, k], r3.at[b, k], zs[k])
                      for k in range(7)])

    def along_sum(b):
        n = CHS[b]
        total = st[b, z, 0:n, :]
        for k in range(7):
            total += rz[b, k, 0:n, :]
        fin[b, 0:n, :] = total

    def pieces(b):
        found = [(fin.at[b, pl.ds(0, GROWS[b])], ga, GBASE[b], GROWS[b], rg4, [unit_zh * 4 + i for i in range(4)], 0)]
        if AROWS[b]:
            found.append((fin.at[b, pl.ds(GROWS[b], AROWS[b])], aa, ABASE[b], AROWS[b], ra4,
                          [i * 4 + unit_zl for i in range(2)], 4))
        return found

    def slot(buffer, base, size, i):
        return buffer.at[pl.ds(pl.multiple_of(base + i * size, 8), size)]

    def spread(b):
        for src, buffer, base, size, rsem, planes, first in pieces(b):
            dst = slot(buffer, base, size, z)
            for i, to in enumerate(planes):
                @pl.when(to == z)
                def _():
                    pltpu.make_async_copy(src, dst, rsem.at[b, z]).start()

                @pl.when(to != z)
                def _():
                    remote(src, dst, s4.at[b, first + i], rsem.at[b, z], at(x, y, to, core)).start()

    def spread_sent(b):
        for src, buffer, base, size, rsem, planes, first in pieces(b):
            dst = slot(buffer, base, size, z)
            for i, to in enumerate(planes):
                @pl.when(to != z)
                def _():
                    remote(src, dst, s4.at[b, first + i], rsem.at[b, z], at(x, y, to, core)).wait_send()

    def parts(b):
        for (src, buffer, base, size, rsem, _, first), (on, to, out, part, sem, at_sem) in zip(
                pieces(b), ((g_on, xs, fg, g_part, rg5, 0), (a_on, ys + across, fa, a_part, ra5, 3))):
            rows = pl.ds(base, 8 * size)
            yield src, buffer, base, size, rsem, on, to, buffer.at[rows], out, rows, part, sem, at_sem

    def give(b):
        for piece, buffer, base, size, arrive, on, to, src, out, rows, part, sem, first in parts(b):
            @pl.when(on)
            def _():
                for i in range(8):
                    pltpu.make_async_copy(piece, slot(buffer, base, size, i), arrive.at[b, i]).wait()
                dst = out.at[part, rows]
                for i, device in enumerate(to):
                    remote(src, dst, s5.at[b, first + i], sem.at[b, part], device).start()
                pltpu.make_async_copy(src, dst, sem.at[b, part]).start()

    def given(b):
        for piece, buffer, base, size, arrive, on, to, src, out, rows, part, sem, first in parts(b):
            @pl.when(on)
            def _():
                for i, device in enumerate(to):
                    remote(src, out.at[part, rows], s5.at[b, first + i], sem.at[b, part], device).wait_send()

    def taken(b):
        for piece, buffer, base, size, arrive, on, to, src, out, rows, part, sem, first in parts(b):
            for i in range(2):
                pltpu.make_async_copy(src, out.at[i, rows], sem.at[b, i]).wait()

    batches = range(NB)
    first, second, third = {}, {}, {}

    def step(name, b):
        if name == "plane":
            first[b] = plane(b)
        elif name == "pass":
            plane_pass(b, first[b])
        elif name == "cross":
            plane_sum(b, first[b])
            second[b] = cross(b)
        elif name == "along":
            end(second[b])
            cross_sum(b)
            third[b] = along(b)
        elif name == "spread":
            end(third[b])
            along_sum(b)
            spread(b)
        else:
            give(b)

    step("plane", 0)
    rest()
    q = begin([remote(tr, q1.at[k], ts.at[k], tr_sem.at[k], xs[k]) for k in range(3)])
    step("pass", 0)
    step("plane", 1)
    step("cross", 0)
    end(q)
    t1[...] = (tr[...] + q1[0]) + (q1[1] + q1[2])
    q = begin([remote(t1, q2.at[k], ts.at[3 + k], tr_sem.at[3 + k], ys[k]) for k in range(3)])
    step("pass", 1)
    step("plane", 2)
    step("along", 0)
    end(q)
    t2[...] = (t1[...] + q2[0]) + (q2[1] + q2[2])
    q = begin([remote(t2, q3.at[k], ts.at[6 + k], tr_sem.at[6 + k], zs[k]) for k in range(7)])
    step("cross", 1)
    step("pass", 2)
    step("spread", 0)
    end(q)
    trace = t2[...]
    for k in range(7):
        trace += q3[k]
    t3[...] = trace
    q = begin([remote(t3, q4, ts.at[13], tr_sem.at[13], (sib, own))])
    step("along", 1)
    step("cross", 2)
    step("give", 0)
    step("spread", 1)
    step("along", 2)
    step("give", 1)
    step("spread", 2)
    step("give", 2)
    end(q)
    tt[core] = t3[...]
    tt[1 - core] = q4[...]
    t_out[0:8, :] = tt[0, 0:8, :] + tt[1, 0:8, :]
    t_out[8:16, :] = jnp.broadcast_to(tt[own // 8, pl.ds(8 + lax.rem(own, 8), 1), :], (8, 128))
    for b in batches:
        taken(b)
    for b in batches:
        spread_sent(b)
        given(b)


def reduce_all(acts, grads):
    rows = acts.shape[0]
    vmem = pl.BlockSpec(memory_space=pltpu.VMEM)
    dma = pltpu.SemaphoreType.DMA
    tile = pltpu.VMEM((16, 128), F32)

    def buf(*shape):
        return pltpu.VMEM(shape + (128,), F32)

    return pl.pallas_call(
        reduce_kernel,
        out_shape=(jax.ShapeDtypeStruct((2, 8 * sum(GROWS), 128), F32),
                   jax.ShapeDtypeStruct((2, 8 * sum(AROWS), 128), F32),
                   jax.ShapeDtypeStruct((16, 128), F32)),
        in_specs=[pl.BlockSpec(memory_space=pl.ANY)] * 2,
        out_specs=(vmem,) * 3,
        scratch_shapes=[
            pltpu.VMEM((2 * rows, D // 2), acts.dtype), pltpu.VMEM((2 * rows, 8 * WIN), acts.dtype),
            pltpu.VMEM((16, 2 * rows, 384), acts.dtype),
            buf(NB, 16, HALF), buf(NB, 16, HALF), tile,
            buf(2, NB, 4, HALF), buf(2, NB, 2, 2, HALF), buf(2, NB, 2, 2, HALF), buf(2, NB, 2, 4, HALF),
            buf(NB, 3, HALF), buf(NB, 3, HALF), buf(NB, 8, CH), buf(NB, 7, CH), buf(NB, CH),
            buf(8 * sum(GROWS)), buf(8 * sum(AROWS)),
            tile, tile, tile, buf(3, 16), buf(3, 16), buf(7, 16), tile, buf(2, 16),
            dma((3, 4)), dma((3, 4)), dma((3, 4)), dma((2, NB, 6)), dma((2, NB, 6)), dma((NB, 6)), dma((NB, 6)), dma((NB, 7)), dma((NB, 7)),
            dma((NB, 6)), dma((NB, 8)), dma((NB, 8)), dma((NB, 10)), dma((NB, 2)), dma((NB, 2)), dma((14,)), dma((14,)),
        ],
        compiler_params=pltpu.CompilerParams(collective_id=1, has_side_effects=True, vmem_limit_bytes=VLIM),
        name="reduce_all",
    )(acts, grads)


def split(v):
    high = v.astype(jnp.bfloat16).astype(F32)
    rest = v - high
    mid = rest.astype(jnp.bfloat16).astype(F32)
    return high, mid, rest - mid


def dot(a, b, ca=1, cb=0):
    ah, am, al = split(a)
    bh, bm, bl = split(b)
    left = jnp.concatenate([ah, ah, am, ah, am, al], axis=ca).astype(jnp.bfloat16)
    right = jnp.concatenate([bh, bm, bh, bl, bm, bh], axis=cb).astype(jnp.bfloat16)
    return lax.dot_general(left, right, (((ca,), (cb,)), ((), ())), preferred_element_type=F32)


def sweep_four(now, at, row, sub, lane):
    def full(v):
        return jnp.broadcast_to(v, (8, 128))

    four = range(4)
    cols = [full(now[:, at + i:at + i + 1]) for i in four]
    rows = [full(now[row + i:row + i + 1, :]) for i in four]
    m = {(i, j): full(cols[j][row + i:row + i + 1, :]) for i in four for j in range(i + 1)}
    for p in four:
        inv = 1.0 / m[(p, p)]
        line = {i: m[(max(i, p), min(i, p))] * inv for i in four if i != p}
        new = {}
        for i in four:
            for j in range(i + 1):
                if i == p and j == p:
                    new[(i, j)] = -inv
                elif i == p:
                    new[(i, j)] = line[j]
                elif j == p:
                    new[(i, j)] = line[i]
                else:
                    new[(i, j)] = m[(i, j)] - m[(max(i, p), min(i, p))] * line[j]
        m = new
    in_rows = jnp.logical_and(sub >= row, sub < row + 4)
    in_cols = jnp.logical_and(lane >= at, lane < at + 4)
    out = jnp.where(jnp.logical_or(in_rows, in_cols), 0.0, now)
    rows = [jnp.where(in_cols, jnp.where(lane == at + i, -1.0, 0.0), rows[i]) for i in four]
    terms = []
    for i in four:
        col = jnp.where(in_rows, jnp.where(sub == row + i, -1.0, 0.0), cols[i])
        t = [m[(max(i, j), min(i, j))] * rows[j] for j in four]
        terms.append(col * ((t[0] + t[1]) + (t[2] + t[3])))
    return (out + terms[0]) + (terms[1] + (terms[2] + terms[3]))


def sweep_tiles(refs, panels, others=()):
    others = list(others)
    sub = lax.broadcasted_iota(jnp.int32, (8, 128), 0)
    lane = lax.broadcasted_iota(jnp.int32, (8, 128), 1)
    lane_all = lax.broadcasted_iota(jnp.int32, (128, 128), 1)
    for p in range(panels):
        base = 8 * p
        inside = jnp.logical_and(lane_all >= base, lane_all < base + 8)
        olds = [ref[base:base + 8, :] for ref in refs]
        news = [sweep_four(old, base, 0, sub, lane) for old in olds]
        news = [sweep_four(new, base + 4, 4, sub, lane) for new in news]
        for ref, old, new in zip(refs, olds, news):
            ref[...] = jnp.where(inside, 0.0, ref[...]) - dot(old, new, 0, 0)
            ref[base:base + 8, :] = new
        count = -(-len(others) // (panels - p))
        for step in others[:count]:
            step()
        others = others[count:]


def solve_kernel(fg_ref, fa_ref, t_ref, w_ref, p_ref, g_ref, a_ref, l_ref, x_ref, ai_ref):
    act_trace = jnp.sum(t_ref[0:1, :], keepdims=True) / TOKENS
    grad_trace = jnp.sum(t_ref[1:2, :], keepdims=True) / TOKENS
    ratio = jnp.sqrt(act_trace / D / (grad_trace / FF))
    act_damp = ratio * DAMP
    grad_damp = DAMP / ratio
    r = lax.broadcasted_iota(jnp.int32, (128, 128), 0)
    c = lax.broadcasted_iota(jnp.int32, (128, 128), 1)
    last = GB - 256

    def pair(both, second):
        turned = both.T
        first = jnp.where(r >= c, both, turned)
        other = jnp.where(r < c, both, jnp.where(r == c, jnp.broadcast_to(second, (128, 128)), turned))
        return first, other

    def damped(tile, damp):
        return tile / TOKENS + jnp.where(r == c, damp, 0.0)

    zeros = jnp.zeros((128 - last, 128), F32)
    for b in range(2):
        first, second = pair(fg_ref[b, 128:256, :], fg_ref[b, 480:481, :])
        g_ref[b * 6] = damped(first, grad_damp)
        g_ref[b * 6 + 1] = fg_ref[b, 0:128, :] / TOKENS
        g_ref[b * 6 + 2] = damped(second, grad_damp)
        g_ref[b * 6 + 3] = jnp.concatenate([fg_ref[b, 256:344, :] / TOKENS, zeros], axis=0)
        g_ref[b * 6 + 4] = jnp.concatenate([fg_ref[b, 344:432, :] / TOKENS, zeros], axis=0)
        packed = fg_ref[b, 432:480, :]
        low = pltpu.roll(packed[0:40], 88, 1)
        upper = jnp.concatenate([packed, low, jnp.zeros((40, 128), F32)], axis=0)
        corner = jnp.where(jnp.logical_and(r >= 48, c < 48), upper.T, upper)
        inside = jnp.logical_and(r < last, c < last)
        g_ref[b * 6 + 5] = jnp.where(inside, damped(corner, grad_damp), jnp.where(r == c, 1.0, 0.0))
    first, second = pair(fa_ref[128:256, :], t_ref[8:9, :])
    a_ref[0] = damped(first, act_damp)
    a_ref[1] = fa_ref[0:128, :] / TOKENS
    a_ref[2] = damped(second, act_damp)
    gs = [[g_ref.at[b * 6 + t] for t in range(6)] for b in range(2)]
    am = [a_ref.at[t] for t in range(3)]
    sweep_tiles([gs[0][0], gs[1][0], am[0]], 16)
    for m in gs + [am]:
        a10 = m[1][...]
        l10 = -dot(a10, m[0][...])
        m[2][...] -= dot(l10, a10, 1, 1)
        l_ref[0 if m is gs[0] else 1 if m is gs[1] else 2] = l10

    def row_two(b):
        m = gs[b]
        a20 = m[3][...]

        def lower():
            l_ref[3 + b] = -dot(a20, m[0][...])

        def side():
            m[4][...] -= dot(l_ref[3 + b], m[1][...], 1, 1)

        def corner():
            m[5][...] -= dot(l_ref[3 + b], a20, 1, 1)
        return [lower, side, corner]

    steps = [step for pair_of in zip(row_two(0), row_two(1)) for step in pair_of]
    sweep_tiles([gs[0][2], gs[1][2], am[2]], 16, steps)
    for b, m in enumerate(gs):
        a21 = m[4][...]
        l21 = -dot(a21, m[2][...])
        m[5][...] -= dot(l21, a21, 1, 1)
        l_ref[5 + b] = l21

    def act_cross():
        v10 = -dot(am[2][...], l_ref[2])
        ai_ref[128:256, 0:128] = -v10
        ai_ref[0:128, 128:256] = -v10.T
        ai_ref[128:256, 128:256] = -am[2][...]

    def act_first():
        ai_ref[0:128, 0:128] = -am[0][...] - dot(l_ref[2], ai_ref[128:256, 0:128], 0, 0)

    def right_side(b):
        w = w_ref[...].astype(F32)[b * GB:(b + 1) * GB]
        w = jnp.concatenate([w, jnp.zeros((384 - GB, 256), F32)], axis=0).astype(jnp.bfloat16)
        pieces = jnp.concatenate(split(ai_ref[...]), axis=0).astype(jnp.bfloat16)
        x_ref[b] = jnp.dot(jnp.concatenate([w, w, w], axis=1), pieces, preferred_element_type=F32)

    def through(b):
        x = [x_ref.at[b, pl.ds(128 * i, 128)] for i in range(3)]
        l10, l20, l21 = l_ref.at[b], l_ref.at[3 + b], l_ref.at[5 + b]
        m = gs[b]

        def one():
            x[1][...] -= dot(l10[...], x[0][...])

        def two():
            x[2][...] -= dot(l20[...], x[0][...])

        def three():
            x[2][...] -= dot(l21[...], x[1][...])

        def four():
            x[1][...] = -dot(m[2][...], x[1][...])

        def five():
            x[0][...] = -dot(m[0][...], x[0][...])

        def six():
            x[0][...] -= dot(l10[...], x[1][...], 0, 0)

        def seven():
            l20[...] -= dot(l21[...], l10[...])
        return [one, two, three, four, five, six, seven]

    steps = [act_cross, act_first, lambda: right_side(0), lambda: right_side(1)]
    steps += [step for pair_of in zip(through(0), through(1)) for step in pair_of]
    sweep_tiles([gs[0][5], gs[1][5]], last // 8, steps)
    out = []
    for b, m in enumerate(gs):
        y2 = -dot(m[5][...], x_ref[b, 256:384])
        out += [x_ref[b, 0:128] - dot(l_ref[3 + b], y2, 0, 0),
                x_ref[b, 128:256] - dot(l_ref[5 + b], y2, 0, 0), y2[0:last]]
    p_ref[...] = jnp.concatenate(out, axis=0).astype(jnp.bfloat16)


def solve(fg, fa, tr, w):
    vmem = pl.BlockSpec(memory_space=pltpu.VMEM)
    return pl.pallas_call(
        solve_kernel,
        out_shape=jax.ShapeDtypeStruct((2 * GB, 256), jnp.bfloat16),
        in_specs=[vmem] * 4,
        out_specs=vmem,
        scratch_shapes=[pltpu.VMEM((12, 128, 128), F32), pltpu.VMEM((3, 128, 128), F32),
                        pltpu.VMEM((7, 128, 128), F32), pltpu.VMEM((2, 384, 256), F32),
                        pltpu.VMEM((256, 256), F32)],
        compiler_params=pltpu.CompilerParams(vmem_limit_bytes=VLIM),
        name="solve",
    )(fg, fa, tr, w)


def gather_kernel(p_ref, o_ref, local, sz, rz, sy, ry, sh, rh, sc, rc):
    dp, own = place()
    core = lax.rem(dp, 2)
    y = dp // 4
    sib = dp + 1 - 2 * core
    zh = lax.rem(dp // 2, 2)
    anti = dp + 2 - 4 * zh
    up = lax.rem(y + 1, 4) * 4 + lax.rem(dp, 4)
    down = lax.rem(y + 3, 4) * 4 + lax.rem(dp, 4)
    barrier = pltpu.get_barrier_semaphore()
    for device in (sib, anti, up, down):
        pl.semaphore_signal(barrier, inc=1, device_id=(device, own), device_id_type=MESH)
    pl.semaphore_wait(barrier, 4)

    def other(d):
        return d + 2 - 4 * lax.rem(d // 2, 2)

    far = lax.rem(y + 2, 4) * 4 + lax.rem(dp, 4)
    waits = []

    def half(ref, h):
        return ref.at[pl.ds(h * CUT[0], CUT[h])]

    def send(d, h, sems, i, device, src=None):
        src = o_ref.at[d] if src is None else src
        copy = pltpu.make_async_remote_copy(
            src_ref=half(src, h), dst_ref=half(o_ref.at[d], h), send_sem=sems[0].at[i], recv_sem=sems[1].at[i],
            device_id=(device, own), device_id_type=MESH)
        copy.start()
        waits.append(copy)

    def arrived(d, h, sems, i):
        dst = half(o_ref.at[d], h)
        pltpu.make_async_remote_copy(src_ref=dst, dst_ref=dst, send_sem=sems[0].at[i], recv_sem=sems[1].at[i],
                                     device_id=(sib, own), device_id_type=MESH).wait_recv()

    zsem, ysem, hsem, csem = (sz, rz), (sy, ry), (sh, rh), (sc, rc)
    for h in range(2):
        send(dp, h, zsem, h, anti, p_ref)
        send(dp, h, ysem, h, up, p_ref)
        send(dp, 1 - h, ysem, 3 - h, down, p_ref)
    for h in range(2):
        send(dp, h, csem, h, sib, p_ref)
    keep = pltpu.make_async_copy(p_ref, o_ref.at[dp], local)
    keep.start()
    arrived(down, 0, ysem, 0)
    send(down, 0, hsem, 0, up)
    arrived(up, 1, ysem, 3)
    send(up, 1, hsem, 1, down)
    send(down, 0, csem, 2, sib)
    send(up, 1, csem, 5, sib)
    arrived(down, 1, ysem, 1)
    send(down, 1, csem, 3, sib)
    arrived(up, 0, ysem, 2)
    send(up, 0, csem, 4, sib)
    arrived(anti, 0, zsem, 0)
    send(anti, 0, ysem, 4, up)
    send(anti, 0, ysem, 6, down)
    send(anti, 0, csem, 6, sib)
    arrived(far, 0, hsem, 0)
    send(far, 0, csem, 8, sib)
    arrived(far, 1, hsem, 1)
    send(far, 1, csem, 9, sib)
    arrived(anti, 1, zsem, 1)
    send(anti, 1, ysem, 5, up)
    send(anti, 1, ysem, 7, down)
    send(anti, 1, csem, 7, sib)
    arrived(other(down), 0, ysem, 4)
    send(other(down), 0, hsem, 2, up)
    send(other(down), 0, csem, 10, sib)
    arrived(other(up), 0, ysem, 6)
    send(other(up), 0, csem, 12, sib)
    arrived(other(up), 1, ysem, 7)
    send(other(up), 1, hsem, 3, down)
    send(other(up), 1, csem, 13, sib)
    arrived(other(down), 1, ysem, 5)
    send(other(down), 1, csem, 11, sib)
    arrived(other(far), 0, hsem, 2)
    send(other(far), 0, csem, 14, sib)
    arrived(other(far), 1, hsem, 3)
    send(other(far), 1, csem, 15, sib)

    def twin(d):
        return d + 1 - 2 * lax.rem(d, 2)

    for i, d in enumerate((dp, down, up, anti, far, other(down), other(up), other(far))):
        for h in range(2):
            arrived(twin(d), h, csem, 2 * i + h)
    keep.wait()
    for copy in waits:
        copy.wait_send()


def gather(p):
    dma = pltpu.SemaphoreType.DMA
    return pl.pallas_call(
        gather_kernel,
        out_shape=jax.ShapeDtypeStruct((16, 2 * GB, 256), jnp.bfloat16),
        in_specs=[pl.BlockSpec(memory_space=pl.ANY)],
        out_specs=pl.BlockSpec(memory_space=pl.ANY),
        scratch_shapes=[dma, dma((2,)), dma((2,)), dma((8,)), dma((8,)), dma((4,)), dma((4,)), dma((16,)), dma((16,))],
        compiler_params=pltpu.CompilerParams(collective_id=2, has_side_effects=True),
        name="gather",
    )(p)


def turn_kernel(i_ref, o_ref, ibuf, obuf, isem, osem):
    tiles = FF // 128
    parts = isem.shape[0]
    cuts = [tiles * k // parts * 128 for k in range(parts + 1)]
    ins = [pltpu.make_async_copy(i_ref.at[pl.ds(a, b - a)], ibuf.at[pl.ds(a, b - a)], isem.at[k])
           for k, (a, b) in enumerate(zip(cuts, cuts[1:]))]
    outs = [pltpu.make_async_copy(obuf.at[:, pl.ds(a, b - a)], o_ref.at[:, pl.ds(a, b - a)], osem.at[k])
            for k, (a, b) in enumerate(zip(cuts, cuts[1:]))]
    for copy in ins:
        copy.start()
    for k in range(parts):
        ins[k].wait()
        for at in range(cuts[k], cuts[k + 1], 128):
            for half in (0, 128):
                obuf[half:half + 128, at:at + 128] = ibuf[at:at + 128, half:half + 128].T
        outs[k].start()
    for copy in outs:
        copy.wait()


def turn(slices):
    anywhere = pl.BlockSpec(memory_space=pl.ANY)
    return pl.pallas_call(
        turn_kernel,
        out_shape=jax.ShapeDtypeStruct((256, FF), jnp.bfloat16),
        in_specs=[anywhere],
        out_specs=anywhere,
        scratch_shapes=[pltpu.VMEM((FF, 256), jnp.bfloat16), pltpu.VMEM((256, FF), jnp.bfloat16),
                        pltpu.SemaphoreType.DMA((4,)), pltpu.SemaphoreType.DMA((4,))],
        compiler_params=pltpu.CompilerParams(vmem_limit_bytes=VLIM),
        name="turn",
    )(slices)


def shards(acts, grads_out, weight_grad):
    fg, fa, tr = reduce_all(acts, grads_out)
    p = solve(fg, fa.reshape(256, 128), tr, weight_grad.T)
    return turn(gather(p).reshape(FF, 256))


def solution(mesh):
    in_specs = (P(("dp", "owner"), None), P(("dp", "owner"), None), P("owner", "dp"))
    out_specs = P("owner", None)
    return jax.shard_map(shards, mesh=mesh, in_specs=in_specs, out_specs=out_specs, check_vma=False)
```

```python
import functools
import math

import jax
import jax.numpy as jnp
from jax import lax
from jax.experimental import pallas as pl
from jax.experimental.pallas import tpu as pltpu
from jax.sharding import PartitionSpec as P

D = 4096
FF = 11008
AB = 256
GB = 344
TOKENS = 57344
DAMP = math.sqrt(0.03)
MESH = pl.DeviceIdType.MESH
F32 = jnp.float32
GROWS = (32, 16, 16)
AROWS = (16, 0, 0)
NB = len(GROWS)
CHS = tuple(g + a for g, a in zip(GROWS, AROWS))
GBASE = tuple(8 * sum(GROWS[:b]) for b in range(NB))
ABASE = tuple(8 * sum(AROWS[:b]) for b in range(NB))
CH = max(CHS)
HALF = 4 * CH
VLIM = 56 * 1024 * 1024
WIN = 7 * 128
WIDTHS = [WIN] * 7 + [WIN - 128]
CUT = (352, 336)


def grad_position(p, part, core):
    y = p // 2
    return 2 * part + (p + y + core) % 2, y


def act_position(k, part):
    return k % 4, 2 * part + k // 4


def window(d):
    return 128 * (43 * d // 8)


def place():
    dp = lax.axis_index("dp")
    own = lax.axis_index("owner")
    return dp, own


def gram(block):
    return lax.dot_general(block, block, (((0,), (0,)), ((), ())), preferred_element_type=F32)


def fetch(a_ref, g_ref, abuf, gbuf, core, sibling, sems, send, recv):
    rows = a_ref.shape[0]
    mine, theirs = pl.ds(0, rows), pl.ds(rows, rows)
    width = abuf.shape[1]

    def half(c):
        return a_ref.at[:, pl.ds(pl.multiple_of(c * width, 128), width)]

    def columns(p, c):
        return g_ref.at[:, pl.ds(pl.multiple_of(window(2 * p + c), 128), WIDTHS[p])]

    here = [[(half(core), abuf.at[mine])], [], []]
    away = [[(half(1 - core), abuf.at[theirs])], [], []]
    for p in range(8):
        at = pl.ds(p * WIN, WIDTHS[p])
        here[1 + p // 4].append((columns(p, core), gbuf.at[mine, at]))
        away[1 + p // 4].append((columns(p, 1 - core), gbuf.at[theirs, at]))
    here = [[pltpu.make_async_copy(src, dst, sems.at[i, n]) for n, (src, dst) in enumerate(group)]
            for i, group in enumerate(here)]
    away = [[pltpu.make_async_remote_copy(src_ref=src, dst_ref=dst, send_sem=send.at[i, n], recv_sem=recv.at[i, n],
                                          device_id=sibling, device_id_type=MESH)
             for n, (src, dst) in enumerate(group)] for i, group in enumerate(away)]
    for group in here:
        for copy in group:
            copy.start()
    return here, away


def gram_step(copies, core, abuf, gbuf, even, x_ref, y_ref, t_ref):
    def store_all(where, sizes, bases, row, value):
        px, py = where
        done = 0
        while done < value.shape[0]:
            at = row + done
            batch = max(b for b in range(NB) if bases[b] <= at and sizes[b])
            size = sizes[batch]
            chunk, left = divmod(at - bases[batch], size)
            n = min(size - left, value.shape[0] - done)
            lead = 0 if sizes is GROWS else GROWS[batch]
            rows_at = pl.ds(chunk % 4 * CHS[batch] + lead + left, n)
            if chunk < 4:
                x_ref[batch, px * 4 + py, rows_at, :] = value[done:done + n]
            else:
                y_ref[batch, py * 4 + px, rows_at, :] = value[done:done + n]
            done += n

    r = lax.broadcasted_iota(jnp.int32, (128, 128), 0)
    c = lax.broadcasted_iota(jnp.int32, (128, 128), 1)

    def diag(tile):
        return jnp.sum(jnp.where(r == c, tile, 0.0), axis=0, keepdims=True)

    act_sum = jnp.zeros((1, 128), F32)
    grad_sum = jnp.zeros((1, 128), F32)
    for copy in copies[0]:
        copy.wait()
    for k in range(8):
        g = gram(abuf[:, k * AB:(k + 1) * AB])
        t0, t2 = g[0:128, 0:128], g[128:256, 128:256]
        second = diag(t2)
        act_sum += diag(t0) + second
        t_ref[8 + k:9 + k, :] = second
        store_all(act_position(k, 0), AROWS, ABASE, 0, g[128:256, 0:128])
        store_all(act_position(k, 1), AROWS, ABASE, 0, jnp.where(r >= c, t0, t2))
    for j in range(16):
        if j in (0, 8):
            for copy in copies[1 + j // 8]:
                copy.wait()
            for odd in range(2):
                @pl.when(core == odd)
                def _():
                    for i in range(j, j + 8):
                        d = i // 2 * 2 + odd
                        start = i // 2 * WIN + 2 * GB * d - window(d) + i % 2 * GB
                        even[i, :, 0:GB] = gbuf[:, start:start + GB]
        g = gram(even[j, :, 0:256])
        t0, t2 = g[0:128, 0:128], g[128:256, 128:256]
        second = diag(t2)
        grad_sum += diag(t0) + second
        where = grad_position(j // 2, j % 2, core)
        store_all(where, GROWS, GBASE, 0, g[128:256, 0:128])
        store_all(where, GROWS, GBASE, 128, jnp.where(r >= c, t0, t2))
        store_all(where, GROWS, GBASE, 480, jnp.concatenate([second, jnp.zeros((31, 128), F32)], axis=0))

    def rest():
        corner_sum = grad_sum
        for j in range(16):
            low = lax.dot_general(even[j, :, 256:GB], even[j, :, 0:GB], (((0,), (0,)), ((), ())),
                                  preferred_element_type=F32)
            t5 = jnp.concatenate([low[:, 256:GB], jnp.zeros((88, 40), F32)], axis=1)
            corner_sum += jnp.sum(jnp.where(r[:88] == c[:88], t5, 0.0), axis=0, keepdims=True)
            tail = jnp.concatenate([pltpu.roll(t5[48:88], 40, 1), jnp.zeros((8, 128), F32)], axis=0)
            where = grad_position(j // 2, j % 2, core)
            store_all(where, GROWS, GBASE, 256, low[:, 0:128])
            store_all(where, GROWS, GBASE, 344, low[:, 128:256])
            store_all(where, GROWS, GBASE, 432, jnp.where(c[:48] < 88, t5[0:48], tail))
        t_ref[0:8, :] = jnp.concatenate([act_sum, corner_sum, jnp.zeros((6, 128), F32)], axis=0)

    return rest


def reduce_kernel(a_ref, g_ref, fg, fa, t_out, swept,
                  abuf, gbuf, even, gx, gy, tr, ps, pk, pm, pr, rx2, ry2, st, rz, fin, ga, aa, t1, t2, t3, q1, q2, q3, q4, tt,
                  local, s0, r0, s1, r1, s2, r2, s3, r3, s4, rg4, ra4, s5, rg5, ra5, ts, tr_sem):
    dp, own = place()
    core = lax.rem(dp, 2)
    zh = lax.rem(dp // 2, 2)
    y = dp // 4
    x = lax.rem(own, 4)
    zl = own // 4
    z = zh * 4 + zl
    sib = dp + 1 - 2 * core

    def at(ax, ay, az, ac):
        return ((ay * 2 + az // 4) * 2 + ac, lax.rem(az, 4) * 4 + ax)

    xs = [at(lax.rem(x + k, 4), y, z, core) for k in (1, 2, 3)]
    ys = [at(x, lax.rem(y + k, 4), z, core) for k in (1, 2, 3)]
    zs = [at(x, y, lax.rem(z + k, 8), core) for k in range(1, 8)]
    g_part, a_part = x // 2, y // 2
    unit_zh = lax.rem(x + y + core, 2)
    unit_zl = 2 * core + lax.rem(y, 2)
    g_on = zh == unit_zh
    a_on = zl == unit_zl
    across = [at(x, lax.rem(y + k, 4), z, 1 - core) for k in range(4)]

    here, away = fetch(a_ref, g_ref, abuf, gbuf, core, (sib, own), local, s0, r0)
    barrier = pltpu.get_barrier_semaphore()
    for device in xs + ys + zs + across:
        pl.semaphore_signal(barrier, inc=1, device_id=device, device_id_type=MESH)
    pl.semaphore_wait(barrier, 17)
    for group in away:
        for copy in group:
            copy.start()
    rest = gram_step([h + a for h, a in zip(here, away)], core, abuf, gbuf, even, gx, gy, tr)

    def remote(src, dst, ssem, rsem, device):
        return pltpu.make_async_remote_copy(src_ref=src, dst_ref=dst, send_sem=ssem, recv_sem=rsem,
                                            device_id=device, device_id_type=MESH)

    def begin(copies):
        for copy in copies:
            copy.start()
        return copies

    def end(copies):
        for copy in copies:
            copy.wait()

    axes = ((0, gx, x, (xs[0], xs[2])), (1, gy, y, (ys[0], ys[2])))

    def high(b):
        return pl.ds(0, 4 * CHS[b])

    def chunk_rows(b, i):
        return pl.ds(pl.multiple_of(i * CHS[b], 8), CHS[b])

    def plane(b):
        copies = []
        two, rows = pl.ds(0, 2), high(b)
        for a, g, me, (up, down) in axes:
            opposite = lax.rem(me + 2, 4) * 4
            copies.append(remote(g.at[b, pl.ds(opposite, 2), rows], pm.at[a, b, 0, two, rows],
                                 s1.at[a, b, 0], r1.at[a, b, 0], up))
            copies.append(remote(g.at[b, pl.ds(opposite + 2, 2), rows], pm.at[a, b, 1, two, rows],
                                 s1.at[a, b, 1], r1.at[a, b, 1], down))
        for a, g, me, (up, down) in axes:
            over, under = lax.rem(me + 1, 4) * 4, lax.rem(me + 3, 4) * 4
            copies.append(remote(g.at[b, pl.ds(over + 2, 2), rows], pr.at[a, b, 0, pl.ds(2, 2), rows],
                                 s1.at[a, b, 2], r1.at[a, b, 2], up))
            copies.append(remote(g.at[b, pl.ds(under, 2), rows], pr.at[a, b, 1, two, rows],
                                 s1.at[a, b, 3], r1.at[a, b, 3], down))
        return begin(copies)

    def plane_pass(b, copies):
        end(copies[:4])
        @pl.loop(0, 8)
        def _(i):
            h, rows = i // 4, chunk_rows(b, lax.rem(i, 4))
            for a, g, me, _ in axes:
                over, under = lax.rem(me + 1, 4) * 4, lax.rem(me + 3, 4) * 4
                pk[a, b, 0, h, rows, :] = g[b, over + h, rows, :] + pm[a, b, 0, h, rows, :]
                pk[a, b, 1, h, rows, :] = g[b, under + 2 + h, rows, :] + pm[a, b, 1, h, rows, :]
        for a, _, _, to in axes:
            for d in range(2):
                copies.append(remote(pk.at[a, b, d, pl.ds(0, 2), high(b)], pr.at[a, b, d, pl.ds(2 * d, 2), high(b)],
                                     s1.at[a, b, 4 + d], r1.at[a, b, 4 + d], to[d]))
                copies[-1].start()

    def plane_sum(b, copies):
        end(copies[4:])
        @pl.loop(0, 16)
        def _(i):
            q, rows = i // 4, chunk_rows(b, lax.rem(i, 4))
            for a, g, me, _ in axes:
                ps[a, b, q, rows, :] = g[b, me * 4 + q, rows, :] + (pr[a, b, 0, q, rows, :] + pr[a, b, 1, q, rows, :])

    def cross(b):
        copies = []
        rows = high(b)
        for k in range(3):
            copies.append(remote(ps.at[0, b, lax.rem(y + k + 1, 4), rows], rx2.at[b, k, rows],
                                 s2.at[b, k], r2.at[b, k], ys[k]))
            copies.append(remote(ps.at[1, b, lax.rem(x + k + 1, 4), rows], ry2.at[b, k, rows],
                                 s2.at[b, 3 + k], r2.at[b, 3 + k], xs[k]))
        return begin(copies)

    def cross_sum(b):
        n = CHS[b]
        @pl.loop(0, 4)
        def _(i):
            rows = chunk_rows(b, i)
            st[b, i, 0:n, :] = (ps[0, b, y, rows, :] + rx2[b, 0, rows, :]) + (rx2[b, 1, rows, :] + rx2[b, 2, rows, :])
            st[b, 4 + i, 0:n, :] = ((ps[1, b, x, rows, :] + ry2[b, 0, rows, :])
                                    + (ry2[b, 1, rows, :] + ry2[b, 2, rows, :]))

    def along(b):
        rows = pl.ds(0, CHS[b])
        return begin([remote(st.at[b, lax.rem(z + k + 1, 8), rows], rz.at[b, k, rows], s3.at[b, k], r3.at[b, k], zs[k])
                      for k in range(7)])

    def along_sum(b):
        n = CHS[b]
        total = st[b, z, 0:n, :]
        for k in range(7):
            total += rz[b, k, 0:n, :]
        fin[b, 0:n, :] = total

    def pieces(b):
        found = [(fin.at[b, pl.ds(0, GROWS[b])], ga, GBASE[b], GROWS[b], rg4, [unit_zh * 4 + i for i in range(4)], 0)]
        if AROWS[b]:
            found.append((fin.at[b, pl.ds(GROWS[b], AROWS[b])], aa, ABASE[b], AROWS[b], ra4,
                          [i * 4 + unit_zl for i in range(2)], 4))
        return found

    def slot(buffer, base, size, i):
        return buffer.at[pl.ds(pl.multiple_of(base + i * size, 8), size)]

    def spread(b):
        for src, buffer, base, size, rsem, planes, first in pieces(b):
            dst = slot(buffer, base, size, z)
            for i, to in enumerate(planes):
                @pl.when(to == z)
                def _():
                    pltpu.make_async_copy(src, dst, rsem.at[b, z]).start()

                @pl.when(to != z)
                def _():
                    remote(src, dst, s4.at[b, first + i], rsem.at[b, z], at(x, y, to, core)).start()

    def spread_sent(b):
        for src, buffer, base, size, rsem, planes, first in pieces(b):
            dst = slot(buffer, base, size, z)
            for i, to in enumerate(planes):
                @pl.when(to != z)
                def _():
                    remote(src, dst, s4.at[b, first + i], rsem.at[b, z], at(x, y, to, core)).wait_send()

    def parts(b):
        for (src, buffer, base, size, rsem, _, first), (on, to, out, part, sem, at_sem) in zip(
                pieces(b), ((g_on, xs, fg, g_part, rg5, 0), (a_on, ys + across, fa, a_part, ra5, 3))):
            rows = pl.ds(base, 8 * size)
            yield src, buffer, base, size, rsem, on, to, buffer.at[rows], out, rows, part, sem, at_sem

    def give(b):
        for piece, buffer, base, size, arrive, on, to, src, out, rows, part, sem, first in parts(b):
            @pl.when(on)
            def _():
                for i in range(8):
                    pltpu.make_async_copy(piece, slot(buffer, base, size, i), arrive.at[b, i]).wait()
                dst = out.at[part, rows]
                for i, device in enumerate(to):
                    remote(src, dst, s5.at[b, first + i], sem.at[b, part], device).start()
                pltpu.make_async_copy(src, dst, sem.at[b, part]).start()

    def given(b):
        for piece, buffer, base, size, arrive, on, to, src, out, rows, part, sem, first in parts(b):
            @pl.when(on)
            def _():
                for i, device in enumerate(to):
                    remote(src, out.at[part, rows], s5.at[b, first + i], sem.at[b, part], device).wait_send()

    def taken(b):
        for piece, buffer, base, size, arrive, on, to, src, out, rows, part, sem, first in parts(b):
            for i in range(2):
                pltpu.make_async_copy(src, out.at[i, rows], sem.at[b, i]).wait()

    batches = range(NB)
    first, second, third = {}, {}, {}

    def step(name, b):
        if name == "plane":
            first[b] = plane(b)
        elif name == "pass":
            plane_pass(b, first[b])
        elif name == "cross":
            plane_sum(b, first[b])
            second[b] = cross(b)
        elif name == "along":
            end(second[b])
            cross_sum(b)
            third[b] = along(b)
        elif name == "spread":
            end(third[b])
            along_sum(b)
            spread(b)
        else:
            give(b)

    step("plane", 0)
    rest()
    q = begin([remote(tr, q1.at[k], ts.at[k], tr_sem.at[k], xs[k]) for k in range(3)])
    step("pass", 0)
    step("plane", 1)
    step("cross", 0)
    end(q)
    t1[...] = (tr[...] + q1[0]) + (q1[1] + q1[2])
    q = begin([remote(t1, q2.at[k], ts.at[3 + k], tr_sem.at[3 + k], ys[k]) for k in range(3)])
    step("pass", 1)
    step("plane", 2)
    step("along", 0)
    end(q)
    t2[...] = (t1[...] + q2[0]) + (q2[1] + q2[2])
    q = begin([remote(t2, q3.at[k], ts.at[6 + k], tr_sem.at[6 + k], zs[k]) for k in range(7)])
    step("cross", 1)
    step("pass", 2)
    step("spread", 0)
    end(q)
    trace = t2[...]
    for k in range(7):
        trace += q3[k]
    t3[...] = trace
    q = begin([remote(t3, q4, ts.at[13], tr_sem.at[13], (sib, own))])
    step("along", 1)
    step("cross", 2)
    step("give", 0)
    step("spread", 1)
    step("along", 2)
    end(q)
    tt[core] = t3[...]
    tt[1 - core] = q4[...]
    t_out[0:8, :] = tt[0, 0:8, :] + tt[1, 0:8, :]
    t_out[8:16, :] = jnp.broadcast_to(tt[own // 8, pl.ds(8 + lax.rem(own, 8), 1), :], (8, 128))
    taken(0)
    act_damp, grad_damp = dampings(t_out)
    r = lax.broadcasted_iota(jnp.int32, (128, 128), 0)
    c = lax.broadcasted_iota(jnp.int32, (128, 128), 1)
    for i, both, damp in ((0, fg[0, 128:256, :], grad_damp), (1, fg[1, 128:256, :], grad_damp),
                          (2, fa[1], act_damp)):
        swept[i] = jnp.where(r >= c, both, both.T) / TOKENS + jnp.where(r == c, damp, 0.0)
    tiles = [swept.at[i] for i in range(3)]
    sweep_tiles(tiles, 4)
    step("give", 1)
    step("spread", 2)
    sweep_tiles(tiles, 10, start=4)
    step("give", 2)
    sweep_tiles(tiles, 16, start=10)
    for b in batches[1:]:
        taken(b)
    for b in batches:
        spread_sent(b)
        given(b)


def reduce_all(acts, grads):
    rows = acts.shape[0]
    vmem = pl.BlockSpec(memory_space=pltpu.VMEM)
    dma = pltpu.SemaphoreType.DMA
    tile = pltpu.VMEM((16, 128), F32)

    def buf(*shape):
        return pltpu.VMEM(shape + (128,), F32)

    return pl.pallas_call(
        reduce_kernel,
        out_shape=(jax.ShapeDtypeStruct((2, 8 * sum(GROWS), 128), F32),
                   jax.ShapeDtypeStruct((2, 8 * sum(AROWS), 128), F32),
                   jax.ShapeDtypeStruct((16, 128), F32), jax.ShapeDtypeStruct((3, 128, 128), F32)),
        in_specs=[pl.BlockSpec(memory_space=pl.ANY)] * 2,
        out_specs=(vmem,) * 4,
        scratch_shapes=[
            pltpu.VMEM((2 * rows, D // 2), acts.dtype), pltpu.VMEM((2 * rows, 8 * WIN), acts.dtype),
            pltpu.VMEM((16, 2 * rows, 384), acts.dtype),
            buf(NB, 16, HALF), buf(NB, 16, HALF), tile,
            buf(2, NB, 4, HALF), buf(2, NB, 2, 2, HALF), buf(2, NB, 2, 2, HALF), buf(2, NB, 2, 4, HALF),
            buf(NB, 3, HALF), buf(NB, 3, HALF), buf(NB, 8, CH), buf(NB, 7, CH), buf(NB, CH),
            buf(8 * sum(GROWS)), buf(8 * sum(AROWS)),
            tile, tile, tile, buf(3, 16), buf(3, 16), buf(7, 16), tile, buf(2, 16),
            dma((3, 4)), dma((3, 4)), dma((3, 4)), dma((2, NB, 6)), dma((2, NB, 6)), dma((NB, 6)), dma((NB, 6)), dma((NB, 7)), dma((NB, 7)),
            dma((NB, 6)), dma((NB, 8)), dma((NB, 8)), dma((NB, 10)), dma((NB, 2)), dma((NB, 2)), dma((14,)), dma((14,)),
        ],
        compiler_params=pltpu.CompilerParams(collective_id=1, has_side_effects=True, vmem_limit_bytes=VLIM),
        name="reduce_all",
    )(acts, grads)


def split(v):
    high = v.astype(jnp.bfloat16).astype(F32)
    rest = v - high
    mid = rest.astype(jnp.bfloat16).astype(F32)
    return high, mid, rest - mid


def dot(a, b, ca=1, cb=0):
    ah, am, al = split(a)
    bh, bm, bl = split(b)
    left = jnp.concatenate([ah, ah, am, ah, am, al], axis=ca).astype(jnp.bfloat16)
    right = jnp.concatenate([bh, bm, bh, bl, bm, bh], axis=cb).astype(jnp.bfloat16)
    return lax.dot_general(left, right, (((ca,), (cb,)), ((), ())), preferred_element_type=F32)


def sweep_four(now, at, row, sub, lane):
    def full(v):
        return jnp.broadcast_to(v, (8, 128))

    four = range(4)
    cols = [full(now[:, at + i:at + i + 1]) for i in four]
    rows = [full(now[row + i:row + i + 1, :]) for i in four]
    m = {(i, j): full(cols[j][row + i:row + i + 1, :]) for i in four for j in range(i + 1)}
    for p in four:
        inv = 1.0 / m[(p, p)]
        line = {i: m[(max(i, p), min(i, p))] * inv for i in four if i != p}
        new = {}
        for i in four:
            for j in range(i + 1):
                if i == p and j == p:
                    new[(i, j)] = -inv
                elif i == p:
                    new[(i, j)] = line[j]
                elif j == p:
                    new[(i, j)] = line[i]
                else:
                    new[(i, j)] = m[(i, j)] - m[(max(i, p), min(i, p))] * line[j]
        m = new
    in_rows = jnp.logical_and(sub >= row, sub < row + 4)
    in_cols = jnp.logical_and(lane >= at, lane < at + 4)
    out = jnp.where(jnp.logical_or(in_rows, in_cols), 0.0, now)
    rows = [jnp.where(in_cols, jnp.where(lane == at + i, -1.0, 0.0), rows[i]) for i in four]
    terms = []
    for i in four:
        col = jnp.where(in_rows, jnp.where(sub == row + i, -1.0, 0.0), cols[i])
        t = [m[(max(i, j), min(i, j))] * rows[j] for j in four]
        terms.append(col * ((t[0] + t[1]) + (t[2] + t[3])))
    return (out + terms[0]) + (terms[1] + (terms[2] + terms[3]))


def sweep_tiles(refs, panels, others=(), start=0):
    others = list(others)
    sub = lax.broadcasted_iota(jnp.int32, (8, 128), 0)
    lane = lax.broadcasted_iota(jnp.int32, (8, 128), 1)
    lane_all = lax.broadcasted_iota(jnp.int32, (128, 128), 1)
    for p in range(start, panels):
        base = 8 * p
        inside = jnp.logical_and(lane_all >= base, lane_all < base + 8)
        olds = [ref[base:base + 8, :] for ref in refs]
        news = [sweep_four(old, base, 0, sub, lane) for old in olds]
        news = [sweep_four(new, base + 4, 4, sub, lane) for new in news]
        for ref, old, new in zip(refs, olds, news):
            ref[...] = jnp.where(inside, 0.0, ref[...]) - dot(old, new, 0, 0)
            ref[base:base + 8, :] = new
        count = -(-len(others) // (panels - p))
        for step in others[:count]:
            step()
        others = others[count:]


def dampings(t_ref):
    act_trace = jnp.sum(t_ref[0:1, :], keepdims=True) / TOKENS
    grad_trace = jnp.sum(t_ref[1:2, :], keepdims=True) / TOKENS
    ratio = jnp.sqrt(act_trace / D / (grad_trace / FF))
    return ratio * DAMP, DAMP / ratio


def solve_kernel(fg_ref, fa_ref, t_ref, s_ref, w_ref, p_ref, g_ref, a_ref, l_ref, x_ref, ai_ref):
    act_damp, grad_damp = dampings(t_ref)
    r = lax.broadcasted_iota(jnp.int32, (128, 128), 0)
    c = lax.broadcasted_iota(jnp.int32, (128, 128), 1)
    last = GB - 256

    def second_of(both, second):
        return jnp.where(r < c, both, jnp.where(r == c, jnp.broadcast_to(second, (128, 128)), both.T))

    def damped(tile, damp):
        return tile / TOKENS + jnp.where(r == c, damp, 0.0)

    zeros = jnp.zeros((128 - last, 128), F32)
    for b in range(2):
        second = second_of(fg_ref[b, 128:256, :], fg_ref[b, 480:481, :])
        g_ref[b * 6] = s_ref[b]
        g_ref[b * 6 + 1] = fg_ref[b, 0:128, :] / TOKENS
        g_ref[b * 6 + 2] = damped(second, grad_damp)
        g_ref[b * 6 + 3] = jnp.concatenate([fg_ref[b, 256:344, :] / TOKENS, zeros], axis=0)
        g_ref[b * 6 + 4] = jnp.concatenate([fg_ref[b, 344:432, :] / TOKENS, zeros], axis=0)
        packed = fg_ref[b, 432:480, :]
        low = pltpu.roll(packed[0:40], 88, 1)
        upper = jnp.concatenate([packed, low, jnp.zeros((40, 128), F32)], axis=0)
        corner = jnp.where(jnp.logical_and(r >= 48, c < 48), upper.T, upper)
        inside = jnp.logical_and(r < last, c < last)
        g_ref[b * 6 + 5] = jnp.where(inside, damped(corner, grad_damp), jnp.where(r == c, 1.0, 0.0))
    second = second_of(fa_ref[128:256, :], t_ref[8:9, :])
    a_ref[0] = s_ref[2]
    a_ref[1] = fa_ref[0:128, :] / TOKENS
    a_ref[2] = damped(second, act_damp)
    gs = [[g_ref.at[b * 6 + t] for t in range(6)] for b in range(2)]
    am = [a_ref.at[t] for t in range(3)]
    for m in gs + [am]:
        a10 = m[1][...]
        l10 = -dot(a10, m[0][...])
        m[2][...] -= dot(l10, a10, 1, 1)
        l_ref[0 if m is gs[0] else 1 if m is gs[1] else 2] = l10

    def row_two(b):
        m = gs[b]
        a20 = m[3][...]

        def lower():
            l_ref[3 + b] = -dot(a20, m[0][...])

        def side():
            m[4][...] -= dot(l_ref[3 + b], m[1][...], 1, 1)

        def corner():
            m[5][...] -= dot(l_ref[3 + b], a20, 1, 1)
        return [lower, side, corner]

    steps = [step for pair_of in zip(row_two(0), row_two(1)) for step in pair_of]
    sweep_tiles([gs[0][2], gs[1][2], am[2]], 16, steps)
    for b, m in enumerate(gs):
        a21 = m[4][...]
        l21 = -dot(a21, m[2][...])
        m[5][...] -= dot(l21, a21, 1, 1)
        l_ref[5 + b] = l21

    def act_cross():
        v10 = -dot(am[2][...], l_ref[2])
        ai_ref[128:256, 0:128] = -v10
        ai_ref[0:128, 128:256] = -v10.T
        ai_ref[128:256, 128:256] = -am[2][...]

    def act_first():
        ai_ref[0:128, 0:128] = -am[0][...] - dot(l_ref[2], ai_ref[128:256, 0:128], 0, 0)

    def right_side(b):
        w = w_ref[...].astype(F32)[b * GB:(b + 1) * GB]
        w = jnp.concatenate([w, jnp.zeros((384 - GB, 256), F32)], axis=0).astype(jnp.bfloat16)
        pieces = jnp.concatenate(split(ai_ref[...]), axis=0).astype(jnp.bfloat16)
        x_ref[b] = jnp.dot(jnp.concatenate([w, w, w], axis=1), pieces, preferred_element_type=F32)

    def through(b):
        x = [x_ref.at[b, pl.ds(128 * i, 128)] for i in range(3)]
        l10, l20, l21 = l_ref.at[b], l_ref.at[3 + b], l_ref.at[5 + b]
        m = gs[b]

        def one():
            x[1][...] -= dot(l10[...], x[0][...])

        def two():
            x[2][...] -= dot(l20[...], x[0][...])

        def three():
            x[2][...] -= dot(l21[...], x[1][...])

        def four():
            x[1][...] = -dot(m[2][...], x[1][...])

        def five():
            x[0][...] = -dot(m[0][...], x[0][...])

        def six():
            x[0][...] -= dot(l10[...], x[1][...], 0, 0)

        def seven():
            l20[...] -= dot(l21[...], l10[...])
        return [one, two, three, four, five, six, seven]

    steps = [act_cross, act_first, lambda: right_side(0), lambda: right_side(1)]
    steps += [step for pair_of in zip(through(0), through(1)) for step in pair_of]
    sweep_tiles([gs[0][5], gs[1][5]], last // 8, steps)
    out = []
    for b, m in enumerate(gs):
        y2 = -dot(m[5][...], x_ref[b, 256:384])
        out += [x_ref[b, 0:128] - dot(l_ref[3 + b], y2, 0, 0),
                x_ref[b, 128:256] - dot(l_ref[5 + b], y2, 0, 0), y2[0:last]]
    p_ref[...] = jnp.concatenate(out, axis=0).astype(jnp.bfloat16)


def solve(fg, fa, tr, swept, w):
    vmem = pl.BlockSpec(memory_space=pltpu.VMEM)
    return pl.pallas_call(
        solve_kernel,
        out_shape=jax.ShapeDtypeStruct((2 * GB, 256), jnp.bfloat16),
        in_specs=[vmem] * 5,
        out_specs=vmem,
        scratch_shapes=[pltpu.VMEM((12, 128, 128), F32), pltpu.VMEM((3, 128, 128), F32),
                        pltpu.VMEM((7, 128, 128), F32), pltpu.VMEM((2, 384, 256), F32),
                        pltpu.VMEM((256, 256), F32)],
        compiler_params=pltpu.CompilerParams(vmem_limit_bytes=VLIM),
        name="solve",
    )(fg, fa, tr, swept, w)


def gather_kernel(p_ref, o_ref, local, sz, rz, sy, ry, sh, rh, sc, rc):
    dp, own = place()
    core = lax.rem(dp, 2)
    y = dp // 4
    sib = dp + 1 - 2 * core
    zh = lax.rem(dp // 2, 2)
    anti = dp + 2 - 4 * zh
    up = lax.rem(y + 1, 4) * 4 + lax.rem(dp, 4)
    down = lax.rem(y + 3, 4) * 4 + lax.rem(dp, 4)
    barrier = pltpu.get_barrier_semaphore()
    for device in (sib, anti, up, down):
        pl.semaphore_signal(barrier, inc=1, device_id=(device, own), device_id_type=MESH)
    pl.semaphore_wait(barrier, 4)

    def other(d):
        return d + 2 - 4 * lax.rem(d // 2, 2)

    far = lax.rem(y + 2, 4) * 4 + lax.rem(dp, 4)
    waits = []

    def half(ref, h):
        return ref.at[pl.ds(h * CUT[0], CUT[h])]

    def send(d, h, sems, i, device, src=None):
        src = o_ref.at[d] if src is None else src
        copy = pltpu.make_async_remote_copy(
            src_ref=half(src, h), dst_ref=half(o_ref.at[d], h), send_sem=sems[0].at[i], recv_sem=sems[1].at[i],
            device_id=(device, own), device_id_type=MESH)
        copy.start()
        waits.append(copy)

    def arrived(d, h, sems, i):
        dst = half(o_ref.at[d], h)
        pltpu.make_async_remote_copy(src_ref=dst, dst_ref=dst, send_sem=sems[0].at[i], recv_sem=sems[1].at[i],
                                     device_id=(sib, own), device_id_type=MESH).wait_recv()

    zsem, ysem, hsem, csem = (sz, rz), (sy, ry), (sh, rh), (sc, rc)
    for h in range(2):
        send(dp, h, zsem, h, anti, p_ref)
        send(dp, h, ysem, h, up, p_ref)
        send(dp, 1 - h, ysem, 3 - h, down, p_ref)
    for h in range(2):
        send(dp, h, csem, h, sib, p_ref)
    keep = pltpu.make_async_copy(p_ref, o_ref.at[dp], local)
    keep.start()
    arrived(down, 0, ysem, 0)
    send(down, 0, hsem, 0, up)
    arrived(up, 1, ysem, 3)
    send(up, 1, hsem, 1, down)
    send(down, 0, csem, 2, sib)
    send(up, 1, csem, 5, sib)
    arrived(down, 1, ysem, 1)
    send(down, 1, csem, 3, sib)
    arrived(up, 0, ysem, 2)
    send(up, 0, csem, 4, sib)
    arrived(anti, 0, zsem, 0)
    send(anti, 0, ysem, 4, up)
    send(anti, 0, ysem, 6, down)
    send(anti, 0, csem, 6, sib)
    arrived(far, 0, hsem, 0)
    send(far, 0, csem, 8, sib)
    arrived(far, 1, hsem, 1)
    send(far, 1, csem, 9, sib)
    arrived(anti, 1, zsem, 1)
    send(anti, 1, ysem, 5, up)
    send(anti, 1, ysem, 7, down)
    send(anti, 1, csem, 7, sib)
    arrived(other(down), 0, ysem, 4)
    send(other(down), 0, hsem, 2, up)
    send(other(down), 0, csem, 10, sib)
    arrived(other(up), 0, ysem, 6)
    send(other(up), 0, csem, 12, sib)
    arrived(other(up), 1, ysem, 7)
    send(other(up), 1, hsem, 3, down)
    send(other(up), 1, csem, 13, sib)
    arrived(other(down), 1, ysem, 5)
    send(other(down), 1, csem, 11, sib)
    arrived(other(far), 0, hsem, 2)
    send(other(far), 0, csem, 14, sib)
    arrived(other(far), 1, hsem, 3)
    send(other(far), 1, csem, 15, sib)

    def twin(d):
        return d + 1 - 2 * lax.rem(d, 2)

    for i, d in enumerate((dp, down, up, anti, far, other(down), other(up), other(far))):
        for h in range(2):
            arrived(twin(d), h, csem, 2 * i + h)
    keep.wait()
    for copy in waits:
        copy.wait_send()


def gather(p):
    dma = pltpu.SemaphoreType.DMA
    return pl.pallas_call(
        gather_kernel,
        out_shape=jax.ShapeDtypeStruct((16, 2 * GB, 256), jnp.bfloat16),
        in_specs=[pl.BlockSpec(memory_space=pl.ANY)],
        out_specs=pl.BlockSpec(memory_space=pl.ANY),
        scratch_shapes=[dma, dma((2,)), dma((2,)), dma((8,)), dma((8,)), dma((4,)), dma((4,)), dma((16,)), dma((16,))],
        compiler_params=pltpu.CompilerParams(collective_id=2, has_side_effects=True),
        name="gather",
    )(p)


def turn_kernel(i_ref, o_ref, ibuf, obuf, isem, osem):
    tiles = FF // 128
    parts = isem.shape[0]
    cuts = [tiles * k // parts * 128 for k in range(parts + 1)]
    ins = [pltpu.make_async_copy(i_ref.at[pl.ds(a, b - a)], ibuf.at[pl.ds(a, b - a)], isem.at[k])
           for k, (a, b) in enumerate(zip(cuts, cuts[1:]))]
    outs = [pltpu.make_async_copy(obuf.at[:, pl.ds(a, b - a)], o_ref.at[:, pl.ds(a, b - a)], osem.at[k])
            for k, (a, b) in enumerate(zip(cuts, cuts[1:]))]
    for copy in ins:
        copy.start()
    for k in range(parts):
        ins[k].wait()
        for at in range(cuts[k], cuts[k + 1], 128):
            for half in (0, 128):
                obuf[half:half + 128, at:at + 128] = ibuf[at:at + 128, half:half + 128].T
        outs[k].start()
    for copy in outs:
        copy.wait()


def turn(slices):
    anywhere = pl.BlockSpec(memory_space=pl.ANY)
    return pl.pallas_call(
        turn_kernel,
        out_shape=jax.ShapeDtypeStruct((256, FF), jnp.bfloat16),
        in_specs=[anywhere],
        out_specs=anywhere,
        scratch_shapes=[pltpu.VMEM((FF, 256), jnp.bfloat16), pltpu.VMEM((256, FF), jnp.bfloat16),
                        pltpu.SemaphoreType.DMA((4,)), pltpu.SemaphoreType.DMA((4,))],
        compiler_params=pltpu.CompilerParams(vmem_limit_bytes=VLIM),
        name="turn",
    )(slices)


def shards(acts, grads_out, weight_grad):
    fg, fa, tr, swept = reduce_all(acts, grads_out)
    p = solve(fg, fa.reshape(256, 128), tr, swept, weight_grad.T)
    return turn(gather(p).reshape(FF, 256))


def solution(mesh):
    in_specs = (P(("dp", "owner"), None), P(("dp", "owner"), None), P("owner", "dp"))
    out_specs = P("owner", None)
    return jax.shard_map(shards, mesh=mesh, in_specs=in_specs, out_specs=out_specs, check_vma=False)
```

```python
import functools
import math

import jax
import jax.numpy as jnp
from jax import lax
from jax.experimental import pallas as pl
from jax.experimental.pallas import tpu as pltpu
from jax.sharding import PartitionSpec as P

D = 4096
FF = 11008
AB = 256
GB = 344
TOKENS = 57344
DAMP = math.sqrt(0.03)
MESH = pl.DeviceIdType.MESH
F32 = jnp.float32
GROWS = (32, 16, 16)
AROWS = (16, 0, 0)
NB = len(GROWS)
CHS = tuple(g + a for g, a in zip(GROWS, AROWS))
GBASE = tuple(8 * sum(GROWS[:b]) for b in range(NB))
ABASE = tuple(8 * sum(AROWS[:b]) for b in range(NB))
CH = max(CHS)
HALF = 4 * CH
VLIM = 56 * 1024 * 1024
WIN = 7 * 128
WIDTHS = [WIN - 128 * (p % 4 in (0, 3)) for p in range(8)]
CUT = (352, 336)


def grad_position(p, part, core):
    y = p // 2
    return 2 * part + (p + y + core) % 2, y


def act_position(k, part):
    return k % 4, 2 * part + k // 4


def window(d):
    return 128 * (43 * d // 8)


def place():
    dp = lax.axis_index("dp")
    own = lax.axis_index("owner")
    return dp, own


def gram(block):
    return lax.dot_general(block, block, (((0,), (0,)), ((), ())), preferred_element_type=F32)


def fetch(a_ref, g_ref, abuf, gbuf, core, sibling, sems, send, recv):
    rows = a_ref.shape[0]
    mine, theirs = pl.ds(0, rows), pl.ds(rows, rows)
    width = abuf.shape[1]

    def half(c):
        return a_ref.at[:, pl.ds(pl.multiple_of(c * width, 128), width)]

    def columns(p, c):
        return g_ref.at[:, pl.ds(pl.multiple_of(window(2 * p + c), 128), WIDTHS[p])]

    here = [[(half(core), abuf.at[mine])], [], []]
    away = [[(half(1 - core), abuf.at[theirs])], [], []]
    for p in range(8):
        at = pl.ds(p * WIN, WIDTHS[p])
        here[1 + p // 4].append((columns(p, core), gbuf.at[mine, at]))
        away[1 + p // 4].append((columns(p, 1 - core), gbuf.at[theirs, at]))
    here = [[pltpu.make_async_copy(src, dst, sems.at[i, n]) for n, (src, dst) in enumerate(group)]
            for i, group in enumerate(here)]
    away = [[pltpu.make_async_remote_copy(src_ref=src, dst_ref=dst, send_sem=send.at[i, n], recv_sem=recv.at[i, n],
                                          device_id=sibling, device_id_type=MESH)
             for n, (src, dst) in enumerate(group)] for i, group in enumerate(away)]
    for group in here:
        for copy in group:
            copy.start()
    return here, away


def gram_step(copies, core, abuf, gbuf, even, x_ref, y_ref, t_ref):
    def store_all(where, sizes, bases, row, value):
        px, py = where
        done = 0
        while done < value.shape[0]:
            at = row + done
            batch = max(b for b in range(NB) if bases[b] <= at and sizes[b])
            size = sizes[batch]
            chunk, left = divmod(at - bases[batch], size)
            n = min(size - left, value.shape[0] - done)
            lead = 0 if sizes is GROWS else GROWS[batch]
            rows_at = pl.ds(chunk % 4 * CHS[batch] + lead + left, n)
            if chunk < 4:
                x_ref[batch, px * 4 + py, rows_at, :] = value[done:done + n]
            else:
                y_ref[batch, py * 4 + px, rows_at, :] = value[done:done + n]
            done += n

    r = lax.broadcasted_iota(jnp.int32, (128, 128), 0)
    c = lax.broadcasted_iota(jnp.int32, (128, 128), 1)

    def diag(tile):
        return jnp.sum(jnp.where(r == c, tile, 0.0), axis=0, keepdims=True)

    act_sum = jnp.zeros((1, 128), F32)
    grad_sum = jnp.zeros((1, 128), F32)
    for copy in copies[0]:
        copy.wait()
    for k in range(8):
        g = gram(abuf[:, k * AB:(k + 1) * AB])
        t0, t2 = g[0:128, 0:128], g[128:256, 128:256]
        second = diag(t2)
        act_sum += diag(t0) + second
        t_ref[8 + k:9 + k, :] = second
        store_all(act_position(k, 0), AROWS, ABASE, 0, g[128:256, 0:128])
        store_all(act_position(k, 1), AROWS, ABASE, 0, jnp.where(r >= c, t0, t2))
    for j in range(16):
        if j in (0, 8):
            for copy in copies[1 + j // 8]:
                copy.wait()
            for odd in range(2):
                @pl.when(core == odd)
                def _():
                    for i in range(j, j + 8):
                        d = i // 2 * 2 + odd
                        start = i // 2 * WIN + 2 * GB * d - window(d) + i % 2 * GB
                        even[i, :, 0:GB] = gbuf[:, start:start + GB]
        g = gram(even[j, :, 0:256])
        t0, t2 = g[0:128, 0:128], g[128:256, 128:256]
        second = diag(t2)
        grad_sum += diag(t0) + second
        where = grad_position(j // 2, j % 2, core)
        store_all(where, GROWS, GBASE, 0, g[128:256, 0:128])
        store_all(where, GROWS, GBASE, 128, jnp.where(r >= c, t0, t2))
        store_all(where, GROWS, GBASE, 480, jnp.concatenate([second, jnp.zeros((31, 128), F32)], axis=0))

    def rest():
        corner_sum = grad_sum
        for j in range(16):
            low = lax.dot_general(even[j, :, 256:GB], even[j, :, 0:GB], (((0,), (0,)), ((), ())),
                                  preferred_element_type=F32)
            t5 = jnp.concatenate([low[:, 256:GB], jnp.zeros((88, 40), F32)], axis=1)
            corner_sum += jnp.sum(jnp.where(r[:88] == c[:88], t5, 0.0), axis=0, keepdims=True)
            tail = jnp.concatenate([pltpu.roll(t5[48:88], 40, 1), jnp.zeros((8, 128), F32)], axis=0)
            where = grad_position(j // 2, j % 2, core)
            store_all(where, GROWS, GBASE, 256, low[:, 0:128])
            store_all(where, GROWS, GBASE, 344, low[:, 128:256])
            store_all(where, GROWS, GBASE, 432, jnp.where(c[:48] < 88, t5[0:48], tail))
        t_ref[0:8, :] = jnp.concatenate([act_sum, corner_sum, jnp.zeros((6, 128), F32)], axis=0)

    return rest


def reduce_kernel(a_ref, g_ref, fg, fa, t_out, swept,
                  abuf, gbuf, even, gx, gy, tr, ps, pk, pm, pr, rx2, ry2, st, rz, fin, ga, aa, t1, t2, t3, q1, q2, q3, q4, tt,
                  local, s0, r0, s1, r1, s2, r2, s3, r3, s4, rg4, ra4, s5, rg5, ra5, ts, tr_sem):
    dp, own = place()
    core = lax.rem(dp, 2)
    zh = lax.rem(dp // 2, 2)
    y = dp // 4
    x = lax.rem(own, 4)
    zl = own // 4
    z = zh * 4 + zl
    sib = dp + 1 - 2 * core

    def at(ax, ay, az, ac):
        return ((ay * 2 + az // 4) * 2 + ac, lax.rem(az, 4) * 4 + ax)

    xs = [at(lax.rem(x + k, 4), y, z, core) for k in (1, 2, 3)]
    ys = [at(x, lax.rem(y + k, 4), z, core) for k in (1, 2, 3)]
    zs = [at(x, y, lax.rem(z + k, 8), core) for k in range(1, 8)]
    g_part, a_part = x // 2, y // 2
    unit_zh = lax.rem(x + y + core, 2)
    unit_zl = 2 * core + lax.rem(y, 2)
    g_on = zh == unit_zh
    a_on = zl == unit_zl
    across = [at(x, lax.rem(y + k, 4), z, 1 - core) for k in range(4)]

    here, away = fetch(a_ref, g_ref, abuf, gbuf, core, (sib, own), local, s0, r0)
    barrier = pltpu.get_barrier_semaphore()
    for device in xs + ys + zs + across:
        pl.semaphore_signal(barrier, inc=1, device_id=device, device_id_type=MESH)
    pl.semaphore_wait(barrier, 17)
    for group in away:
        for copy in group:
            copy.start()
    rest = gram_step([h + a for h, a in zip(here, away)], core, abuf, gbuf, even, gx, gy, tr)

    def remote(src, dst, ssem, rsem, device):
        return pltpu.make_async_remote_copy(src_ref=src, dst_ref=dst, send_sem=ssem, recv_sem=rsem,
                                            device_id=device, device_id_type=MESH)

    def begin(copies):
        for copy in copies:
            copy.start()
        return copies

    def end(copies):
        for copy in copies:
            copy.wait()

    axes = ((0, gx, x, (xs[0], xs[2])), (1, gy, y, (ys[0], ys[2])))

    def high(b):
        return pl.ds(0, 4 * CHS[b])

    def chunk_rows(b, i):
        return pl.ds(pl.multiple_of(i * CHS[b], 8), CHS[b])

    def plane(b):
        copies = []
        two, rows = pl.ds(0, 2), high(b)
        for a, g, me, (up, down) in axes:
            opposite = lax.rem(me + 2, 4) * 4
            copies.append(remote(g.at[b, pl.ds(opposite, 2), rows], pm.at[a, b, 0, two, rows],
                                 s1.at[a, b, 0], r1.at[a, b, 0], up))
            copies.append(remote(g.at[b, pl.ds(opposite + 2, 2), rows], pm.at[a, b, 1, two, rows],
                                 s1.at[a, b, 1], r1.at[a, b, 1], down))
        for a, g, me, (up, down) in axes:
            over, under = lax.rem(me + 1, 4) * 4, lax.rem(me + 3, 4) * 4
            copies.append(remote(g.at[b, pl.ds(over + 2, 2), rows], pr.at[a, b, 0, pl.ds(2, 2), rows],
                                 s1.at[a, b, 2], r1.at[a, b, 2], up))
            copies.append(remote(g.at[b, pl.ds(under, 2), rows], pr.at[a, b, 1, two, rows],
                                 s1.at[a, b, 3], r1.at[a, b, 3], down))
        return begin(copies)

    def plane_pass(b, copies):
        end(copies[:4])
        @pl.loop(0, 8)
        def _(i):
            h, rows = i // 4, chunk_rows(b, lax.rem(i, 4))
            for a, g, me, _ in axes:
                over, under = lax.rem(me + 1, 4) * 4, lax.rem(me + 3, 4) * 4
                pk[a, b, 0, h, rows, :] = g[b, over + h, rows, :] + pm[a, b, 0, h, rows, :]
                pk[a, b, 1, h, rows, :] = g[b, under + 2 + h, rows, :] + pm[a, b, 1, h, rows, :]
        for a, _, _, to in axes:
            for d in range(2):
                copies.append(remote(pk.at[a, b, d, pl.ds(0, 2), high(b)], pr.at[a, b, d, pl.ds(2 * d, 2), high(b)],
                                     s1.at[a, b, 4 + d], r1.at[a, b, 4 + d], to[d]))
                copies[-1].start()

    def plane_sum(b, copies):
        end(copies[4:])
        @pl.loop(0, 16)
        def _(i):
            q, rows = i // 4, chunk_rows(b, lax.rem(i, 4))
            for a, g, me, _ in axes:
                ps[a, b, q, rows, :] = g[b, me * 4 + q, rows, :] + (pr[a, b, 0, q, rows, :] + pr[a, b, 1, q, rows, :])

    def cross(b):
        copies = []
        rows = high(b)
        for k in range(3):
            copies.append(remote(ps.at[0, b, lax.rem(y + k + 1, 4), rows], rx2.at[b, k, rows],
                                 s2.at[b, k], r2.at[b, k], ys[k]))
            copies.append(remote(ps.at[1, b, lax.rem(x + k + 1, 4), rows], ry2.at[b, k, rows],
                                 s2.at[b, 3 + k], r2.at[b, 3 + k], xs[k]))
        return begin(copies)

    def cross_sum(b):
        n = CHS[b]
        @pl.loop(0, 4)
        def _(i):
            rows = chunk_rows(b, i)
            st[b, i, 0:n, :] = (ps[0, b, y, rows, :] + rx2[b, 0, rows, :]) + (rx2[b, 1, rows, :] + rx2[b, 2, rows, :])
            st[b, 4 + i, 0:n, :] = ((ps[1, b, x, rows, :] + ry2[b, 0, rows, :])
                                    + (ry2[b, 1, rows, :] + ry2[b, 2, rows, :]))

    def along(b):
        rows = pl.ds(0, CHS[b])
        return begin([remote(st.at[b, lax.rem(z + k + 1, 8), rows], rz.at[b, k, rows], s3.at[b, k], r3.at[b, k], zs[k])
                      for k in range(7)])

    def along_sum(b):
        n = CHS[b]
        total = st[b, z, 0:n, :]
        for k in range(7):
            total += rz[b, k, 0:n, :]
        fin[b, 0:n, :] = total

    def pieces(b):
        found = [(fin.at[b, pl.ds(0, GROWS[b])], ga, GBASE[b], GROWS[b], rg4, [unit_zh * 4 + i for i in range(4)], 0)]
        if AROWS[b]:
            found.append((fin.at[b, pl.ds(GROWS[b], AROWS[b])], aa, ABASE[b], AROWS[b], ra4,
                          [i * 4 + unit_zl for i in range(2)], 4))
        return found

    def slot(buffer, base, size, i):
        return buffer.at[pl.ds(pl.multiple_of(base + i * size, 8), size)]

    def spread(b):
        for src, buffer, base, size, rsem, planes, first in pieces(b):
            dst = slot(buffer, base, size, z)
            for i, to in enumerate(planes):
                @pl.when(to == z)
                def _():
                    pltpu.make_async_copy(src, dst, rsem.at[b, z]).start()

                @pl.when(to != z)
                def _():
                    remote(src, dst, s4.at[b, first + i], rsem.at[b, z], at(x, y, to, core)).start()

    def spread_sent(b):
        for src, buffer, base, size, rsem, planes, first in pieces(b):
            dst = slot(buffer, base, size, z)
            for i, to in enumerate(planes):
                @pl.when(to != z)
                def _():
                    remote(src, dst, s4.at[b, first + i], rsem.at[b, z], at(x, y, to, core)).wait_send()

    def parts(b):
        for (src, buffer, base, size, rsem, _, first), (on, to, out, part, sem, at_sem) in zip(
                pieces(b), ((g_on, xs, fg, g_part, rg5, 0), (a_on, ys + across, fa, a_part, ra5, 3))):
            rows = pl.ds(base, 8 * size)
            yield src, buffer, base, size, rsem, on, to, buffer.at[rows], out, rows, part, sem, at_sem

    def give(b):
        for piece, buffer, base, size, arrive, on, to, src, out, rows, part, sem, first in parts(b):
            @pl.when(on)
            def _():
                for i in range(8):
                    pltpu.make_async_copy(piece, slot(buffer, base, size, i), arrive.at[b, i]).wait()
                dst = out.at[part, rows]
                for i, device in enumerate(to):
                    remote(src, dst, s5.at[b, first + i], sem.at[b, part], device).start()
                pltpu.make_async_copy(src, dst, sem.at[b, part]).start()

    def given(b):
        for piece, buffer, base, size, arrive, on, to, src, out, rows, part, sem, first in parts(b):
            @pl.when(on)
            def _():
                for i, device in enumerate(to):
                    remote(src, out.at[part, rows], s5.at[b, first + i], sem.at[b, part], device).wait_send()

    def taken(b):
        for piece, buffer, base, size, arrive, on, to, src, out, rows, part, sem, first in parts(b):
            for i in range(2):
                pltpu.make_async_copy(src, out.at[i, rows], sem.at[b, i]).wait()

    batches = range(NB)
    first, second, third = {}, {}, {}

    def step(name, b):
        if name == "plane":
            first[b] = plane(b)
        elif name == "pass":
            plane_pass(b, first[b])
        elif name == "cross":
            plane_sum(b, first[b])
            second[b] = cross(b)
        elif name == "along":
            end(second[b])
            cross_sum(b)
            third[b] = along(b)
        elif name == "spread":
            end(third[b])
            along_sum(b)
            spread(b)
        else:
            give(b)

    step("plane", 0)
    rest()
    q = begin([remote(tr, q1.at[k], ts.at[k], tr_sem.at[k], xs[k]) for k in range(3)])
    step("pass", 0)
    step("plane", 1)
    step("cross", 0)
    end(q)
    t1[...] = (tr[...] + q1[0]) + (q1[1] + q1[2])
    q = begin([remote(t1, q2.at[k], ts.at[3 + k], tr_sem.at[3 + k], ys[k]) for k in range(3)])
    step("pass", 1)
    step("plane", 2)
    step("along", 0)
    end(q)
    t2[...] = (t1[...] + q2[0]) + (q2[1] + q2[2])
    q = begin([remote(t2, q3.at[k], ts.at[6 + k], tr_sem.at[6 + k], zs[k]) for k in range(7)])
    step("cross", 1)
    step("pass", 2)
    step("spread", 0)
    end(q)
    trace = t2[...]
    for k in range(7):
        trace += q3[k]
    t3[...] = trace
    q = begin([remote(t3, q4, ts.at[13], tr_sem.at[13], (sib, own))])
    step("along", 1)
    step("cross", 2)
    step("give", 0)
    step("spread", 1)
    step("along", 2)
    end(q)
    tt[core] = t3[...]
    tt[1 - core] = q4[...]
    t_out[0:8, :] = tt[0, 0:8, :] + tt[1, 0:8, :]
    t_out[8:16, :] = jnp.broadcast_to(tt[own // 8, pl.ds(8 + lax.rem(own, 8), 1), :], (8, 128))
    taken(0)
    act_damp, grad_damp = dampings(t_out)
    r = lax.broadcasted_iota(jnp.int32, (128, 128), 0)
    c = lax.broadcasted_iota(jnp.int32, (128, 128), 1)
    for i, both, damp in ((0, fg[0, 128:256, :], grad_damp), (1, fg[1, 128:256, :], grad_damp),
                          (2, fa[1], act_damp)):
        swept[i] = jnp.where(r >= c, both, both.T) / TOKENS + jnp.where(r == c, damp, 0.0)
    tiles = [swept.at[i] for i in range(3)]
    sweep_tiles(tiles, 4)
    step("give", 1)
    step("spread", 2)
    sweep_tiles(tiles, 10, start=4)
    step("give", 2)
    sweep_tiles(tiles, 16, start=10)
    for b in batches[1:]:
        taken(b)
    for b in batches:
        spread_sent(b)
        given(b)


def reduce_all(acts, grads):
    rows = acts.shape[0]
    vmem = pl.BlockSpec(memory_space=pltpu.VMEM)
    dma = pltpu.SemaphoreType.DMA
    tile = pltpu.VMEM((16, 128), F32)

    def buf(*shape):
        return pltpu.VMEM(shape + (128,), F32)

    return pl.pallas_call(
        reduce_kernel,
        out_shape=(jax.ShapeDtypeStruct((2, 8 * sum(GROWS), 128), F32),
                   jax.ShapeDtypeStruct((2, 8 * sum(AROWS), 128), F32),
                   jax.ShapeDtypeStruct((16, 128), F32), jax.ShapeDtypeStruct((3, 128, 128), F32)),
        in_specs=[pl.BlockSpec(memory_space=pl.ANY)] * 2,
        out_specs=(vmem,) * 4,
        scratch_shapes=[
            pltpu.VMEM((2 * rows, D // 2), acts.dtype), pltpu.VMEM((2 * rows, 8 * WIN), acts.dtype),
            pltpu.VMEM((16, 2 * rows, 384), acts.dtype),
            buf(NB, 16, HALF), buf(NB, 16, HALF), tile,
            buf(2, NB, 4, HALF), buf(2, NB, 2, 2, HALF), buf(2, NB, 2, 2, HALF), buf(2, NB, 2, 4, HALF),
            buf(NB, 3, HALF), buf(NB, 3, HALF), buf(NB, 8, CH), buf(NB, 7, CH), buf(NB, CH),
            buf(8 * sum(GROWS)), buf(8 * sum(AROWS)),
            tile, tile, tile, buf(3, 16), buf(3, 16), buf(7, 16), tile, buf(2, 16),
            dma((3, 4)), dma((3, 4)), dma((3, 4)), dma((2, NB, 6)), dma((2, NB, 6)), dma((NB, 6)), dma((NB, 6)), dma((NB, 7)), dma((NB, 7)),
            dma((NB, 6)), dma((NB, 8)), dma((NB, 8)), dma((NB, 10)), dma((NB, 2)), dma((NB, 2)), dma((14,)), dma((14,)),
        ],
        compiler_params=pltpu.CompilerParams(collective_id=1, has_side_effects=True, vmem_limit_bytes=VLIM),
        name="reduce_all",
    )(acts, grads)


def split(v):
    high = v.astype(jnp.bfloat16).astype(F32)
    rest = v - high
    mid = rest.astype(jnp.bfloat16).astype(F32)
    return high, mid, rest - mid


def dot(a, b, ca=1, cb=0):
    ah, am, al = split(a)
    bh, bm, bl = split(b)
    left = jnp.concatenate([ah, ah, am, ah, am, al], axis=ca).astype(jnp.bfloat16)
    right = jnp.concatenate([bh, bm, bh, bl, bm, bh], axis=cb).astype(jnp.bfloat16)
    return lax.dot_general(left, right, (((ca,), (cb,)), ((), ())), preferred_element_type=F32)


def sweep_four(now, at, row, sub, lane):
    def full(v):
        return jnp.broadcast_to(v, (8, 128))

    four = range(4)
    cols = [full(now[:, at + i:at + i + 1]) for i in four]
    rows = [full(now[row + i:row + i + 1, :]) for i in four]
    m = {(i, j): full(cols[j][row + i:row + i + 1, :]) for i in four for j in range(i + 1)}
    for p in four:
        inv = 1.0 / m[(p, p)]
        line = {i: m[(max(i, p), min(i, p))] * inv for i in four if i != p}
        new = {}
        for i in four:
            for j in range(i + 1):
                if i == p and j == p:
                    new[(i, j)] = -inv
                elif i == p:
                    new[(i, j)] = line[j]
                elif j == p:
                    new[(i, j)] = line[i]
                else:
                    new[(i, j)] = m[(i, j)] - m[(max(i, p), min(i, p))] * line[j]
        m = new
    in_rows = jnp.logical_and(sub >= row, sub < row + 4)
    in_cols = jnp.logical_and(lane >= at, lane < at + 4)
    out = jnp.where(jnp.logical_or(in_rows, in_cols), 0.0, now)
    rows = [jnp.where(in_cols, jnp.where(lane == at + i, -1.0, 0.0), rows[i]) for i in four]
    terms = []
    for i in four:
        col = jnp.where(in_rows, jnp.where(sub == row + i, -1.0, 0.0), cols[i])
        t = [m[(max(i, j), min(i, j))] * rows[j] for j in four]
        terms.append(col * ((t[0] + t[1]) + (t[2] + t[3])))
    return (out + terms[0]) + (terms[1] + (terms[2] + terms[3]))


def sweep_tiles(refs, panels, others=(), start=0):
    others = list(others)
    sub = lax.broadcasted_iota(jnp.int32, (8, 128), 0)
    lane = lax.broadcasted_iota(jnp.int32, (8, 128), 1)
    lane_all = lax.broadcasted_iota(jnp.int32, (128, 128), 1)
    for p in range(start, panels):
        base = 8 * p
        inside = jnp.logical_and(lane_all >= base, lane_all < base + 8)
        olds = [ref[base:base + 8, :] for ref in refs]
        news = [sweep_four(old, base, 0, sub, lane) for old in olds]
        news = [sweep_four(new, base + 4, 4, sub, lane) for new in news]
        for ref, old, new in zip(refs, olds, news):
            ref[...] = jnp.where(inside, 0.0, ref[...]) - dot(old, new, 0, 0)
            ref[base:base + 8, :] = new
        count = -(-len(others) // (panels - p))
        for step in others[:count]:
            step()
        others = others[count:]


def dampings(t_ref):
    act_trace = jnp.sum(t_ref[0:1, :], keepdims=True) / TOKENS
    grad_trace = jnp.sum(t_ref[1:2, :], keepdims=True) / TOKENS
    ratio = jnp.sqrt(act_trace / D / (grad_trace / FF))
    return ratio * DAMP, DAMP / ratio


def solve_kernel(fg_ref, fa_ref, t_ref, s_ref, w_ref, p_ref, g_ref, a_ref, l_ref, x_ref, ai_ref):
    act_damp, grad_damp = dampings(t_ref)
    r = lax.broadcasted_iota(jnp.int32, (128, 128), 0)
    c = lax.broadcasted_iota(jnp.int32, (128, 128), 1)
    last = GB - 256

    def second_of(both, second):
        return jnp.where(r < c, both, jnp.where(r == c, jnp.broadcast_to(second, (128, 128)), both.T))

    def damped(tile, damp):
        return tile / TOKENS + jnp.where(r == c, damp, 0.0)

    zeros = jnp.zeros((128 - last, 128), F32)
    for b in range(2):
        second = second_of(fg_ref[b, 128:256, :], fg_ref[b, 480:481, :])
        g_ref[b * 6] = s_ref[b]
        g_ref[b * 6 + 1] = fg_ref[b, 0:128, :] / TOKENS
        g_ref[b * 6 + 2] = damped(second, grad_damp)
        g_ref[b * 6 + 3] = jnp.concatenate([fg_ref[b, 256:344, :] / TOKENS, zeros], axis=0)
        g_ref[b * 6 + 4] = jnp.concatenate([fg_ref[b, 344:432, :] / TOKENS, zeros], axis=0)
        packed = fg_ref[b, 432:480, :]
        low = pltpu.roll(packed[0:40], 88, 1)
        upper = jnp.concatenate([packed, low, jnp.zeros((40, 128), F32)], axis=0)
        corner = jnp.where(jnp.logical_and(r >= 48, c < 48), upper.T, upper)
        inside = jnp.logical_and(r < last, c < last)
        g_ref[b * 6 + 5] = jnp.where(inside, damped(corner, grad_damp), jnp.where(r == c, 1.0, 0.0))
    second = second_of(fa_ref[128:256, :], t_ref[8:9, :])
    a_ref[0] = s_ref[2]
    a_ref[1] = fa_ref[0:128, :] / TOKENS
    a_ref[2] = damped(second, act_damp)
    gs = [[g_ref.at[b * 6 + t] for t in range(6)] for b in range(2)]
    am = [a_ref.at[t] for t in range(3)]
    for m in gs + [am]:
        a10 = m[1][...]
        l10 = -dot(a10, m[0][...])
        m[2][...] -= dot(l10, a10, 1, 1)
        l_ref[0 if m is gs[0] else 1 if m is gs[1] else 2] = l10

    def row_two(b):
        m = gs[b]
        a20 = m[3][...]

        def lower():
            l_ref[3 + b] = -dot(a20, m[0][...])

        def side():
            m[4][...] -= dot(l_ref[3 + b], m[1][...], 1, 1)

        def corner():
            m[5][...] -= dot(l_ref[3 + b], a20, 1, 1)
        return [lower, side, corner]

    steps = [step for pair_of in zip(row_two(0), row_two(1)) for step in pair_of]
    sweep_tiles([gs[0][2], gs[1][2], am[2]], 16, steps)
    for b, m in enumerate(gs):
        a21 = m[4][...]
        l21 = -dot(a21, m[2][...])
        m[5][...] -= dot(l21, a21, 1, 1)
        l_ref[5 + b] = l21

    def act_cross():
        v10 = -dot(am[2][...], l_ref[2])
        ai_ref[128:256, 0:128] = -v10
        ai_ref[0:128, 128:256] = -v10.T
        ai_ref[128:256, 128:256] = -am[2][...]

    def act_first():
        ai_ref[0:128, 0:128] = -am[0][...] - dot(l_ref[2], ai_ref[128:256, 0:128], 0, 0)

    def right_side(b):
        w = w_ref[...].astype(F32)[b * GB:(b + 1) * GB]
        w = jnp.concatenate([w, jnp.zeros((384 - GB, 256), F32)], axis=0).astype(jnp.bfloat16)
        pieces = jnp.concatenate(split(ai_ref[...]), axis=0).astype(jnp.bfloat16)
        x_ref[b] = jnp.dot(jnp.concatenate([w, w, w], axis=1), pieces, preferred_element_type=F32)

    def through(b):
        x = [x_ref.at[b, pl.ds(128 * i, 128)] for i in range(3)]
        l10, l20, l21 = l_ref.at[b], l_ref.at[3 + b], l_ref.at[5 + b]
        m = gs[b]

        def one():
            x[1][...] -= dot(l10[...], x[0][...])

        def two():
            x[2][...] -= dot(l20[...], x[0][...])

        def three():
            x[2][...] -= dot(l21[...], x[1][...])

        def four():
            x[1][...] = -dot(m[2][...], x[1][...])

        def five():
            x[0][...] = -dot(m[0][...], x[0][...])

        def six():
            x[0][...] -= dot(l10[...], x[1][...], 0, 0)

        def seven():
            l20[...] -= dot(l21[...], l10[...])
        return [one, two, three, four, five, six, seven]

    steps = [act_cross, act_first, lambda: right_side(0), lambda: right_side(1)]
    steps += [step for pair_of in zip(through(0), through(1)) for step in pair_of]
    sweep_tiles([gs[0][5], gs[1][5]], last // 8, steps)
    out = []
    for b, m in enumerate(gs):
        y2 = -dot(m[5][...], x_ref[b, 256:384])
        out += [x_ref[b, 0:128] - dot(l_ref[3 + b], y2, 0, 0),
                x_ref[b, 128:256] - dot(l_ref[5 + b], y2, 0, 0), y2[0:last]]
    p_ref[...] = jnp.concatenate(out, axis=0).astype(jnp.bfloat16)


def solve(fg, fa, tr, swept, w):
    vmem = pl.BlockSpec(memory_space=pltpu.VMEM)
    return pl.pallas_call(
        solve_kernel,
        out_shape=jax.ShapeDtypeStruct((2 * GB, 256), jnp.bfloat16),
        in_specs=[vmem] * 5,
        out_specs=vmem,
        scratch_shapes=[pltpu.VMEM((12, 128, 128), F32), pltpu.VMEM((3, 128, 128), F32),
                        pltpu.VMEM((7, 128, 128), F32), pltpu.VMEM((2, 384, 256), F32),
                        pltpu.VMEM((256, 256), F32)],
        compiler_params=pltpu.CompilerParams(vmem_limit_bytes=VLIM),
        name="solve",
    )(fg, fa, tr, swept, w)


def gather_kernel(p_ref, o_ref, local, sz, rz, sy, ry, sh, rh, sc, rc):
    dp, own = place()
    core = lax.rem(dp, 2)
    y = dp // 4
    sib = dp + 1 - 2 * core
    zh = lax.rem(dp // 2, 2)
    anti = dp + 2 - 4 * zh
    up = lax.rem(y + 1, 4) * 4 + lax.rem(dp, 4)
    down = lax.rem(y + 3, 4) * 4 + lax.rem(dp, 4)
    barrier = pltpu.get_barrier_semaphore()
    for device in (sib, anti, up, down):
        pl.semaphore_signal(barrier, inc=1, device_id=(device, own), device_id_type=MESH)
    pl.semaphore_wait(barrier, 4)

    def other(d):
        return d + 2 - 4 * lax.rem(d // 2, 2)

    far = lax.rem(y + 2, 4) * 4 + lax.rem(dp, 4)
    waits = []

    def half(ref, h):
        return ref.at[pl.ds(h * CUT[0], CUT[h])]

    def send(d, h, sems, i, device, src=None):
        src = o_ref.at[d] if src is None else src
        copy = pltpu.make_async_remote_copy(
            src_ref=half(src, h), dst_ref=half(o_ref.at[d], h), send_sem=sems[0].at[i], recv_sem=sems[1].at[i],
            device_id=(device, own), device_id_type=MESH)
        copy.start()
        waits.append(copy)

    def arrived(d, h, sems, i):
        dst = half(o_ref.at[d], h)
        pltpu.make_async_remote_copy(src_ref=dst, dst_ref=dst, send_sem=sems[0].at[i], recv_sem=sems[1].at[i],
                                     device_id=(sib, own), device_id_type=MESH).wait_recv()

    zsem, ysem, hsem, csem = (sz, rz), (sy, ry), (sh, rh), (sc, rc)
    for h in range(2):
        send(dp, h, zsem, h, anti, p_ref)
        send(dp, h, ysem, h, up, p_ref)
        send(dp, 1 - h, ysem, 3 - h, down, p_ref)
    for h in range(2):
        send(dp, h, csem, h, sib, p_ref)
    keep = pltpu.make_async_copy(p_ref, o_ref.at[dp], local)
    keep.start()
    arrived(down, 0, ysem, 0)
    send(down, 0, hsem, 0, up)
    arrived(up, 1, ysem, 3)
    send(up, 1, hsem, 1, down)
    send(down, 0, csem, 2, sib)
    send(up, 1, csem, 5, sib)
    arrived(down, 1, ysem, 1)
    send(down, 1, csem, 3, sib)
    arrived(up, 0, ysem, 2)
    send(up, 0, csem, 4, sib)
    arrived(anti, 0, zsem, 0)
    send(anti, 0, ysem, 4, up)
    send(anti, 0, ysem, 6, down)
    send(anti, 0, csem, 6, sib)
    arrived(far, 0, hsem, 0)
    send(far, 0, csem, 8, sib)
    arrived(far, 1, hsem, 1)
    send(far, 1, csem, 9, sib)
    arrived(anti, 1, zsem, 1)
    send(anti, 1, ysem, 5, up)
    send(anti, 1, ysem, 7, down)
    send(anti, 1, csem, 7, sib)
    arrived(other(down), 0, ysem, 4)
    send(other(down), 0, hsem, 2, up)
    send(other(down), 0, csem, 10, sib)
    arrived(other(up), 0, ysem, 6)
    send(other(up), 0, csem, 12, sib)
    arrived(other(up), 1, ysem, 7)
    send(other(up), 1, hsem, 3, down)
    send(other(up), 1, csem, 13, sib)
    arrived(other(down), 1, ysem, 5)
    send(other(down), 1, csem, 11, sib)
    arrived(other(far), 0, hsem, 2)
    send(other(far), 0, csem, 14, sib)
    arrived(other(far), 1, hsem, 3)
    send(other(far), 1, csem, 15, sib)

    def twin(d):
        return d + 1 - 2 * lax.rem(d, 2)

    for i, d in enumerate((dp, down, up, anti, far, other(down), other(up), other(far))):
        for h in range(2):
            arrived(twin(d), h, csem, 2 * i + h)
    keep.wait()
    for copy in waits:
        copy.wait_send()


def gather(p):
    dma = pltpu.SemaphoreType.DMA
    return pl.pallas_call(
        gather_kernel,
        out_shape=jax.ShapeDtypeStruct((16, 2 * GB, 256), jnp.bfloat16),
        in_specs=[pl.BlockSpec(memory_space=pl.ANY)],
        out_specs=pl.BlockSpec(memory_space=pl.ANY),
        scratch_shapes=[dma, dma((2,)), dma((2,)), dma((8,)), dma((8,)), dma((4,)), dma((4,)), dma((16,)), dma((16,))],
        compiler_params=pltpu.CompilerParams(collective_id=2, has_side_effects=True),
        name="gather",
    )(p)


def turn_kernel(i_ref, o_ref, ibuf, obuf, isem, osem):
    tiles = FF // 128
    parts = isem.shape[0]
    cuts = [tiles * k // parts * 128 for k in range(parts + 1)]
    ins = [pltpu.make_async_copy(i_ref.at[pl.ds(a, b - a)], ibuf.at[pl.ds(a, b - a)], isem.at[k])
           for k, (a, b) in enumerate(zip(cuts, cuts[1:]))]
    outs = [pltpu.make_async_copy(obuf.at[:, pl.ds(a, b - a)], o_ref.at[:, pl.ds(a, b - a)], osem.at[k])
            for k, (a, b) in enumerate(zip(cuts, cuts[1:]))]
    for copy in ins:
        copy.start()
    for k in range(parts):
        ins[k].wait()
        for at in range(cuts[k], cuts[k + 1], 128):
            for half in (0, 128):
                obuf[half:half + 128, at:at + 128] = ibuf[at:at + 128, half:half + 128].T
        outs[k].start()
    for copy in outs:
        copy.wait()


def turn(slices):
    anywhere = pl.BlockSpec(memory_space=pl.ANY)
    return pl.pallas_call(
        turn_kernel,
        out_shape=jax.ShapeDtypeStruct((256, FF), jnp.bfloat16),
        in_specs=[anywhere],
        out_specs=anywhere,
        scratch_shapes=[pltpu.VMEM((FF, 256), jnp.bfloat16), pltpu.VMEM((256, FF), jnp.bfloat16),
                        pltpu.SemaphoreType.DMA((4,)), pltpu.SemaphoreType.DMA((4,))],
        compiler_params=pltpu.CompilerParams(vmem_limit_bytes=VLIM),
        name="turn",
    )(slices)


def shards(acts, grads_out, weight_grad):
    fg, fa, tr, swept = reduce_all(acts, grads_out)
    p = solve(fg, fa.reshape(256, 128), tr, swept, weight_grad.T)
    return turn(gather(p).reshape(FF, 256))


def solution(mesh):
    in_specs = (P(("dp", "owner"), None), P(("dp", "owner"), None), P("owner", "dp"))
    out_specs = P("owner", None)
    return jax.shard_map(shards, mesh=mesh, in_specs=in_specs, out_specs=out_specs, check_vma=False)
```
